512 devices in a mesh: lat: 8 (over z_lo), lon: 64 (over y, x, z_hi, core).
Axes of the slice: x: 4, y: 4, z: 16 (z_hi: 2, z_lo: 8; z = z_hi * 8 + z_lo), core: 2. Of those that a mesh axis runs over, the one named last changes fastest.
Arguments:
- tokens: bfloat16 [96, 768, 512], P('lat', 'lon'), may hold values from -50 to 50
- query_key_value_weight: bfloat16 [512, 1536], replicated, may hold values from -0.25 to 0.25
- output_weight: bfloat16 [512, 512], replicated, may hold values from -0.25 to 0.25
- adapter_down_map: bfloat16 [2, 8, 512], replicated, may hold values from -0.25 to 0.25
- adapter_up_map: bfloat16 [2, 8, 512], replicated, may hold values from -2 to 2
- relative_position_bias: float32 [16, 72, 72], replicated, may hold values from -4 to 320
- readout: bfloat16 [512], replicated, may hold values from -0.25 to 0.25
- observation_index: int32 [8, 64, 64, 4, 128], P('lat', 'lon'), may hold values from 0 to 143
- observation_weight: float32 [8, 64, 64, 4, 128], P('lat', 'lon'), may hold values from 0.05 to 1
- observation_value: float32 [8, 64, 64, 128], P('lat', 'lon'), may hold values from -6 to 6
- observation_count: int32 [8, 64, 64], P('lat', 'lon'), may hold values from 0 to 128, as said below
Outputs:
- block_out: bfloat16 [96, 768, 512], P('lat', 'lon')
- innovation: float32 [8, 64, 64, 128], P('lat', 'lon')
- rolled_adjoint: float32 [96, 768], P('lat', 'lon')
- down_map_gradient: float32 [2, 8, 512], replicated
- up_map_gradient: float32 [2, 8, 512], replicated
The draws below stay inside these ranges and needn't reach their ends.
Inputs may be any that keep to these rules, and one draw needn't show every extreme that they name: `observation_index`: positions, row by row, inside the destination tile of 12 x 12 patches. `observation_count`: in every band one strip receives 128 live slots from every shard of the band, and every shard fills some strip.
All inputs are finite; a program needn't handle non-finite values.
Results may differ from the reference program's by a relative error of at most 0.008.
Values may be sent and summed in bfloat16 or wider, within the bound.
No kernel may reach another device: no remote copies, remote signals or barrier semaphores. Data moves between devices by JAX's collectives and lax.ppermute only.
A program may use at most 64 MiB of HBM per device.

```python
import math
import jax
import jax.numpy as jnp
from jax import lax

MODEL_DIM = 512
HEADS = 16
HEAD_DIM = 32
ADAPTER_RANK = 8
WIN_LAT = 6
WIN_LON = 12
SHIFT_LAT = 3
SHIFT_LON = 6
K = 4
LAT_DEV = 12
LON_DEV = 12
NLAT = 96
NLON = 768
BANDS = 8
STRIPS = 64
CAP = 128
WIN_TOK = 72


def draw_tokens(key, part):
    key = jax.random.fold_in(key, 3)
    key_base, key_row, key_col = jax.random.split(key, 3)
    shape = (NLAT, NLON, MODEL_DIM)
    row_scale = jnp.exp(jax.random.uniform(key_row, (NLAT, NLON, 1), jnp.float32, 0.0, math.log(10.0)))
    col_scale = jnp.exp(jax.random.uniform(key_col, (1, 1, MODEL_DIM), jnp.float32, 0.0, math.log(10.0)))
    base = jnp.clip(jax.random.normal(key_base, shape, jnp.float32), -4.0, 4.0)
    return (base * row_scale * col_scale / 8.0).astype(jnp.bfloat16)


def draw_relative_position_bias(key, part):
    key = jax.random.fold_in(key, 5)
    keys = jax.random.split(key, 1)
    shape = (HEADS, WIN_TOK, WIN_TOK)
    return jnp.clip(jax.random.normal(keys[0], shape, jnp.float32), -4.0, 4.0)


def draw_observation_count(key, part):
    key = jax.random.fold_in(key, 11)
    key_base, key_full, key_hot = jax.random.split(key, 3)
    shape = (BANDS, STRIPS, STRIPS)
    base = jax.random.randint(key_base, shape, 0, 2 * CAP)
    full_strip = jax.random.randint(key_full, (BANDS, STRIPS, 1), 0, STRIPS)
    hot_strip = jax.random.randint(key_hot, (BANDS, 1, 1), 0, STRIPS)
    strips = jnp.arange(STRIPS, dtype=jnp.int32)[None, None, :]
    counts = jnp.minimum(base, CAP)
    counts = jnp.where((strips == full_strip) | (strips == hot_strip), CAP, counts)
    return counts.astype(jnp.int32)


def place_ends(entries, stream_key, smallest, high):
    longest = entries.shape.index(max(entries.shape))
    spots = []
    for shift in (0, 1):
        where = [jax.random.randint(jax.random.fold_in(stream_key, axis), (), 0, length) for axis, length in enumerate(entries.shape)]
        where[longest] = (where[longest] + shift) % entries.shape[longest]
        spots.append(tuple(where))
    return entries.at[spots[0]].set(smallest).at[spots[1]].set(high)


def levels(rng, extent, shards, least, high):
    def one(axis_at, shards_of):
        steps = jax.random.uniform(jax.random.fold_in(jax.random.fold_in(rng, 6), axis_at), (shards_of,), jnp.float32, least / len(shards), high / len(shards))
        return jnp.repeat(jnp.exp(steps), extent[axis_at] // shards_of).reshape((-1,) + (1,) * (len(extent) - axis_at - 1))

    gain = one(*shards[0])
    for cut in shards[1:]:
        gain = gain * one(*cut)
    return gain


def bell_draw(rng, shape, deviation, limit, shards=(), held_as=jnp.bfloat16):
    loudness = levels(rng, shape, shards, -0.22, 0.18) if shards else 1.0
    drawn = jax.random.normal(rng, shape, jnp.float32) * deviation * loudness
    return jnp.minimum(jnp.maximum(drawn, -limit), limit).astype(held_as)


def setup_inputs(seed: int = 0) -> dict:
    arg_keys = jax.random.split(jax.random.key(seed), 12)
    tokens = draw_tokens(jax.random.fold_in(arg_keys[11], 71), 0)
    query_key_value_weight = bell_draw(arg_keys[1], (MODEL_DIM, 3 * MODEL_DIM), MODEL_DIM ** -0.5, 0.25)
    output_weight = bell_draw(arg_keys[2], (MODEL_DIM, MODEL_DIM), MODEL_DIM ** -0.5, 0.25)
    adapter_down_map = bell_draw(arg_keys[3], (2, ADAPTER_RANK, MODEL_DIM), MODEL_DIM ** -0.5, 0.25)
    adapter_up_map = bell_draw(arg_keys[4], (2, ADAPTER_RANK, MODEL_DIM), ADAPTER_RANK ** -0.5, 2.0)
    relative_position_bias = draw_relative_position_bias(jax.random.fold_in(arg_keys[11], 71), 0)
    readout = bell_draw(arg_keys[6], (MODEL_DIM,), MODEL_DIM ** -0.5, 0.25)
    observation_index = place_ends(jax.random.randint(arg_keys[7], (BANDS, STRIPS, STRIPS, K, CAP), 0, LAT_DEV * LON_DEV), jax.random.fold_in(arg_keys[7], 1), 0, (LAT_DEV * LON_DEV) - 1).astype(jnp.int32)
    observation_weight = jnp.clip(0.05 + 0.95 * jax.random.uniform(arg_keys[8], (BANDS, STRIPS, STRIPS, K, CAP), jnp.float32) ** levels(arg_keys[8], (BANDS, STRIPS, STRIPS, K, CAP), ((0, 8), (1, 64)), -0.2, 0.2), 0.05, 1.0)
    observation_value = bell_draw(arg_keys[9], (BANDS, STRIPS, STRIPS, CAP), 1.0, 6.0, ((0, 8), (1, 64)), jnp.float32)
    observation_count = draw_observation_count(jax.random.fold_in(arg_keys[11], 71), 0)
    return {"tokens": tokens, "query_key_value_weight": query_key_value_weight, "output_weight": output_weight, "adapter_down_map": adapter_down_map, "adapter_up_map": adapter_up_map, "relative_position_bias": relative_position_bias, "readout": readout, "observation_index": observation_index, "observation_weight": observation_weight, "observation_value": observation_value, "observation_count": observation_count}


adapter_scale = 0.5
norm_eps = 1e-05
mask_fill = -1000000000.0

def split_into_windows(tile):
    n_rows, n_cols = (tile.shape[0], tile.shape[1])
    tail_shape = tile.shape[2:]
    blocks = tile.reshape((n_rows // WIN_LAT, WIN_LAT, n_cols // WIN_LON, WIN_LON) + tail_shape)
    blocks = jnp.swapaxes(blocks, 1, 2)
    return blocks.reshape((n_rows // WIN_LAT * (n_cols // WIN_LON), WIN_LAT * WIN_LON) + tail_shape)

def from_windows(window_tokens, n_rows, n_cols):
    tail_shape = window_tokens.shape[2:]
    blocks = window_tokens.reshape((n_rows // WIN_LAT, n_cols // WIN_LON, WIN_LAT, WIN_LON) + tail_shape)
    blocks = jnp.swapaxes(blocks, 1, 2)
    return blocks.reshape((n_rows, n_cols) + tail_shape)

def split_heads(array):
    return array.reshape(array.shape[:2] + (HEADS, HEAD_DIM))

def layer_norm(features):
    center = features - lax.optimization_barrier(jnp.mean(features, axis=-1, keepdims=True))
    spread = lax.optimization_barrier(jnp.mean(center * center, axis=-1, keepdims=True))
    return center * lax.rsqrt(spread + norm_eps)

def window_front_pass(window_tokens, window_region, query_key_value_weight, output_weight, adapter_down_map, adapter_up_map, relative_position_bias):
    width_of_model = window_tokens.shape[2]
    normalized_input = layer_norm(window_tokens.astype(jnp.float32)).astype(jnp.bfloat16)
    frozen_query_key_value = jnp.einsum('ntd,de->nte', normalized_input.astype(jnp.float32), query_key_value_weight.astype(jnp.float32))
    reduced_rank_input = jnp.einsum('qip,jyp->jqiy', normalized_input.astype(jnp.float32), adapter_down_map.astype(jnp.float32)).astype(jnp.bfloat16)
    adapter_update = adapter_scale * jnp.einsum('vwus,vso->vwuo', reduced_rank_input.astype(jnp.float32), adapter_up_map.astype(jnp.float32))
    query_rows = (frozen_query_key_value[..., :width_of_model] + adapter_update[0]).astype(jnp.bfloat16)
    key_rows = frozen_query_key_value[..., width_of_model:2 * width_of_model].astype(jnp.bfloat16)
    value_block_rows = (frozen_query_key_value[..., 2 * width_of_model:] + adapter_update[1]).astype(jnp.bfloat16)
    scale_factor = 1.0 / math.sqrt(HEAD_DIM)
    scores = jnp.einsum('nthe,nuhe->nhtu', split_heads(query_rows).astype(jnp.float32), split_heads(key_rows).astype(jnp.float32)) * scale_factor + relative_position_bias[None]
    same_region = (window_region[:, :, None] == window_region[:, None, :])[:, None]
    scores = jnp.where(same_region, scores, mask_fill)
    row_max = lax.optimization_barrier(jnp.max(scores, axis=-1, keepdims=True))
    raised = jnp.exp(scores - row_max)
    probs = raised / lax.optimization_barrier(jnp.sum(raised, axis=-1, keepdims=True))
    probs_bf = probs.astype(jnp.bfloat16)
    attended = jnp.einsum('nhtu,nuhe->nthe', probs_bf.astype(jnp.float32), split_heads(value_block_rows).astype(jnp.float32))
    attended = attended.reshape(window_tokens.shape).astype(jnp.bfloat16)
    projected = jnp.einsum('ntd,de->nte', attended.astype(jnp.float32), output_weight.astype(jnp.float32))
    output_rows = (window_tokens.astype(jnp.float32) + projected).astype(jnp.bfloat16)
    return (output_rows, (normalized_input, reduced_rank_input, key_rows, value_block_rows, probs, probs_bf))

def window_reverse_pass(input_gradient, stored_state, output_weight, adapter_up_map):
    normalized_input, reduced_rank_input, key_rows, value_block_rows, probs, probs_bf = stored_state
    grad_attn = jnp.einsum('nte,de->ntd', input_gradient.astype(jnp.float32), output_weight.astype(jnp.float32)).astype(jnp.bfloat16)
    heads_grad = split_heads(grad_attn).astype(jnp.float32)
    grad_probs = jnp.einsum('nthe,nuhe->nhtu', heads_grad, split_heads(value_block_rows).astype(jnp.float32))
    grad_value = jnp.einsum('nhtu,nthe->nuhe', probs_bf.astype(jnp.float32), heads_grad).reshape(input_gradient.shape)
    weighted_sum = lax.optimization_barrier(jnp.sum(grad_probs * probs, axis=-1, keepdims=True))
    grad_scores = (probs * (grad_probs - weighted_sum) / math.sqrt(HEAD_DIM)).astype(jnp.bfloat16)
    grad_query = jnp.einsum('nhtu,nuhe->nthe', grad_scores.astype(jnp.float32), split_heads(key_rows).astype(jnp.float32)).reshape(input_gradient.shape)
    paired_gradient = jnp.stack([grad_query, grad_value]).astype(jnp.bfloat16)
    up_map_gradient = adapter_scale * jnp.einsum('msqa,msqu->mau', reduced_rank_input.astype(jnp.float32), paired_gradient.astype(jnp.float32))
    low_rank_gradient = (adapter_scale * jnp.einsum('busf,baf->busa', paired_gradient.astype(jnp.float32), adapter_up_map.astype(jnp.float32))).astype(jnp.bfloat16)
    down_map_gradient = jnp.einsum('cntr,ntd->crd', low_rank_gradient.astype(jnp.float32), normalized_input.astype(jnp.float32))
    return (down_map_gradient, up_map_gradient)

def reference(tokens, query_key_value_weight, output_weight, adapter_down_map, adapter_up_map, relative_position_bias, readout, observation_index, observation_weight, observation_value, observation_count):
    cyclic_shifted = jnp.roll(tokens, (-SHIFT_LAT, -SHIFT_LON), axis=(0, 1))
    band_count = NLAT // WIN_LAT
    band_tokens = cyclic_shifted.reshape(band_count, WIN_LAT, NLON, MODEL_DIM)
    band_ids = jnp.arange(band_count, dtype=jnp.int32)

    def band_territory(band_number):
        global_row = band_number * WIN_LAT + jnp.arange(WIN_LAT, dtype=jnp.int32)
        region_rows = (global_row >= NLAT - SHIFT_LAT).astype(jnp.int32)
        return split_into_windows(jnp.broadcast_to(region_rows[:, None], (WIN_LAT, NLON)))

    def forward_band(packed):
        band_row_block, band_number = packed
        output_rows, stored_state = window_front_pass(split_into_windows(band_row_block), band_territory(band_number), query_key_value_weight, output_weight, adapter_down_map, adapter_up_map, relative_position_bias)
        return from_windows(output_rows, WIN_LAT, NLON)
    rolled_out = lax.map(forward_band, (band_tokens, band_ids)).reshape(NLAT, NLON, MODEL_DIM)
    block_out = jnp.roll(rolled_out, (SHIFT_LAT, SHIFT_LON), axis=(0, 1))
    obs_field = jnp.dot(block_out.reshape(NLAT * NLON, MODEL_DIM), readout, preferred_element_type=jnp.float32)
    tiles = obs_field.reshape(BANDS, LAT_DEV, STRIPS, LON_DEV).transpose(0, 2, 1, 3).reshape(BANDS, STRIPS, LAT_DEV * LON_DEV)
    band_axis = jnp.arange(BANDS, dtype=jnp.int32)[:, None, None, None, None]
    strip_axis = jnp.arange(STRIPS, dtype=jnp.int32)[None, None, :, None, None]
    predicted = lax.optimization_barrier(jnp.sum(observation_weight * tiles[band_axis, strip_axis, observation_index], axis=3))
    live_slots = jnp.arange(CAP, dtype=jnp.int32) < observation_count[..., None]
    innovation = jnp.where(live_slots, predicted - observation_value, 0.0)
    loss_scale = 1.0 / math.sqrt(BANDS * STRIPS)
    adjoint_terms = loss_scale * observation_weight * innovation[:, :, :, None, :]
    adjoint_tiles = jnp.zeros((BANDS, STRIPS, LAT_DEV * LON_DEV), jnp.float32).at[band_axis, strip_axis, observation_index].add(adjoint_terms)
    adjoint = adjoint_tiles.reshape(BANDS, STRIPS, LAT_DEV, LON_DEV).transpose(0, 2, 1, 3).reshape(NLAT, NLON)
    adjoint_field = jnp.roll(adjoint, (-SHIFT_LAT, -SHIFT_LON), axis=(0, 1))
    rolled_adjoint = adjoint_field * math.sqrt(BANDS * STRIPS)
    adjoint_rolled = adjoint_field.reshape(band_count, WIN_LAT, NLON)

    def backward_band(carry, packed):
        band_row_block, band_adjoint, band_number = packed
        output_rows, stored_state = window_front_pass(split_into_windows(band_row_block), band_territory(band_number), query_key_value_weight, output_weight, adapter_down_map, adapter_up_map, relative_position_bias)
        input_gradient = (band_adjoint[:, :, None] * readout.astype(jnp.float32)).astype(jnp.bfloat16)
        down_map_gradient, up_map_gradient = window_reverse_pass(split_into_windows(input_gradient), stored_state, output_weight, adapter_up_map)
        return ((carry[0] + down_map_gradient, carry[1] + up_map_gradient), None)
    empty = jnp.zeros((2, ADAPTER_RANK, MODEL_DIM), jnp.float32)
    totals, unused = lax.scan(backward_band, (empty, empty), (band_tokens, adjoint_rolled, band_ids))
    return (block_out, innovation, rolled_adjoint, totals[0], totals[1])
```

```python
import functools
import math

import jax
import jax.numpy as jnp
from jax import lax
from jax.experimental import pallas as pl
from jax.experimental.pallas import tpu as pltpu
from jax.sharding import PartitionSpec as P

F32 = jnp.float32
BF16 = jnp.bfloat16
HEADS = 16
HEAD_DIM = 32
MODEL = 512
GROUP = 24
SLOT = 32
LIVE = 18
OWN = 8 * GROUP
NORM_EPS = 1e-05
NEG = -1e30
NT = (((1,), (1,)), ((), ()))
TN = (((0,), (0,)), ((), ()))
NN = (((1,), (0,)), ((), ()))


def mm(a, b, dims=NN, precision=None):
    return lax.dot_general(a, b, dims, precision=precision, preferred_element_type=F32)


def exact(a, b, dims=NN):
    return mm(a, b, dims, precision=lax.Precision.HIGHEST)


def own_slot(n):
    half, row = n // 4, n % 4
    window_row, part = (row + 1) // 2, (row + 1) % 2
    return ((half * 3 + window_row) * 2 + (1 - half)) * 2 + part


def bias_kernel(bias_ref, out_ref, wide_ref):
    shape = (72, 128)
    lane = lax.broadcasted_iota(jnp.int32, shape, 1)
    row = lane % SLOT
    column = 12 * (3 * ((lane // SLOT) % 2) + row // 6) + 6 * (lane // 64) + row % 6
    hit = (column == lax.broadcasted_iota(jnp.int32, shape, 0)) & (row < LIVE)
    wide = exact(bias_ref[...], hit.astype(F32))
    lanes = lax.broadcasted_iota(jnp.int32, (1, 128), 1)
    wide = wide + jnp.where(lanes % SLOT < LIVE, 0.0, NEG)
    wide_ref[...] = wide.reshape(HEADS, 72, 128)
    out_ref[...] = jnp.zeros_like(out_ref)
    for parity in range(2):
        for half in range(2):
            for m in range(3):
                start = 12 * (3 * (1 - parity) + m) + 6 * (1 - half)
                out_ref[parity * 2 + half, :, 6 * m : 6 * m + 6, :] = wide_ref[:, start : start + 6, :]


def ordered_bias(bias):
    return pl.pallas_call(
        bias_kernel,
        out_shape=jax.ShapeDtypeStruct((4, HEADS, GROUP, 128), F32),
        scratch_shapes=[pltpu.VMEM((HEADS, 72, 128), F32)],
        cost_estimate=pl.CostEstimate(flops=2 * 10**8, bytes_accessed=2 * 10**6, transcendentals=0),
        name="ordered_bias",
    )(bias.reshape(HEADS * 72, 72))


def forward_kernel(
    flags_ref,
    own_ref,
    near_lon_ref,
    far_lon_ref,
    near_lat_ref,
    far_lat_ref,
    qkv_ref,
    wo_ref,
    down_ref,
    up_ref,
    readout_ref,
    bias_ref,
    block_ref,
    field_ref,
    probs_ref,
    gq_ref,
    low_ref,
    norm_ref,
    w_ref,
    k_ref,
    v_ref,
    q_ref,
    att_ref,
):
    even_lon = flags_ref[0] == 0
    even_lat = flags_ref[1] == 0
    first = flags_ref[2].astype(F32)
    last = flags_ref[3].astype(F32)

    def pick(cond, a, b):
        return jnp.where(cond, a.astype(F32), b.astype(F32))

    for strip in range(4):
        for group in range(6):
            if group == 0:
                x = pick(even_lat, far_lat_ref[strip], near_lat_ref[strip])
            elif group == 5:
                x = pick(even_lat, near_lat_ref[strip], far_lat_ref[strip])
            elif strip == 0:
                x = pick(even_lon, far_lon_ref[group - 1], near_lon_ref[group - 1])
            elif strip == 3:
                x = pick(even_lon, near_lon_ref[group - 1], far_lon_ref[group - 1])
            else:
                x = own_ref[strip - 1, group - 1].astype(F32)
            center = x - jnp.mean(x, axis=1, keepdims=True)
            spread = jnp.mean(center * center, axis=1, keepdims=True)
            y = center * lax.rsqrt(spread + NORM_EPS)
            y = jnp.concatenate([y, jnp.zeros((SLOT - GROUP, MODEL), F32)], axis=0).astype(BF16)
            slot = (((strip // 2) * 3 + group // 2) * 2 + strip % 2) * 2 + group % 2
            norm_ref[slot * SLOT : (slot + 1) * SLOT, :] = y

    normed = norm_ref[...]
    rank_row = lax.broadcasted_iota(jnp.int32, (16, MODEL), 0)
    up_half = 0.5 * up_ref[...].astype(F32)
    up_query = jnp.where(rank_row < 8, up_half, 0.0).astype(BF16)
    up_value = jnp.where(rank_row >= 8, up_half, 0.0).astype(BF16)
    low = mm(normed, down_ref[...], NT).astype(BF16)
    low_ref[...] = low
    k_ref[...] = mm(normed, qkv_ref[:, MODEL : 2 * MODEL]).astype(BF16)
    v_ref[...] = (mm(normed, qkv_ref[:, 2 * MODEL :]) + mm(low, up_value)).astype(BF16)
    own_rows = [slice(own_slot(n) * SLOT, (own_slot(n) + 1) * SLOT) for n in range(8)]
    normed_own = jnp.concatenate([norm_ref[rows, :] for rows in own_rows], axis=0)
    low_own = jnp.concatenate([low_ref[rows, :] for rows in own_rows], axis=0)
    query = mm(normed_own, qkv_ref[:, :MODEL]) + mm(low_own, up_query)
    q_ref[...] = query.astype(BF16).astype(F32)

    readout = jnp.broadcast_to(readout_ref[...].astype(F32), (8, MODEL)).astype(BF16)
    w_row = mm(readout, wo_ref[...], NT)
    w_ref[...] = w_row

    scale = 1.0 / math.sqrt(HEAD_DIM)
    head_of = lax.broadcasted_iota(jnp.int32, (8, 1, 256), 2) // HEAD_DIM
    head_mask = head_of == lax.broadcasted_iota(jnp.int32, (8, 1, 256), 0)
    lane_part = (lax.broadcasted_iota(jnp.int32, (1, 128), 1) // SLOT) % 2
    masked_first = jnp.where(lane_part == 0, NEG * first, 0.0)
    masked_last = jnp.where(lane_part == 1, NEG * last, 0.0)

    def fold(rows):
        return jnp.sum(jnp.where(head_mask, rows.reshape(8, GROUP, 256), 0.0), axis=0)

    for n in range(8):
        half, row = n // 4, n % 4
        window = half * 3 + (row + 1) // 2
        keys = slice(window * 128, (window + 1) * 128)
        for part in range(2):
            cols = slice(256 * part, 256 * (part + 1))
            k_win, v_win = k_ref[keys, cols], v_ref[keys, cols]
            q_own = q_ref[n * SLOT : n * SLOT + GROUP, cols]
            lhs = jnp.where(head_mask, q_own[None], 0.0).reshape(8 * GROUP, 256).astype(BF16)
            bias = bias_ref[(row % 2) * 2 + half, 8 * part : 8 * part + 8].reshape(8 * GROUP, 128)
            scores = mm(lhs, k_win, NT) * scale + bias
            if row == 0:
                scores = scores + masked_first
            if row == 3:
                scores = scores + masked_last
            raised = jnp.exp(scores - jnp.max(scores, axis=1, keepdims=True))
            probs = raised * (1.0 / jnp.sum(raised, axis=1, keepdims=True))
            probs_bf = probs.astype(BF16)
            probs_ref[n, 8 * GROUP * part : 8 * GROUP * (part + 1), :] = probs_bf
            att_ref[n * GROUP : (n + 1) * GROUP, cols] = fold(mm(probs_bf, v_win))
            w_masked = jnp.where(head_mask[:, 0, :], w_row[:, cols], 0.0)
            w_high = w_masked.astype(BF16).astype(F32)
            w_pair = jnp.concatenate([w_high, w_masked - w_high], axis=0).astype(BF16)
            v_pair = mm(w_pair, v_win, NT)
            v_w = (v_pair[:8] + v_pair[8:]).reshape(8, 1, 128)
            probs3 = probs.reshape(8, GROUP, 128)
            mean = jnp.sum(probs3 * v_w, axis=2, keepdims=True)
            slope = (probs3 * (v_w - mean) * scale).reshape(8 * GROUP, 128).astype(BF16)
            gq_ref[n * GROUP : (n + 1) * GROUP, cols] = fold(mm(slope, k_win))

    x_own = own_ref[...].astype(F32).reshape(OWN, MODEL)
    out = (x_own + mm(att_ref[...].astype(BF16), wo_ref[...])).astype(BF16)
    block_ref[...] = out
    field_ref[...] = jnp.zeros_like(field_ref)
    field_ref[:, :OWN] = mm(readout, out, NT)


def forward(flags, own, near_lon, far_lon, near_lat, far_lat, qkv, wo, down, up, readout, bias):
    shape = jax.ShapeDtypeStruct
    vmem = pl.BlockSpec(memory_space=pltpu.VMEM)
    return pl.pallas_call(
        forward_kernel,
        in_specs=[pl.BlockSpec(memory_space=pltpu.SMEM)] + [vmem] * 11,
        out_specs=[vmem] * 7,
        out_shape=[
            shape((OWN, MODEL), BF16),
            shape((8, 256), F32),
            shape((8, HEADS * GROUP, 128), BF16),
            shape((OWN, MODEL), F32),
            shape((24 * SLOT, 16), BF16),
            shape((24 * SLOT, MODEL), BF16),
            shape((8, MODEL), F32),
        ],
        scratch_shapes=[
            pltpu.VMEM((24 * SLOT, MODEL), BF16),
            pltpu.VMEM((24 * SLOT, MODEL), BF16),
            pltpu.VMEM((8 * SLOT, MODEL), F32),
            pltpu.VMEM((OWN, MODEL), F32),
        ],
        compiler_params=pltpu.CompilerParams(vmem_limit_bytes=40 * 1024 * 1024),
        cost_estimate=pl.CostEstimate(
            flops=3 * 10**9, bytes_accessed=8 * 10**6, transcendentals=4 * 10**5
        ),
        name="window_forward",
    )(flags, own, near_lon, far_lon, near_lat, far_lat, qkv, wo, down, up, readout, bias)


def observe_kernel(
    slots_ref,
    field_ref,
    probs_ref,
    gq_ref,
    low_ref,
    norm_ref,
    w_ref,
    up_ref,
    innov_ref,
    adjoint_ref,
    grads_ref,
    term_ref,
    place_ref,
    loss_scale,
):
    sources = innov_ref.shape[0]
    field_low = jnp.broadcast_to(field_ref[0:1, 0:128], (sources, 128))
    field_high = jnp.broadcast_to(field_ref[0:1, 128:256], (sources, 128))
    places, weights = [], []
    for pair in range(2):
        packed = slots_ref[pl.ds(pair, sources, stride=8), :].astype(jnp.int32)
        places += [packed & 1023, packed >> 10]
    predicted = jnp.zeros((sources, 128), F32)
    for k in range(4):
        lane = places[k] & 127
        picked = jnp.where(
            places[k] < 128,
            jnp.take_along_axis(field_low, lane, axis=1),
            jnp.take_along_axis(field_high, lane, axis=1),
        )
        weights.append(slots_ref[pl.ds(2 + k, sources, stride=8), :])
        predicted = predicted + weights[k] * picked
    innov = predicted - slots_ref[pl.ds(6, sources, stride=8), :]
    innov_ref[...] = innov
    for k in range(4):
        term_ref[k * sources : (k + 1) * sources, :] = weights[k] * innov
        place_ref[k * sources : (k + 1) * sources, :] = places[k]

    cell = lax.broadcasted_iota(jnp.int32, (OWN, 128), 0)

    def add_rows(step, total):
        for inner in range(8):
            at = step * 8 + inner
            hit = cell == place_ref[pl.ds(at, 1), :]
            total = total + jnp.where(hit, term_ref[pl.ds(at, 1), :], 0.0)
        return total

    total = lax.fori_loop(0, 4 * sources // 8, add_rows, jnp.zeros((OWN, 128), F32))
    adjoint = jnp.sum(total, axis=1, keepdims=True)
    adjoint_ref[...] = jnp.zeros_like(adjoint_ref)
    adjoint_ref[:, :OWN] = exact(jnp.ones((8, 128), F32), total, NT)

    def own_of(ref):
        blocks = [ref[own_slot(n) * SLOT : (own_slot(n) + 1) * SLOT, :].astype(F32)[:GROUP] for n in range(8)]
        return jnp.concatenate(blocks, axis=0)

    factor = 0.5 * loss_scale
    g_query = gq_ref[...].astype(BF16)
    up = up_ref[...]
    grad_low = mm(g_query, up, NT)
    up_query = mm((own_of(low_ref) * adjoint).astype(BF16), g_query, TN)
    down_query = mm((grad_low * adjoint).astype(BF16), own_of(norm_ref).astype(BF16), TN)

    weighted = [None] * 6
    for n in range(8):
        window = (n // 4) * 3 + (n % 4 + 1) // 2
        probs = probs_ref[n].astype(F32).reshape(HEADS, GROUP, 128)
        part = jnp.sum(probs * adjoint[n * GROUP : (n + 1) * GROUP].reshape(1, GROUP, 1), axis=1)
        weighted[window] = part if weighted[window] is None else weighted[window] + part
    weighted = jnp.concatenate(weighted, axis=1)
    head = lax.broadcasted_iota(jnp.int32, (HEADS, MODEL), 0)
    of_head = head == lax.broadcasted_iota(jnp.int32, (HEADS, MODEL), 1) // HEAD_DIM
    w_masked = jnp.where(of_head, jnp.broadcast_to(w_ref[0:1, :], (HEADS, MODEL)), 0.0)
    rank_head = exact(up.astype(F32), w_masked, NT)
    weighted_bf = weighted.astype(BF16)
    sums = mm(weighted_bf, low_ref[...])
    up_value = exact(sums, w_masked, TN)
    down_value = mm(exact(rank_head, weighted).astype(BF16), norm_ref[...])

    parts = (up_query[:8], up_value[8:], down_query[:8], down_value[8:])
    for m, part in enumerate(parts):
        part = part * factor
        for q in range(4):
            grads_ref[pl.ds(q * 32 + m, 8, stride=4), :] = part[:, 128 * q : 128 * (q + 1)]


def observe(slots, field, probs, gq, low, normed, w, up, loss_scale):
    sources = slots.shape[0] // 8
    shape = jax.ShapeDtypeStruct
    vmem = pl.BlockSpec(memory_space=pltpu.VMEM)
    return pl.pallas_call(
        functools.partial(observe_kernel, loss_scale=loss_scale),
        in_specs=[vmem] * 8,
        out_specs=[vmem] * 3,
        out_shape=[shape((sources, 128), F32), shape((8, 256), F32), shape((128, 128), F32)],
        scratch_shapes=[
            pltpu.VMEM((4 * sources, 128), F32),
            pltpu.VMEM((4 * sources, 128), jnp.int32),
        ],
        compiler_params=pltpu.CompilerParams(vmem_limit_bytes=32 * 1024 * 1024),
        cost_estimate=pl.CostEstimate(flops=10**8, bytes_accessed=4 * 10**6, transcendentals=0),
        name="observe",
    )(slots, field, probs, gq, low, normed, w, up)


def paired(value, axis, odd_first):
    count = lax.axis_size(axis)
    if odd_first:
        pairs = [(i, (i + 1) % count if i % 2 else (i - 1) % count) for i in range(count)]
    else:
        pairs = [(i, i ^ 1) for i in range(count)]
    return lax.ppermute(value, axis, pairs)


def shards(
    tokens,
    query_key_value_weight,
    output_weight,
    adapter_down_map,
    adapter_up_map,
    relative_position_bias,
    readout,
    observation_index,
    observation_weight,
    observation_value,
    observation_count,
):
    lat_count, lon_count = lax.axis_size("lat"), lax.axis_size("lon")
    lat, lon = lax.axis_index("lat"), lax.axis_index("lon")
    even_lat, even_lon = lat % 2 == 0, lon % 2 == 0

    own = tokens.reshape(4, 3, 2, 6, MODEL).transpose(2, 0, 1, 3, 4).reshape(2, 4, LIVE, MODEL)
    own = jnp.pad(own, ((0, 0), (0, 0), (0, GROUP - LIVE), (0, 0)))
    near_lon = paired(jnp.where(even_lon, own[1], own[0]), "lon", False)
    far_lon = paired(jnp.where(even_lon, own[0], own[1]), "lon", True)

    patch_row, patch_col = observation_index[0, 0] // 12, observation_index[0, 0] % 12
    place = ((patch_col // 6) * 4 + patch_row // 3) * GROUP + (patch_row % 3) * 6 + patch_col % 6
    live = jnp.arange(128, dtype=jnp.int32)[None, :] < observation_count[0, 0][:, None]
    slots = jnp.concatenate(
        [
            (place[:, 0::2] + 1024 * place[:, 1::2]).astype(F32),
            jnp.where(live[:, None, :], observation_weight[0, 0], 0.0),
            jnp.where(live[:, None, :], observation_value[0, 0][:, None, :], 0.0),
            jnp.zeros((lon_count, 1, 128), F32),
        ],
        axis=1,
    )
    slots = lax.all_to_all(slots, "lon", 0, 0, tiled=True).reshape(lon_count * 8, 128)

    left = jnp.where(even_lon, far_lon, near_lon)
    right = jnp.where(even_lon, near_lon, far_lon)
    top = jnp.stack([left[0], own[0, 0], own[1, 0], right[0]])
    bottom = jnp.stack([left[3], own[0, 3], own[1, 3], right[3]])
    near_lat = paired(jnp.where(even_lat, bottom, top), "lat", False)
    far_lat = paired(jnp.where(even_lat, top, bottom), "lat", True)

    flags = jnp.stack([lon % 2, lat % 2, (lat == 0).astype(jnp.int32), (lat == lat_count - 1).astype(jnp.int32)])
    down_rows = adapter_down_map.reshape(16, MODEL)
    up_rows = adapter_up_map.reshape(16, MODEL)
    block, field, probs, gq, low, normed, w = forward(
        flags.astype(jnp.int32),
        own,
        near_lon,
        far_lon,
        near_lat,
        far_lat,
        query_key_value_weight,
        output_weight,
        down_rows,
        up_rows,
        readout.reshape(1, MODEL),
        ordered_bias(relative_position_bias),
    )
    block = block.reshape(2, 4, GROUP, MODEL)[:, :, :LIVE].reshape(2, 4, 3, 6, MODEL)
    block_out = block.transpose(1, 2, 0, 3, 4).reshape(12, 12, MODEL)

    loss_scale = 1.0 / math.sqrt(lat_count * lon_count)
    innov, adjoint, grads = observe(slots, field, probs, gq, low, normed, w, up_rows, loss_scale)

    planes = [[i for i in range(lon_count) if (i // 2) % 2 == h] for h in range(2)]
    columns = [
        [a * lon_count + plane * 4 + h * 2 + c for h in range(2) for a in range(lat_count)]
        for plane in range(lon_count // 4)
        for c in range(2)
    ]
    chunks = lax.all_to_all(
        grads.reshape(32, 4, 128), "lon", 0, 0, axis_index_groups=planes, tiled=True
    )
    chunk = jnp.sum(chunks, axis=0).reshape(2, 1, 2, 128)
    adjoint_row = adjoint[0].reshape(1, 1, 2, 128)
    chunk = jnp.concatenate(
        [
            jnp.broadcast_to(chunk, (2, lat_count, 2, 128)),
            jnp.broadcast_to(adjoint_row, (2, lat_count, 2, 128)),
        ],
        axis=2,
    ).reshape(2 * lat_count, 4, 128)
    along = lax.all_to_all(chunk, ("lat", "lon"), 0, 0, axis_index_groups=columns, tiled=True)
    half = jnp.sum(along[:, :2], axis=0)
    below = lax.dynamic_index_in_dim(
        along, ((lon // 2) % 2) * lat_count + (lat + 1) % lat_count, 0, keepdims=False
    )[2:]
    below = below.reshape(256)[:OWN].reshape(2, 4, GROUP)
    here = adjoint[0, :OWN].reshape(2, 4, GROUP)
    moved = jnp.concatenate([here[:, 1:], below[:, :1]], axis=1)
    edge = jnp.pad(moved[0].reshape(1, 1, 4 * GROUP), ((0, 0), (0, 0), (0, 128 - 4 * GROUP)))
    last = jnp.concatenate(
        [
            jnp.broadcast_to(half[None], (lon_count, 2, 128)),
            innov[:, None, :],
            jnp.broadcast_to(edge, (lon_count, 1, 128)),
        ],
        axis=1,
    )
    final = lax.all_to_all(last, "lon", 0, 0, tiled=True)
    innovation = final[:, 2][None, None]
    beside = lax.dynamic_index_in_dim(final[:, 3], (lon + 1) % lon_count, 0, keepdims=False)
    beside = beside[: 4 * GROUP].reshape(4, GROUP)
    rolled = jnp.stack([moved[1], beside])[:, :, :LIVE].reshape(2, 4, 3, 6)
    rolled_adjoint = rolled.transpose(1, 2, 0, 3).reshape(12, 12)
    parts = final[:, :2].reshape(lon_count // 4, 2, 2, 2, 128)

    def whole(part):
        part = part.reshape(4, 8, 2, 128)
        return part.transpose(2, 1, 0, 3).reshape(2, 8, MODEL)

    return block_out, innovation, rolled_adjoint, whole(parts[:, 1]), whole(parts[:, 0])


def solution(mesh):
    return jax.shard_map(
        shards,
        mesh=mesh,
        in_specs=(
            P("lat", "lon", None),
            P(),
            P(),
            P(),
            P(),
            P(),
            P(),
            P("lat", "lon", None, None, None),
            P("lat", "lon", None, None, None),
            P("lat", "lon", None, None),
            P("lat", "lon", None),
        ),
        out_specs=(P("lat", "lon", None), P("lat", "lon", None, None), P("lat", "lon"), P(), P()),
        check_vma=False,
    )
```

```python
import functools
import math

import jax
import jax.numpy as jnp
from jax import lax
from jax.experimental import pallas as pl
from jax.experimental.pallas import tpu as pltpu
from jax.sharding import PartitionSpec as P

F32 = jnp.float32
BF16 = jnp.bfloat16
HEADS = 16
HEAD_DIM = 32
MODEL = 512
GROUP = 24
SLOT = 32
LIVE = 18
OWN = 8 * GROUP
NORM_EPS = 1e-05
NEG = -1e30
NT = (((1,), (1,)), ((), ()))
TN = (((0,), (0,)), ((), ()))
NN = (((1,), (0,)), ((), ()))


def mm(a, b, dims=NN, precision=None):
    return lax.dot_general(a, b, dims, precision=precision, preferred_element_type=F32)


def exact(a, b, dims=NN):
    return mm(a, b, dims, precision=lax.Precision.HIGHEST)


def own_slot(n):
    half, row = n // 4, n % 4
    window_row, part = (row + 1) // 2, (row + 1) % 2
    return ((half * 3 + window_row) * 2 + (1 - half)) * 2 + part


def bias_kernel(bias_ref, out_ref, wide_ref):
    shape = (72, 128)
    lane = lax.broadcasted_iota(jnp.int32, shape, 1)
    row = lane % SLOT
    column = 12 * (3 * ((lane // SLOT) % 2) + row // 6) + 6 * (lane // 64) + row % 6
    hit = (column == lax.broadcasted_iota(jnp.int32, shape, 0)) & (row < LIVE)
    wide = exact(bias_ref[...], hit.astype(F32))
    lanes = lax.broadcasted_iota(jnp.int32, (1, 128), 1)
    wide = wide + jnp.where(lanes % SLOT < LIVE, 0.0, NEG)
    wide_ref[...] = wide.reshape(HEADS, 72, 128)
    out_ref[...] = jnp.zeros_like(out_ref)
    for parity in range(2):
        for half in range(2):
            for m in range(3):
                start = 12 * (3 * (1 - parity) + m) + 6 * (1 - half)
                out_ref[parity * 2 + half, :, 6 * m : 6 * m + 6, :] = wide_ref[:, start : start + 6, :]


def ordered_bias(bias):
    return pl.pallas_call(
        bias_kernel,
        out_shape=jax.ShapeDtypeStruct((4, HEADS, GROUP, 128), F32),
        scratch_shapes=[pltpu.VMEM((HEADS, 72, 128), F32)],
        cost_estimate=pl.CostEstimate(flops=2 * 10**8, bytes_accessed=2 * 10**6, transcendentals=0),
        name="ordered_bias",
    )(bias.reshape(HEADS * 72, 72))


def forward_part(
    flags_ref,
    own_ref,
    near_lon_ref,
    far_lon_ref,
    near_lat_ref,
    far_lat_ref,
    qkv_hbm,
    wo_hbm,
    down_ref,
    up_ref,
    readout_ref,
    bias_hbm,
    block_ref,
    field_ref,
    probs_ref,
    gq_ref,
    low_ref,
    norm_ref,
    w_ref,
    k_ref,
    v_ref,
    q_ref,
    att_ref,
    qkv_ref,
    wo_ref,
    bias_ref,
    copy_sems,
):
    loads = [
        pltpu.make_async_copy(source, target, copy_sems.at[i])
        for i, (source, target) in enumerate(
            ((qkv_hbm, qkv_ref), (bias_hbm, bias_ref), (wo_hbm, wo_ref))
        )
    ]
    for load in loads:
        load.start()
    even_lon = flags_ref[0] == 0
    even_lat = flags_ref[1] == 0
    first = flags_ref[2].astype(F32)
    last = flags_ref[3].astype(F32)

    def pick(cond, a, b):
        return jnp.where(cond, a.astype(F32), b.astype(F32))

    for strip in range(4):
        for group in range(6):
            if group == 0:
                x = pick(even_lat, far_lat_ref[strip], near_lat_ref[strip])
            elif group == 5:
                x = pick(even_lat, near_lat_ref[strip], far_lat_ref[strip])
            elif strip == 0:
                x = pick(even_lon, far_lon_ref[group - 1], near_lon_ref[group - 1])
            elif strip == 3:
                x = pick(even_lon, near_lon_ref[group - 1], far_lon_ref[group - 1])
            else:
                x = own_ref[strip - 1, group - 1].astype(F32)
            center = x - jnp.mean(x, axis=1, keepdims=True)
            spread = jnp.mean(center * center, axis=1, keepdims=True)
            y = center * lax.rsqrt(spread + NORM_EPS)
            y = jnp.concatenate([y, jnp.zeros((SLOT - GROUP, MODEL), F32)], axis=0).astype(BF16)
            slot = (((strip // 2) * 3 + group // 2) * 2 + strip % 2) * 2 + group % 2
            norm_ref[slot * SLOT : (slot + 1) * SLOT, :] = y

    normed = norm_ref[...]
    for load in loads:
        load.wait()
    rank_row = lax.broadcasted_iota(jnp.int32, (16, MODEL), 0)
    up_half = 0.5 * up_ref[...].astype(F32)
    up_query = jnp.where(rank_row < 8, up_half, 0.0).astype(BF16)
    up_value = jnp.where(rank_row >= 8, up_half, 0.0).astype(BF16)
    low = mm(normed, down_ref[...], NT).astype(BF16)
    low_ref[...] = low
    k_ref[...] = mm(normed, qkv_ref[:, MODEL : 2 * MODEL]).astype(BF16)
    v_ref[...] = (mm(normed, qkv_ref[:, 2 * MODEL :]) + mm(low, up_value)).astype(BF16)
    own_rows = [slice(own_slot(n) * SLOT, (own_slot(n) + 1) * SLOT) for n in range(8)]
    normed_own = jnp.concatenate([norm_ref[rows, :] for rows in own_rows], axis=0)
    low_own = jnp.concatenate([low_ref[rows, :] for rows in own_rows], axis=0)
    query = mm(normed_own, qkv_ref[:, :MODEL]) + mm(low_own, up_query)
    q_ref[...] = query.astype(BF16).astype(F32)

    readout = jnp.broadcast_to(readout_ref[...].astype(F32), (8, MODEL)).astype(BF16)
    w_row = mm(readout, wo_ref[...], NT)
    w_ref[...] = w_row

    scale = 1.0 / math.sqrt(HEAD_DIM)
    head_of = lax.broadcasted_iota(jnp.int32, (8, 1, 256), 2) // HEAD_DIM
    head_mask = head_of == lax.broadcasted_iota(jnp.int32, (8, 1, 256), 0)
    lane_part = (lax.broadcasted_iota(jnp.int32, (1, 128), 1) // SLOT) % 2
    masked_first = jnp.where(lane_part == 0, NEG * first, 0.0)
    masked_last = jnp.where(lane_part == 1, NEG * last, 0.0)

    def fold(rows):
        return jnp.sum(jnp.where(head_mask, rows.reshape(8, GROUP, 256), 0.0), axis=0)

    for n in range(8):
        half, row = n // 4, n % 4
        window = half * 3 + (row + 1) // 2
        keys = slice(window * 128, (window + 1) * 128)
        for part in range(2):
            cols = slice(256 * part, 256 * (part + 1))
            k_win, v_win = k_ref[keys, cols], v_ref[keys, cols]
            q_own = q_ref[n * SLOT : n * SLOT + GROUP, cols]
            lhs = jnp.where(head_mask, q_own[None], 0.0).reshape(8 * GROUP, 256).astype(BF16)
            bias = bias_ref[(row % 2) * 2 + half, 8 * part : 8 * part + 8].reshape(8 * GROUP, 128)
            scores = mm(lhs, k_win, NT) * scale + bias
            if row == 0:
                scores = scores + masked_first
            if row == 3:
                scores = scores + masked_last
            raised = jnp.exp(scores - jnp.max(scores, axis=1, keepdims=True))
            probs = raised * (1.0 / jnp.sum(raised, axis=1, keepdims=True))
            probs_bf = probs.astype(BF16)
            probs_ref[n, 8 * GROUP * part : 8 * GROUP * (part + 1), :] = probs_bf
            att_ref[n * GROUP : (n + 1) * GROUP, cols] = fold(mm(probs_bf, v_win))
            w_masked = jnp.where(head_mask[:, 0, :], w_row[:, cols], 0.0)
            w_high = w_masked.astype(BF16).astype(F32)
            w_pair = jnp.concatenate([w_high, w_masked - w_high], axis=0).astype(BF16)
            v_pair = mm(w_pair, v_win, NT)
            v_w = (v_pair[:8] + v_pair[8:]).reshape(8, 1, 128)
            probs3 = probs.reshape(8, GROUP, 128)
            mean = jnp.sum(probs3 * v_w, axis=2, keepdims=True)
            slope = (probs3 * (v_w - mean) * scale).reshape(8 * GROUP, 128).astype(BF16)
            gq_ref[n * GROUP : (n + 1) * GROUP, cols] = fold(mm(slope, k_win))

    x_own = own_ref[...].astype(F32).reshape(OWN, MODEL)
    out = (x_own + mm(att_ref[...].astype(BF16), wo_ref[...])).astype(BF16)
    block_ref[...] = out
    field_ref[...] = jnp.zeros_like(field_ref)
    field_ref[:, :OWN] = mm(readout, out, NT)


def observe_part(
    flags_ref,
    slots_ref,
    field_ref,
    probs_ref,
    gq_ref,
    low_ref,
    norm_ref,
    w_ref,
    up_ref,
    adjoint_ref,
    sends_ref,
    innov_ref,
    term_ref,
    place_ref,
    loss_scale,
):
    sources = innov_ref.shape[0]
    field_low = jnp.broadcast_to(field_ref[0:1, 0:128], (sources, 128))
    field_high = jnp.broadcast_to(field_ref[0:1, 128:256], (sources, 128))
    places, weights = [], []
    for pair in range(2):
        packed = slots_ref[pl.ds(pair, sources, stride=8), :].astype(jnp.int32)
        places += [packed & 1023, packed >> 10]
    predicted = jnp.zeros((sources, 128), F32)
    for k in range(4):
        lane = places[k] & 127
        picked = jnp.where(
            places[k] < 128,
            jnp.take_along_axis(field_low, lane, axis=1),
            jnp.take_along_axis(field_high, lane, axis=1),
        )
        weights.append(slots_ref[pl.ds(2 + k, sources, stride=8), :])
        predicted = predicted + weights[k] * picked
    innov = predicted - slots_ref[pl.ds(6, sources, stride=8), :]
    innov_ref[...] = innov
    for k in range(4):
        term_ref[k * sources : (k + 1) * sources, :] = weights[k] * innov
        place_ref[k * sources : (k + 1) * sources, :] = places[k]

    cell = lax.broadcasted_iota(jnp.int32, (OWN, 128), 0)

    def add_rows(step, total):
        for inner in range(8):
            at = step * 8 + inner
            hit = cell == place_ref[pl.ds(at, 1), :]
            total = total + jnp.where(hit, term_ref[pl.ds(at, 1), :], 0.0)
        return total

    total = lax.fori_loop(0, 4 * sources // 8, add_rows, jnp.zeros((OWN, 128), F32))
    adjoint = jnp.sum(total, axis=1, keepdims=True)
    adjoint_ref[...] = jnp.zeros_like(adjoint_ref)
    adjoint_ref[:, :OWN] = exact(jnp.ones((8, 128), F32), total, NT)

    def own_of(ref):
        blocks = [ref[own_slot(n) * SLOT : (own_slot(n) + 1) * SLOT, :].astype(F32)[:GROUP] for n in range(8)]
        return jnp.concatenate(blocks, axis=0)

    factor = 0.5 * loss_scale
    g_query = gq_ref[...].astype(BF16)
    up = up_ref[...]
    grad_low = mm(g_query, up, NT)
    up_query = mm((own_of(low_ref) * adjoint).astype(BF16), g_query, TN)
    down_query = mm((grad_low * adjoint).astype(BF16), own_of(norm_ref).astype(BF16), TN)

    weighted = [None] * 6
    for n in range(8):
        window = (n // 4) * 3 + (n % 4 + 1) // 2
        probs = probs_ref[n].astype(F32).reshape(HEADS, GROUP, 128)
        part = jnp.sum(probs * adjoint[n * GROUP : (n + 1) * GROUP].reshape(1, GROUP, 1), axis=1)
        weighted[window] = part if weighted[window] is None else weighted[window] + part
    weighted = jnp.concatenate(weighted, axis=1)
    head = lax.broadcasted_iota(jnp.int32, (HEADS, MODEL), 0)
    of_head = head == lax.broadcasted_iota(jnp.int32, (HEADS, MODEL), 1) // HEAD_DIM
    w_masked = jnp.where(of_head, jnp.broadcast_to(w_ref[0:1, :], (HEADS, MODEL)), 0.0)
    rank_head = exact(up.astype(F32), w_masked, NT)
    weighted_bf = weighted.astype(BF16)
    sums = mm(weighted_bf, low_ref[...])
    up_value = exact(sums, w_masked, TN)
    down_value = mm(exact(rank_head, weighted).astype(BF16), norm_ref[...])

    sends_ref[...] = jnp.zeros_like(sends_ref)
    parts = (up_query[:8], up_value[8:], down_query[:8], down_value[8:])
    for m, part in enumerate(parts):
        part = part * factor
        for q in range(4):
            sends_ref[pl.ds(q * 64 + m, 8, stride=8), :] = part[:, 128 * q : 128 * (q + 1)]
    low_plane = flags_ref[4] == 0
    for core in range(2):
        planes = [innov_ref[pl.ds(2 * h + core, sources // 4, stride=4), :] for h in range(2)]
        mine = jnp.where(low_plane, planes[0], planes[1])
        other = jnp.where(low_plane, planes[1], planes[0])
        sends_ref[pl.ds(8 * core + 4, sources // 4, stride=16), :] = mine
        sends_ref[pl.ds(8 * core + 5, sources // 4, stride=16), :] = other


def core_kernel(
    flags_ref,
    own_ref,
    near_lon_ref,
    far_lon_ref,
    near_lat_ref,
    far_lat_ref,
    qkv_hbm,
    wo_hbm,
    down_ref,
    up_ref,
    readout_ref,
    bias_hbm,
    slots_hbm,
    block_ref,
    adjoint_ref,
    sends_ref,
    field_ref,
    probs_ref,
    gq_ref,
    low_ref,
    norm_ref,
    w_ref,
    k_ref,
    v_ref,
    q_ref,
    att_ref,
    qkv_ref,
    wo_ref,
    bias_ref,
    copy_sems,
    innov_ref,
    term_ref,
    place_ref,
    slots_ref,
    loss_scale,
):
    slot_load = pltpu.make_async_copy(slots_hbm, slots_ref, copy_sems.at[3])
    slot_load.start()
    forward_part(
        flags_ref,
        own_ref,
        near_lon_ref,
        far_lon_ref,
        near_lat_ref,
        far_lat_ref,
        qkv_hbm,
        wo_hbm,
        down_ref,
        up_ref,
        readout_ref,
        bias_hbm,
        block_ref,
        field_ref,
        probs_ref,
        gq_ref,
        low_ref,
        norm_ref,
        w_ref,
        k_ref,
        v_ref,
        q_ref,
        att_ref,
        qkv_ref,
        wo_ref,
        bias_ref,
        copy_sems,
    )
    slot_load.wait()
    observe_part(
        flags_ref,
        slots_ref,
        field_ref,
        probs_ref,
        gq_ref,
        low_ref,
        norm_ref,
        w_ref,
        up_ref,
        adjoint_ref,
        sends_ref,
        innov_ref,
        term_ref,
        place_ref,
        loss_scale,
    )


def core(flags, own, halos, qkv, wo, down, up, readout, bias, slots, loss_scale):
    sources = slots.shape[0] // 8
    shape = jax.ShapeDtypeStruct
    vmem, far = pl.BlockSpec(memory_space=pltpu.VMEM), pl.BlockSpec(memory_space=pl.ANY)
    smem = pl.BlockSpec(memory_space=pltpu.SMEM)
    return pl.pallas_call(
        functools.partial(core_kernel, loss_scale=loss_scale),
        in_specs=[smem] + [vmem] * 5 + [far] * 2 + [vmem] * 3 + [far] * 2,
        out_specs=[vmem] * 3,
        out_shape=[
            shape((OWN, MODEL), BF16),
            shape((8, 256), F32),
            shape((sources // 2 * 8, 128), F32),
        ],
        scratch_shapes=[
            pltpu.VMEM((8, 256), F32),
            pltpu.VMEM((8, HEADS * GROUP, 128), BF16),
            pltpu.VMEM((OWN, MODEL), F32),
            pltpu.VMEM((24 * SLOT, 16), BF16),
            pltpu.VMEM((24 * SLOT, MODEL), BF16),
            pltpu.VMEM((8, MODEL), F32),
            pltpu.VMEM((24 * SLOT, MODEL), BF16),
            pltpu.VMEM((24 * SLOT, MODEL), BF16),
            pltpu.VMEM((8 * SLOT, MODEL), F32),
            pltpu.VMEM((OWN, MODEL), F32),
            pltpu.VMEM((MODEL, 3 * MODEL), BF16),
            pltpu.VMEM((MODEL, MODEL), BF16),
            pltpu.VMEM((4, HEADS, GROUP, 128), F32),
            pltpu.SemaphoreType.DMA((4,)),
            pltpu.VMEM((sources, 128), F32),
            pltpu.VMEM((4 * sources, 128), F32),
            pltpu.VMEM((4 * sources, 128), jnp.int32),
            pltpu.VMEM((sources * 8, 128), F32),
        ],
        compiler_params=pltpu.CompilerParams(vmem_limit_bytes=58 * 1024 * 1024),
        cost_estimate=pl.CostEstimate(
            flops=3 * 10**9, bytes_accessed=8 * 10**6, transcendentals=4 * 10**5
        ),
        name="window_and_observe",
    )(flags, own, *halos, qkv, wo, down, up, readout, bias, slots)


BLOCK = 48


def scatter_kernel(chunks_ref, adjoint_ref, out_ref, rows_ref):
    total = jnp.sum(chunks_ref[...].reshape(-1, 8, 128), axis=0)
    rows_ref[...] = jnp.zeros_like(rows_ref)
    for at, values in ((0, total[0:4]), (8, None)):
        if values is None:
            values = jnp.concatenate([adjoint_ref[0:1, :128], adjoint_ref[0:1, 128:]], axis=0)
        high = values.astype(BF16).astype(F32)
        count = values.shape[0]
        rows_ref[at : at + count, :] = high
        rows_ref[at + count : at + 2 * count, :] = values - high
    head = rows_ref[...].astype(BF16)
    members = chunks_ref.shape[0] // 8
    other = chunks_ref[pl.ds(5, members, stride=8), :].astype(BF16)
    for at in range(out_ref.shape[0] // BLOCK):
        out_ref[at * BLOCK : at * BLOCK + 16, :] = head
        out_ref[at * BLOCK + 16 : (at + 1) * BLOCK, :] = other


def scatter(chunks, adjoint, members):
    vmem = pl.BlockSpec(memory_space=pltpu.VMEM)
    return pl.pallas_call(
        scatter_kernel,
        in_specs=[vmem] * 2,
        out_specs=vmem,
        out_shape=jax.ShapeDtypeStruct((members * BLOCK, 128), BF16),
        scratch_shapes=[pltpu.VMEM((16, 128), F32)],
        name="scatter_rows",
    )(chunks, adjoint)


def gather_kernel(flags_ref, along_ref, chunks_ref, adjoint_ref, out_ref, innov_ref, moved_ref):
    lat_count = along_ref.shape[0] // BLOCK // 2
    plane, lat = flags_ref[4], flags_ref[5]
    next_lat = jnp.where(lat == lat_count - 1, 0, lat + 1)

    def rows_of(h, a):
        start = pl.multiple_of((h * lat_count + a) * BLOCK, 16)
        return along_ref[pl.ds(start, 16), :].astype(F32)

    def adjoint_of(rows):
        values = rows[8:10] + rows[10:12]
        return jnp.concatenate([values[0:1], values[1:2]], axis=1)

    lane = lax.broadcasted_iota(jnp.int32, (1, 256), 1)

    def shift_rows(here, below):
        kept = pltpu.roll(here, 256 - GROUP, 1)
        new = pltpu.roll(below, 3 * GROUP, 1)
        return jnp.where(lane % (4 * GROUP) < 3 * GROUP, kept, new)

    moved = shift_rows(adjoint_ref[0:1, :], adjoint_of(rows_of(plane, next_lat)))
    twin = shift_rows(
        adjoint_of(rows_of(1 - plane, lat)), adjoint_of(rows_of(1 - plane, next_lat))
    )
    moved_ref[...] = jnp.broadcast_to(moved, (8, 256))

    total = jnp.zeros((16, 128), F32)
    for at in range(2 * lat_count):
        total = total + along_ref[at * BLOCK : at * BLOCK + 16, :].astype(F32)
    total = total[0:4] + total[4:8]
    block = jnp.concatenate([total, moved[:, :128], twin[:, :128], jnp.zeros((2, 128), F32)], axis=0)
    members = out_ref.shape[0] // 8
    for at in range(members):
        out_ref[at * 8 : at * 8 + 8, :] = block

    near = chunks_ref[pl.ds(4, members, stride=8), :]
    start = pl.multiple_of(((1 - plane) * lat_count + lat) * BLOCK + 16, 16)
    far = along_ref[pl.ds(start, members), :].astype(F32)
    low_plane = plane == 0
    planes = (jnp.where(low_plane, near, far), jnp.where(low_plane, far, near))
    for h in range(2):
        for m in range(members // 2):
            innov_ref[4 * m + 2 * h : 4 * m + 2 * h + 2, :] = planes[h][2 * m : 2 * m + 2]


def gather(flags, along, chunks, adjoint):
    members = chunks.shape[0] // 8
    shape = jax.ShapeDtypeStruct
    vmem = pl.BlockSpec(memory_space=pltpu.VMEM)
    return pl.pallas_call(
        gather_kernel,
        in_specs=[pl.BlockSpec(memory_space=pltpu.SMEM)] + [vmem] * 3,
        out_specs=[vmem] * 3,
        out_shape=[shape((members * 8, 128), F32), shape((2 * members, 128), F32), shape((8, 256), F32)],
        name="gather_rows",
    )(flags, along, chunks, adjoint)


def finish_kernel(flags_ref, final_ref, moved_ref, up_ref, down_ref, rolled_ref):
    for m, (ref, which) in enumerate(((up_ref, 0), (up_ref, 1), (down_ref, 0), (down_ref, 1))):
        for q in range(4):
            ref[which, :, 128 * q : 128 * (q + 1)] = final_ref[pl.ds(q * 64 + m, 8, stride=8), :]
    members = final_ref.shape[0] // 8
    plane, member = flags_ref[4], flags_ref[6]
    across = member - 1 + 2 * plane
    across = jnp.where(across >= members, 0, across)
    row = jnp.where(flags_ref[0] == 0, (member + 1) * 8 + 4, across * 8 + 5)
    beside = final_ref[pl.ds(row, 1), :]
    moved = pltpu.roll(moved_ref[0:1, :], 256 - 4 * GROUP, 1)[:, :128]
    lane = lax.broadcasted_iota(jnp.int32, (16, 128), 1)
    out_row = lax.broadcasted_iota(jnp.int32, (16, 128), 0)
    in_group = lane % GROUP
    belongs = (lane // GROUP * 3 + in_group // 6 == out_row) & (in_group < LIVE) & (lane < 4 * GROUP)
    from_lane = lax.broadcasted_iota(jnp.int32, (128, 128), 0)
    to_lane = lax.broadcasted_iota(jnp.int32, (128, 128), 1)
    out = jnp.zeros((16, 128), F32)
    for half, values in enumerate((moved, beside)):
        place = (from_lane % GROUP % 6 + 6 * half == to_lane).astype(F32)
        out = out + exact(jnp.where(belongs, values, 0.0), place)
    rolled_ref[...] = out[:12, :12]


def finish(flags, final, moved):
    shape = jax.ShapeDtypeStruct
    vmem = pl.BlockSpec(memory_space=pltpu.VMEM)
    return pl.pallas_call(
        finish_kernel,
        in_specs=[pl.BlockSpec(memory_space=pltpu.SMEM)] + [vmem] * 2,
        out_specs=[vmem] * 3,
        out_shape=[shape((2, 8, MODEL), F32), shape((2, 8, MODEL), F32), shape((12, 12), F32)],
        name="finish_rows",
    )(flags, final, moved)


def paired(value, axis, odd_first):
    count = lax.axis_size(axis)
    if odd_first:
        pairs = [(i, (i + 1) % count if i % 2 else (i - 1) % count) for i in range(count)]
    else:
        pairs = [(i, i ^ 1) for i in range(count)]
    return lax.ppermute(value, axis, pairs)


def shards(
    tokens,
    query_key_value_weight,
    output_weight,
    adapter_down_map,
    adapter_up_map,
    relative_position_bias,
    readout,
    observation_index,
    observation_weight,
    observation_value,
    observation_count,
):
    lat_count, lon_count = lax.axis_size("lat"), lax.axis_size("lon")
    lat, lon = lax.axis_index("lat"), lax.axis_index("lon")
    even_lat, even_lon = lat % 2 == 0, lon % 2 == 0

    own = tokens.reshape(4, 3, 2, 6, MODEL).transpose(2, 0, 1, 3, 4).reshape(2, 4, LIVE, MODEL)
    own = jnp.pad(own, ((0, 0), (0, 0), (0, GROUP - LIVE), (0, 0)))
    near_lon = paired(jnp.where(even_lon, own[1], own[0]), "lon", False)
    far_lon = paired(jnp.where(even_lon, own[0], own[1]), "lon", True)

    patch_row, patch_col = observation_index[0, 0] // 12, observation_index[0, 0] % 12
    place = ((patch_col // 6) * 4 + patch_row // 3) * GROUP + (patch_row % 3) * 6 + patch_col % 6
    live = jnp.arange(128, dtype=jnp.int32)[None, :] < observation_count[0, 0][:, None]
    slots = jnp.concatenate(
        [
            (place[:, 0::2] + 1024 * place[:, 1::2]).astype(F32),
            jnp.where(live[:, None, :], observation_weight[0, 0], 0.0),
            jnp.where(live[:, None, :], observation_value[0, 0][:, None, :], 0.0),
            jnp.zeros((lon_count, 1, 128), F32),
        ],
        axis=1,
    )
    left = jnp.where(even_lon, far_lon, near_lon)
    right = jnp.where(even_lon, near_lon, far_lon)
    top = jnp.stack([left[0], own[0, 0], own[1, 0], right[0]])
    bottom = jnp.stack([left[3], own[0, 3], own[1, 3], right[3]])
    near_send = jnp.where(even_lat, bottom, top)
    far_send = jnp.where(even_lat, top, bottom)
    near_lat = paired(near_send, "lat", False)
    far_lat = paired(far_send, "lat", True)
    slots, near_lat, far_lat = lax.optimization_barrier((slots, near_lat, far_lat))
    slots = lax.all_to_all(slots, "lon", 0, 0, tiled=True).reshape(lon_count * 8, 128)

    plane, member = (lon // 2) % 2, lon // 4 * 2 + lon % 2
    flags = jnp.stack(
        [lon % 2, lat % 2, lat == 0, lat == lat_count - 1, plane, lat, member, lon]
    ).astype(jnp.int32)
    down_rows = adapter_down_map.reshape(16, MODEL)
    up_rows = adapter_up_map.reshape(16, MODEL)
    loss_scale = 1.0 / math.sqrt(lat_count * lon_count)
    block, adjoint, sends = core(
        flags,
        own,
        (near_lon, far_lon, near_lat, far_lat),
        query_key_value_weight,
        output_weight,
        down_rows,
        up_rows,
        readout.reshape(1, MODEL),
        ordered_bias(relative_position_bias),
        slots,
        loss_scale,
    )
    block = block.reshape(2, 4, GROUP, MODEL)[:, :, :LIVE].reshape(2, 4, 3, 6, MODEL)
    block_out = block.transpose(1, 2, 0, 3, 4).reshape(12, 12, MODEL)

    planes = [[i for i in range(lon_count) if (i // 2) % 2 == h] for h in range(2)]
    columns = [
        [a * lon_count + at * 4 + h * 2 + c for h in range(2) for a in range(lat_count)]
        for at in range(lon_count // 4)
        for c in range(2)
    ]

    def in_plane(rows):
        rows = rows.reshape(lon_count // 2, 8, 128)
        rows = lax.all_to_all(rows, "lon", 0, 0, axis_index_groups=planes, tiled=True)
        return rows.reshape(lon_count * 4, 128)

    chunks = in_plane(sends)
    along = scatter(chunks, adjoint, 2 * lat_count).reshape(2 * lat_count, BLOCK, 128)
    along = lax.all_to_all(along, ("lat", "lon"), 0, 0, axis_index_groups=columns, tiled=True)
    final, innovation, moved = gather(flags, along.reshape(-1, 128), chunks, adjoint)
    up_gradient, down_gradient, rolled_adjoint = finish(flags, in_plane(final), moved)
    return block_out, innovation[None, None], rolled_adjoint, down_gradient, up_gradient


def solution(mesh):
    return jax.shard_map(
        shards,
        mesh=mesh,
        in_specs=(
            P("lat", "lon", None),
            P(),
            P(),
            P(),
            P(),
            P(),
            P(),
            P("lat", "lon", None, None, None),
            P("lat", "lon", None, None, None),
            P("lat", "lon", None, None),
            P("lat", "lon", None),
        ),
        out_specs=(P("lat", "lon", None), P("lat", "lon", None, None), P("lat", "lon"), P(), P()),
        check_vma=False,
    )
```

```python
import functools
import math

import jax
import jax.numpy as jnp
from jax import lax
from jax.experimental import pallas as pl
from jax.experimental.pallas import tpu as pltpu
from jax.sharding import PartitionSpec as P

F32 = jnp.float32
BF16 = jnp.bfloat16
HEADS = 16
HEAD_DIM = 32
MODEL = 512
GROUP = 24
SLOT = 32
LIVE = 18
OWN = 8 * GROUP
NORM_EPS = 1e-05
NEG = -1e30
NT = (((1,), (1,)), ((), ()))
TN = (((0,), (0,)), ((), ()))
NN = (((1,), (0,)), ((), ()))


def mm(a, b, dims=NN, precision=None):
    return lax.dot_general(a, b, dims, precision=precision, preferred_element_type=F32)


def exact(a, b, dims=NN):
    return mm(a, b, dims, precision=lax.Precision.HIGHEST)


def own_slot(n):
    half, row = n // 4, n % 4
    window_row, part = (row + 1) // 2, (row + 1) % 2
    return ((half * 3 + window_row) * 2 + (1 - half)) * 2 + part


def bias_kernel(bias_ref, out_ref, wide_ref):
    shape = (72, 128)
    lane = lax.broadcasted_iota(jnp.int32, shape, 1)
    row = lane % SLOT
    column = 12 * (3 * ((lane // SLOT) % 2) + row // 6) + 6 * (lane // 64) + row % 6
    hit = (column == lax.broadcasted_iota(jnp.int32, shape, 0)) & (row < LIVE)
    wide = exact(bias_ref[...], hit.astype(F32))
    lanes = lax.broadcasted_iota(jnp.int32, (1, 128), 1)
    wide = wide + jnp.where(lanes % SLOT < LIVE, 0.0, NEG)
    wide_ref[...] = wide.reshape(HEADS, 72, 128)
    out_ref[...] = jnp.zeros_like(out_ref)
    for parity in range(2):
        for half in range(2):
            for m in range(3):
                start = 12 * (3 * (1 - parity) + m) + 6 * (1 - half)
                out_ref[parity * 2 + half, :, 6 * m : 6 * m + 6, :] = wide_ref[:, start : start + 6, :]


def ordered_bias(bias):
    return pl.pallas_call(
        bias_kernel,
        out_shape=jax.ShapeDtypeStruct((4, HEADS, GROUP, 128), F32),
        scratch_shapes=[pltpu.VMEM((HEADS, 72, 128), F32)],
        cost_estimate=pl.CostEstimate(flops=2 * 10**10, bytes_accessed=2 * 10**6, transcendentals=0),
        name="ordered_bias",
    )(bias.reshape(HEADS * 72, 72))


def forward_part(
    flags_ref,
    own_ref,
    near_lon_ref,
    far_lon_ref,
    near_lat_ref,
    far_lat_ref,
    qkv_hbm,
    wo_hbm,
    down_ref,
    up_ref,
    readout_ref,
    bias_hbm,
    block_ref,
    field_ref,
    probs_ref,
    gq_ref,
    low_ref,
    norm_ref,
    w_ref,
    k_ref,
    v_ref,
    q_ref,
    att_ref,
    qkv_ref,
    wo_ref,
    bias_ref,
    copy_sems,
):
    loads = [
        pltpu.make_async_copy(source, target, copy_sems.at[i])
        for i, (source, target) in enumerate(
            ((qkv_hbm, qkv_ref), (bias_hbm, bias_ref), (wo_hbm, wo_ref))
        )
    ]
    for load in loads:
        load.start()
    even_lon = flags_ref[0] == 0
    even_lat = flags_ref[1] == 0
    first = flags_ref[2].astype(F32)
    last = flags_ref[3].astype(F32)

    def pick(cond, a, b):
        return jnp.where(cond, a.astype(F32), b.astype(F32))

    for strip in range(4):
        for group in range(6):
            if group == 0:
                x = pick(even_lat, far_lat_ref[strip], near_lat_ref[strip])
            elif group == 5:
                x = pick(even_lat, near_lat_ref[strip], far_lat_ref[strip])
            elif strip == 0:
                x = pick(even_lon, far_lon_ref[group - 1], near_lon_ref[group - 1])
            elif strip == 3:
                x = pick(even_lon, near_lon_ref[group - 1], far_lon_ref[group - 1])
            else:
                x = own_ref[strip - 1, group - 1].astype(F32)
            center = x - jnp.mean(x, axis=1, keepdims=True)
            spread = jnp.mean(center * center, axis=1, keepdims=True)
            y = center * lax.rsqrt(spread + NORM_EPS)
            y = jnp.concatenate([y, jnp.zeros((SLOT - GROUP, MODEL), F32)], axis=0).astype(BF16)
            slot = (((strip // 2) * 3 + group // 2) * 2 + strip % 2) * 2 + group % 2
            norm_ref[slot * SLOT : (slot + 1) * SLOT, :] = y

    normed = norm_ref[...]
    for load in loads:
        load.wait()
    rank_row = lax.broadcasted_iota(jnp.int32, (16, MODEL), 0)
    up_half = 0.5 * up_ref[...].astype(F32)
    up_query = jnp.where(rank_row < 8, up_half, 0.0).astype(BF16)
    up_value = jnp.where(rank_row >= 8, up_half, 0.0).astype(BF16)
    low = mm(normed, down_ref[...], NT).astype(BF16)
    low_ref[...] = low
    k_ref[...] = mm(normed, qkv_ref[:, MODEL : 2 * MODEL]).astype(BF16)
    v_ref[...] = (mm(normed, qkv_ref[:, 2 * MODEL :]) + mm(low, up_value)).astype(BF16)
    own_rows = [slice(own_slot(n) * SLOT, (own_slot(n) + 1) * SLOT) for n in range(8)]
    normed_own = jnp.concatenate([norm_ref[rows, :] for rows in own_rows], axis=0)
    low_own = jnp.concatenate([low_ref[rows, :] for rows in own_rows], axis=0)
    query = mm(normed_own, qkv_ref[:, :MODEL]) + mm(low_own, up_query)
    q_ref[...] = query.astype(BF16).astype(F32)

    readout = jnp.broadcast_to(readout_ref[...].astype(F32), (8, MODEL)).astype(BF16)
    w_row = mm(readout, wo_ref[...], NT)
    w_ref[...] = w_row

    scale = 1.0 / math.sqrt(HEAD_DIM)
    head_of = lax.broadcasted_iota(jnp.int32, (8, 1, 256), 2) // HEAD_DIM
    head_mask = head_of == lax.broadcasted_iota(jnp.int32, (8, 1, 256), 0)
    lane_part = (lax.broadcasted_iota(jnp.int32, (1, 128), 1) // SLOT) % 2
    masked_first = jnp.where(lane_part == 0, NEG * first, 0.0)
    masked_last = jnp.where(lane_part == 1, NEG * last, 0.0)

    def fold(rows):
        return jnp.sum(jnp.where(head_mask, rows.reshape(8, GROUP, 256), 0.0), axis=0)

    for n in range(8):
        half, row = n // 4, n % 4
        window = half * 3 + (row + 1) // 2
        keys = slice(window * 128, (window + 1) * 128)
        for part in range(2):
            cols = slice(256 * part, 256 * (part + 1))
            k_win, v_win = k_ref[keys, cols], v_ref[keys, cols]
            q_own = q_ref[n * SLOT : n * SLOT + GROUP, cols]
            lhs = jnp.where(head_mask, q_own[None], 0.0).reshape(8 * GROUP, 256).astype(BF16)
            bias = bias_ref[(row % 2) * 2 + half, 8 * part : 8 * part + 8].reshape(8 * GROUP, 128)
            scores = mm(lhs, k_win, NT) * scale + bias
            if row == 0:
                scores = scores + masked_first
            if row == 3:
                scores = scores + masked_last
            raised = jnp.exp(scores - jnp.max(scores, axis=1, keepdims=True))
            probs = raised * (1.0 / jnp.sum(raised, axis=1, keepdims=True))
            probs_bf = probs.astype(BF16)
            probs_ref[n, 8 * GROUP * part : 8 * GROUP * (part + 1), :] = probs_bf
            att_ref[n * GROUP : (n + 1) * GROUP, cols] = fold(mm(probs_bf, v_win))
            w_masked = jnp.where(head_mask[:, 0, :], w_row[:, cols], 0.0)
            w_high = w_masked.astype(BF16).astype(F32)
            w_pair = jnp.concatenate([w_high, w_masked - w_high], axis=0).astype(BF16)
            v_pair = mm(w_pair, v_win, NT)
            v_w = (v_pair[:8] + v_pair[8:]).reshape(8, 1, 128)
            probs3 = probs.reshape(8, GROUP, 128)
            mean = jnp.sum(probs3 * v_w, axis=2, keepdims=True)
            slope = (probs3 * (v_w - mean) * scale).reshape(8 * GROUP, 128).astype(BF16)
            gq_ref[n * GROUP : (n + 1) * GROUP, cols] = fold(mm(slope, k_win))

    x_own = own_ref[...].astype(F32).reshape(OWN, MODEL)
    out = (x_own + mm(att_ref[...].astype(BF16), wo_ref[...])).astype(BF16)
    block_ref[...] = out
    field_ref[...] = jnp.zeros_like(field_ref)
    field_ref[:, :OWN] = mm(readout, out, NT)


def observe_part(
    slots_ref,
    field_ref,
    probs_ref,
    gq_ref,
    low_ref,
    norm_ref,
    w_ref,
    up_ref,
    adjoint_ref,
    grads_ref,
    innov_ref,
    term_ref,
    place_ref,
    loss_scale,
):
    sources = innov_ref.shape[0]
    field_low = jnp.broadcast_to(field_ref[0:1, 0:128], (sources, 128))
    field_high = jnp.broadcast_to(field_ref[0:1, 128:256], (sources, 128))
    places, weights = [], []
    for pair in range(2):
        packed = slots_ref[pl.ds(pair, sources, stride=8), :].astype(jnp.int32)
        places += [packed & 1023, packed >> 10]
    predicted = jnp.zeros((sources, 128), F32)
    for k in range(4):
        lane = places[k] & 127
        picked = jnp.where(
            places[k] < 128,
            jnp.take_along_axis(field_low, lane, axis=1),
            jnp.take_along_axis(field_high, lane, axis=1),
        )
        weights.append(slots_ref[pl.ds(2 + k, sources, stride=8), :])
        predicted = predicted + weights[k] * picked
    innov = predicted - slots_ref[pl.ds(6, sources, stride=8), :]
    innov_ref[...] = innov
    for k in range(4):
        term_ref[k * sources : (k + 1) * sources, :] = weights[k] * innov
        place_ref[k * sources : (k + 1) * sources, :] = places[k]

    cell = lax.broadcasted_iota(jnp.int32, (OWN, 128), 0)

    def add_rows(step, total):
        for inner in range(8):
            at = step * 8 + inner
            hit = cell == place_ref[pl.ds(at, 1), :]
            total = total + jnp.where(hit, term_ref[pl.ds(at, 1), :], 0.0)
        return total

    total = lax.fori_loop(0, 4 * sources // 8, add_rows, jnp.zeros((OWN, 128), F32))
    adjoint = jnp.sum(total, axis=1, keepdims=True)
    adjoint_ref[...] = jnp.zeros_like(adjoint_ref)
    adjoint_ref[:, :OWN] = exact(jnp.ones((8, 128), F32), total, NT)

    def own_of(ref):
        blocks = [ref[own_slot(n) * SLOT : (own_slot(n) + 1) * SLOT, :].astype(F32)[:GROUP] for n in range(8)]
        return jnp.concatenate(blocks, axis=0)

    factor = 0.5 * loss_scale
    g_query = gq_ref[...].astype(BF16)
    up = up_ref[...]
    grad_low = mm(g_query, up, NT)
    up_query = mm((own_of(low_ref) * adjoint).astype(BF16), g_query, TN)
    down_query = mm((grad_low * adjoint).astype(BF16), own_of(norm_ref).astype(BF16), TN)

    weighted = [None] * 6
    for n in range(8):
        window = (n // 4) * 3 + (n % 4 + 1) // 2
        probs = probs_ref[n].astype(F32).reshape(HEADS, GROUP, 128)
        part = jnp.sum(probs * adjoint[n * GROUP : (n + 1) * GROUP].reshape(1, GROUP, 1), axis=1)
        weighted[window] = part if weighted[window] is None else weighted[window] + part
    weighted = jnp.concatenate(weighted, axis=1)
    head = lax.broadcasted_iota(jnp.int32, (HEADS, MODEL), 0)
    of_head = head == lax.broadcasted_iota(jnp.int32, (HEADS, MODEL), 1) // HEAD_DIM
    w_masked = jnp.where(of_head, jnp.broadcast_to(w_ref[0:1, :], (HEADS, MODEL)), 0.0)
    rank_head = exact(up.astype(F32), w_masked, NT)
    weighted_bf = weighted.astype(BF16)
    sums = mm(weighted_bf, low_ref[...])
    up_value = exact(sums, w_masked, TN)
    down_value = mm(exact(rank_head, weighted).astype(BF16), norm_ref[...])

    parts = (up_query[:8], up_value[8:], down_query[:8], down_value[8:])
    for m, part in enumerate(parts):
        part = part * factor
        for q in range(4):
            grads_ref[pl.ds(q * 32 + m, 8, stride=4), :] = part[:, 128 * q : 128 * (q + 1)]


def core_kernel(
    flags_ref,
    own_ref,
    near_lon_ref,
    far_lon_ref,
    near_lat_ref,
    far_lat_ref,
    qkv_hbm,
    wo_hbm,
    down_ref,
    up_ref,
    readout_ref,
    bias_hbm,
    slots_hbm,
    block_ref,
    adjoint_ref,
    grads_ref,
    innov_ref,
    field_ref,
    probs_ref,
    gq_ref,
    low_ref,
    norm_ref,
    w_ref,
    k_ref,
    v_ref,
    q_ref,
    att_ref,
    qkv_ref,
    wo_ref,
    bias_ref,
    copy_sems,
    term_ref,
    place_ref,
    slots_ref,
    loss_scale,
):
    slot_load = pltpu.make_async_copy(slots_hbm, slots_ref, copy_sems.at[3])
    slot_load.start()
    forward_part(
        flags_ref,
        own_ref,
        near_lon_ref,
        far_lon_ref,
        near_lat_ref,
        far_lat_ref,
        qkv_hbm,
        wo_hbm,
        down_ref,
        up_ref,
        readout_ref,
        bias_hbm,
        block_ref,
        field_ref,
        probs_ref,
        gq_ref,
        low_ref,
        norm_ref,
        w_ref,
        k_ref,
        v_ref,
        q_ref,
        att_ref,
        qkv_ref,
        wo_ref,
        bias_ref,
        copy_sems,
    )
    slot_load.wait()
    observe_part(
        slots_ref,
        field_ref,
        probs_ref,
        gq_ref,
        low_ref,
        norm_ref,
        w_ref,
        up_ref,
        adjoint_ref,
        grads_ref,
        innov_ref,
        term_ref,
        place_ref,
        loss_scale,
    )


def core(flags, own, halos, qkv, wo, down, up, readout, bias, slots, loss_scale):
    sources = slots.shape[0] // 8
    shape = jax.ShapeDtypeStruct
    vmem, far = pl.BlockSpec(memory_space=pltpu.VMEM), pl.BlockSpec(memory_space=pl.ANY)
    smem = pl.BlockSpec(memory_space=pltpu.SMEM)
    return pl.pallas_call(
        functools.partial(core_kernel, loss_scale=loss_scale),
        in_specs=[smem] + [vmem] * 5 + [far] * 2 + [vmem] * 3 + [far] * 2,
        out_specs=[vmem] * 4,
        out_shape=[
            shape((OWN, MODEL), BF16),
            shape((8, 256), F32),
            shape((128, 128), F32),
            shape((sources, 128), F32),
        ],
        scratch_shapes=[
            pltpu.VMEM((8, 256), F32),
            pltpu.VMEM((8, HEADS * GROUP, 128), BF16),
            pltpu.VMEM((OWN, MODEL), F32),
            pltpu.VMEM((24 * SLOT, 16), BF16),
            pltpu.VMEM((24 * SLOT, MODEL), BF16),
            pltpu.VMEM((8, MODEL), F32),
            pltpu.VMEM((24 * SLOT, MODEL), BF16),
            pltpu.VMEM((24 * SLOT, MODEL), BF16),
            pltpu.VMEM((8 * SLOT, MODEL), F32),
            pltpu.VMEM((OWN, MODEL), F32),
            pltpu.VMEM((MODEL, 3 * MODEL), BF16),
            pltpu.VMEM((MODEL, MODEL), BF16),
            pltpu.VMEM((4, HEADS, GROUP, 128), F32),
            pltpu.SemaphoreType.DMA((4,)),
            pltpu.VMEM((4 * sources, 128), F32),
            pltpu.VMEM((4 * sources, 128), jnp.int32),
            pltpu.VMEM((sources * 8, 128), F32),
        ],
        compiler_params=pltpu.CompilerParams(vmem_limit_bytes=58 * 1024 * 1024),
        cost_estimate=pl.CostEstimate(
            flops=3 * 10**9, bytes_accessed=8 * 10**6, transcendentals=4 * 10**5
        ),
        name="window_and_observe",
    )(flags, own, *halos, qkv, wo, down, up, readout, bias, slots)


def paired(value, axis, odd_first):
    count = lax.axis_size(axis)
    if odd_first:
        pairs = [(i, (i + 1) % count if i % 2 else (i - 1) % count) for i in range(count)]
    else:
        pairs = [(i, i ^ 1) for i in range(count)]
    return lax.ppermute(value, axis, pairs)


def shards(
    tokens,
    query_key_value_weight,
    output_weight,
    adapter_down_map,
    adapter_up_map,
    relative_position_bias,
    readout,
    observation_index,
    observation_weight,
    observation_value,
    observation_count,
):
    lat_count, lon_count = lax.axis_size("lat"), lax.axis_size("lon")
    lat, lon = lax.axis_index("lat"), lax.axis_index("lon")
    even_lat, even_lon = lat % 2 == 0, lon % 2 == 0

    own = tokens.reshape(4, 3, 2, 6, MODEL).transpose(2, 0, 1, 3, 4).reshape(2, 4, LIVE, MODEL)
    own = jnp.pad(own, ((0, 0), (0, 0), (0, GROUP - LIVE), (0, 0)))
    near_send, far_send, observation_index = lax.optimization_barrier(
        (
            jnp.where(even_lon, own[1], own[0]),
            jnp.where(even_lon, own[0], own[1]),
            observation_index,
        )
    )
    near_lon = paired(near_send, "lon", False)
    far_lon = paired(far_send, "lon", True)

    patch_row, patch_col = observation_index[0, 0] // 12, observation_index[0, 0] % 12
    place = ((patch_col // 6) * 4 + patch_row // 3) * GROUP + (patch_row % 3) * 6 + patch_col % 6
    live = jnp.arange(128, dtype=jnp.int32)[None, :] < observation_count[0, 0][:, None]
    slots = jnp.concatenate(
        [
            (place[:, 0::2] + 1024 * place[:, 1::2]).astype(F32),
            jnp.where(live[:, None, :], observation_weight[0, 0], 0.0),
            jnp.where(live[:, None, :], observation_value[0, 0][:, None, :], 0.0),
            jnp.zeros((lon_count, 1, 128), F32),
        ],
        axis=1,
    )
    left = jnp.where(even_lon, far_lon, near_lon)
    right = jnp.where(even_lon, near_lon, far_lon)
    top = jnp.stack([left[0], own[0, 0], own[1, 0], right[0]])
    bottom = jnp.stack([left[3], own[0, 3], own[1, 3], right[3]])
    near_send = jnp.where(even_lat, bottom, top)
    far_send = jnp.where(even_lat, top, bottom)
    near_send, far_send, bias = lax.optimization_barrier(
        (near_send, far_send, relative_position_bias)
    )
    near_lat = paired(near_send, "lat", False)
    far_lat = paired(far_send, "lat", True)
    slots = lax.all_to_all(slots, "lon", 0, 0, tiled=True).reshape(lon_count * 8, 128)

    flags = jnp.stack([lon % 2, lat % 2, lat == 0, lat == lat_count - 1]).astype(jnp.int32)
    down_rows = adapter_down_map.reshape(16, MODEL)
    up_rows = adapter_up_map.reshape(16, MODEL)
    loss_scale = 1.0 / math.sqrt(lat_count * lon_count)
    block, adjoint, grads, innov = core(
        flags,
        own,
        (near_lon, far_lon, near_lat, far_lat),
        query_key_value_weight,
        output_weight,
        down_rows,
        up_rows,
        readout.reshape(1, MODEL),
        ordered_bias(bias),
        slots,
        loss_scale,
    )
    block = block.reshape(2, 4, GROUP, MODEL)[:, :, :LIVE].reshape(2, 4, 3, 6, MODEL)
    block_out = block.transpose(1, 2, 0, 3, 4).reshape(12, 12, MODEL)

    planes = [[i for i in range(lon_count) if (i // 2) % 2 == h] for h in range(2)]
    columns = [
        [a * lon_count + plane * 4 + h * 2 + c for h in range(2) for a in range(lat_count)]
        for plane in range(lon_count // 4)
        for c in range(2)
    ]
    chunks = lax.all_to_all(
        grads.reshape(32, 4, 128), "lon", 0, 0, axis_index_groups=planes, tiled=True
    )
    chunk = jnp.sum(chunks, axis=0).reshape(2, 1, 2, 128)
    adjoint_row = adjoint[0].reshape(1, 1, 2, 128)
    chunk = jnp.concatenate(
        [
            jnp.broadcast_to(chunk, (2, lat_count, 2, 128)),
            jnp.broadcast_to(adjoint_row, (2, lat_count, 2, 128)),
        ],
        axis=2,
    ).reshape(2 * lat_count, 4, 128)
    along = lax.all_to_all(chunk, ("lat", "lon"), 0, 0, axis_index_groups=columns, tiled=True)
    half = jnp.sum(along[:, :2], axis=0)
    below = lax.dynamic_index_in_dim(
        along, ((lon // 2) % 2) * lat_count + (lat + 1) % lat_count, 0, keepdims=False
    )[2:]
    below = below.reshape(256)[:OWN].reshape(2, 4, GROUP)
    here = adjoint[0, :OWN].reshape(2, 4, GROUP)
    moved = jnp.concatenate([here[:, 1:], below[:, :1]], axis=1)
    edge = jnp.pad(moved[0].reshape(1, 1, 4 * GROUP), ((0, 0), (0, 0), (0, 128 - 4 * GROUP)))
    last = jnp.concatenate(
        [
            jnp.broadcast_to(half[None], (lon_count, 2, 128)),
            innov[:, None, :],
            jnp.broadcast_to(edge, (lon_count, 1, 128)),
        ],
        axis=1,
    )
    final = lax.all_to_all(last, "lon", 0, 0, tiled=True)
    innovation = final[:, 2][None, None]
    beside = lax.dynamic_index_in_dim(final[:, 3], (lon + 1) % lon_count, 0, keepdims=False)
    beside = beside[: 4 * GROUP].reshape(4, GROUP)
    rolled = jnp.stack([moved[1], beside])[:, :, :LIVE].reshape(2, 4, 3, 6)
    rolled_adjoint = rolled.transpose(1, 2, 0, 3).reshape(12, 12)
    parts = final[:, :2].reshape(lon_count // 4, 2, 2, 2, 128)

    def whole(part):
        part = part.reshape(4, 8, 2, 128)
        return part.transpose(2, 1, 0, 3).reshape(2, 8, MODEL)

    return block_out, innovation, rolled_adjoint, whole(parts[:, 1]), whole(parts[:, 0])


def solution(mesh):
    return jax.shard_map(
        shards,
        mesh=mesh,
        in_specs=(
            P("lat", "lon", None),
            P(),
            P(),
            P(),
            P(),
            P(),
            P(),
            P("lat", "lon", None, None, None),
            P("lat", "lon", None, None, None),
            P("lat", "lon", None, None),
            P("lat", "lon", None),
        ),
        out_specs=(P("lat", "lon", None), P("lat", "lon", None, None), P("lat", "lon"), P(), P()),
        check_vma=False,
    )
```

```python
import functools
import math

import jax
import jax.numpy as jnp
from jax import lax
from jax.experimental import pallas as pl
from jax.experimental.pallas import tpu as pltpu
from jax.sharding import PartitionSpec as P

F32 = jnp.float32
BF16 = jnp.bfloat16
HEADS = 16
HEAD_DIM = 32
MODEL = 512
GROUP = 24
WINDOW = 4 * GROUP
LIVE = 18
OWN = 8 * GROUP
NORM_EPS = 1e-05
NEG = -1e30
NT = (((1,), (1,)), ((), ()))
TN = (((0,), (0,)), ((), ()))
NN = (((1,), (0,)), ((), ()))


def mm(a, b, dims=NN, precision=None):
    return lax.dot_general(a, b, dims, precision=precision, preferred_element_type=F32)


def exact(a, b, dims=NN):
    return mm(a, b, dims, precision=lax.Precision.HIGHEST)


def bias_kernel(bias_ref, out_ref, wide_ref):
    shape = (72, WINDOW)
    lane = lax.broadcasted_iota(jnp.int32, shape, 1)
    row = lane % GROUP
    column = 12 * (3 * ((lane // GROUP) % 2) + row // 6) + 6 * (lane // (2 * GROUP)) + row % 6
    hit = (column == lax.broadcasted_iota(jnp.int32, shape, 0)) & (row < LIVE)
    wide = exact(bias_ref[...], hit.astype(F32))
    lanes = lax.broadcasted_iota(jnp.int32, (1, WINDOW), 1)
    wide = wide + jnp.where(lanes % GROUP < LIVE, 0.0, NEG)
    wide_ref[...] = wide.reshape(HEADS, 72, WINDOW)
    out_ref[...] = jnp.zeros_like(out_ref)
    for parity in range(2):
        for half in range(2):
            for m in range(3):
                start = 12 * (3 * (1 - parity) + m) + 6 * (1 - half)
                out_ref[parity * 2 + half, :, 6 * m : 6 * m + 6, :] = wide_ref[:, start : start + 6, :]


def ordered_bias(bias):
    return pl.pallas_call(
        bias_kernel,
        out_shape=jax.ShapeDtypeStruct((4, HEADS, GROUP, WINDOW), F32),
        scratch_shapes=[pltpu.VMEM((HEADS, 72, WINDOW), F32)],
        cost_estimate=pl.CostEstimate(flops=2 * 10**10, bytes_accessed=2 * 10**6, transcendentals=0),
        name="ordered_bias",
    )(bias.reshape(HEADS * 72, 72))


def slots_kernel(index_ref, weight_ref, value_ref, count_ref, out_ref):
    strips = value_ref.shape[0]
    square = (strips, strips)
    own_lane = lax.broadcasted_iota(jnp.int32, square, 0) == lax.broadcasted_iota(jnp.int32, square, 1)
    counts = jnp.broadcast_to(count_ref[...].astype(F32), square)
    counts = jnp.sum(jnp.where(own_lane, counts, 0.0), axis=1, keepdims=True).astype(jnp.int32)
    live = lax.broadcasted_iota(jnp.int32, (strips, 128), 1) < counts
    places = []
    for k in range(4):
        cell = index_ref[pl.ds(k, strips, stride=4), :]
        row = (cell * 171) >> 11
        col = cell - 12 * row
        group = (row * 11) >> 5
        half = (col >= 6).astype(jnp.int32)
        places.append((half * 4 + group) * GROUP + (row - 3 * group) * 6 + col - 6 * half)
        weight = weight_ref[pl.ds(k, strips, stride=4), :]
        out_ref[pl.ds(2 + k, strips, stride=8), :] = jnp.where(live, weight, 0.0)
    for pair in range(2):
        packed = places[2 * pair] + 1024 * places[2 * pair + 1]
        out_ref[pl.ds(pair, strips, stride=8), :] = packed.astype(F32)
    out_ref[pl.ds(6, strips, stride=8), :] = jnp.where(live, value_ref[...], 0.0)
    out_ref[pl.ds(7, strips, stride=8), :] = jnp.zeros((strips, 128), F32)


def packed_slots(index, weight, value, count):
    return pl.pallas_call(
        slots_kernel,
        out_shape=jax.ShapeDtypeStruct((value.shape[0] * 8, 128), F32),
        cost_estimate=pl.CostEstimate(flops=10**6, bytes_accessed=5 * 10**5, transcendentals=0),
        name="packed_slots",
    )(index, weight, value, count)


def forward_part(
    lat_count,
    own_ref,
    near_lon_ref,
    far_lon_ref,
    near_lat_ref,
    far_lat_ref,
    qkv_hbm,
    wo_hbm,
    down_ref,
    up_ref,
    readout_ref,
    bias_hbm,
    block_ref,
    field_ref,
    probs_ref,
    gq_ref,
    low_ref,
    norm_ref,
    own_norm_ref,
    low_own_ref,
    w_ref,
    k_ref,
    v_ref,
    q_ref,
    att_ref,
    qkv_ref,
    wo_ref,
    bias_ref,
    copy_sems,
):
    loads = [
        pltpu.make_async_copy(source, target, copy_sems.at[i])
        for i, (source, target) in enumerate(
            ((qkv_hbm, qkv_ref), (bias_hbm, bias_ref), (wo_hbm, wo_ref))
        )
    ]
    for load in loads:
        load.start()
    lat = lax.axis_index("lat")
    even_lon = lax.axis_index("lon") % 2 == 0
    even_lat = lat % 2 == 0
    first = (lat == 0).astype(F32)
    last = (lat == lat_count - 1).astype(F32)

    def padded(x):
        return jnp.concatenate([x, jnp.zeros((GROUP - LIVE, MODEL), F32)], axis=0)

    def pick(cond, a, b):
        return jnp.where(cond, a.astype(F32), b.astype(F32))

    def piece(strip, group):
        if group == 0:
            return pick(even_lat, far_lat_ref[strip], near_lat_ref[strip])
        if group == 5:
            return pick(even_lat, near_lat_ref[strip], far_lat_ref[strip])
        if strip == 0:
            return pick(even_lon, far_lon_ref[group - 1], near_lon_ref[group - 1])
        if strip == 3:
            return pick(even_lon, near_lon_ref[group - 1], far_lon_ref[group - 1])
        return own_ref[strip - 1, group - 1].astype(F32)

    for strip in range(4):
        rows = []
        for pair in range(3):
            x = jnp.concatenate([padded(piece(strip, 2 * pair + i)) for i in range(2)], axis=0)
            center = x - jnp.mean(x, axis=1, keepdims=True)
            spread = jnp.mean(center * center, axis=1, keepdims=True)
            y = center * lax.rsqrt(spread + NORM_EPS)
            at = ((strip // 2) * 3 + pair) * WINDOW + (strip % 2) * 2 * GROUP
            norm_ref[at : at + 2 * GROUP, :] = y.astype(BF16)
            rows.append(y)
        if strip in (1, 2):
            mine = jnp.concatenate([rows[0][GROUP:], rows[1], rows[2][:GROUP]], axis=0)
            own_norm_ref[(strip - 1) * 4 * GROUP : strip * 4 * GROUP, :] = mine.astype(BF16)

    normed = norm_ref[...]
    for load in loads:
        load.wait()
    rank_row = lax.broadcasted_iota(jnp.int32, (16, MODEL), 0)
    up_half = 0.5 * up_ref[...].astype(F32)
    up_query = jnp.where(rank_row < 8, up_half, 0.0).astype(BF16)
    up_value = jnp.where(rank_row >= 8, up_half, 0.0).astype(BF16)
    low = mm(normed, down_ref[...], NT).astype(BF16)
    low_ref[...] = low
    k_ref[...] = mm(normed, qkv_ref[:, MODEL : 2 * MODEL]).astype(BF16)
    v_ref[...] = (mm(normed, qkv_ref[:, 2 * MODEL :]) + mm(low, up_value)).astype(BF16)
    normed_own = own_norm_ref[...]
    low_own = mm(normed_own, down_ref[...], NT).astype(BF16)
    low_own_ref[...] = low_own.astype(F32)
    query = mm(normed_own, qkv_ref[:, :MODEL]) + mm(low_own, up_query)
    q_ref[...] = query.astype(BF16).astype(F32)

    readout = jnp.broadcast_to(readout_ref[...].astype(F32), (8, MODEL)).astype(BF16)
    w_row = mm(readout, wo_ref[...], NT)
    w_ref[...] = w_row

    scale = 1.0 / math.sqrt(HEAD_DIM)
    head_of = lax.broadcasted_iota(jnp.int32, (8, 1, 256), 2) // HEAD_DIM
    head_mask = head_of == lax.broadcasted_iota(jnp.int32, (8, 1, 256), 0)
    lane_part = (lax.broadcasted_iota(jnp.int32, (1, WINDOW), 1) // GROUP) % 2
    masked_first = jnp.where(lane_part == 0, NEG * first, 0.0)
    masked_last = jnp.where(lane_part == 1, NEG * last, 0.0)

    ones = jnp.ones((WINDOW, WINDOW), BF16)

    def fold(rows):
        return jnp.sum(jnp.where(head_mask, rows.reshape(8, GROUP, 256), 0.0), axis=0)

    for n in range(8):
        half, row = n // 4, n % 4
        window = half * 3 + (row + 1) // 2
        keys = slice(window * WINDOW, (window + 1) * WINDOW)
        for part in range(2):
            cols = slice(256 * part, 256 * (part + 1))
            k_win, v_win = k_ref[keys, cols], v_ref[keys, cols]
            q_own = q_ref[n * GROUP : (n + 1) * GROUP, cols]
            lhs = jnp.where(head_mask, q_own[None], 0.0).reshape(8 * GROUP, 256).astype(BF16)
            bias = bias_ref[(row % 2) * 2 + half, 8 * part : 8 * part + 8].reshape(8 * GROUP, WINDOW)
            scores = mm(lhs, k_win, NT) * scale + bias
            if row == 0:
                scores = scores + masked_first
            if row == 3:
                scores = scores + masked_last
            raised = jnp.exp(scores - jnp.max(scores, axis=1, keepdims=True))
            probs = raised * (1.0 / jnp.sum(raised, axis=1, keepdims=True))
            probs_bf = probs.astype(BF16)
            probs_ref[n, 8 * GROUP * part : 8 * GROUP * (part + 1), :] = probs_bf
            att_ref[n * GROUP : (n + 1) * GROUP, cols] = fold(mm(probs_bf, v_win))
            w_masked = jnp.where(head_mask[:, 0, :], w_row[:, cols], 0.0)
            w_high = w_masked.astype(BF16).astype(F32)
            w_pair = jnp.concatenate([w_high, w_masked - w_high], axis=0).astype(BF16)
            v_pair = mm(w_pair, v_win, NT)
            v_w = (v_pair[:8] + v_pair[8:]).reshape(8, 1, WINDOW)
            v_w = jnp.broadcast_to(v_w, (8, GROUP, WINDOW)).reshape(8 * GROUP, WINDOW)
            share = probs * v_w
            share_high = share.astype(BF16)
            share_low = (share - share_high.astype(F32)).astype(BF16)
            mean = jnp.sum(share, axis=1, keepdims=True)
            slope = (probs * (v_w - mean) * scale).astype(BF16)
            gq_ref[n * GROUP : (n + 1) * GROUP, cols] = fold(mm(slope, k_win))

    x_own = [padded(own_ref[n // 4, n % 4].astype(F32)) for n in range(8)]
    x_own = jnp.concatenate(x_own, axis=0)
    out = (x_own + mm(att_ref[...].astype(BF16), wo_ref[...])).astype(BF16)
    block_ref[...] = out
    field_ref[...] = jnp.zeros_like(field_ref)
    field_ref[:, :OWN] = mm(readout, out, NT)


def observe_part(
    slots_ref,
    field_ref,
    probs_ref,
    gq_ref,
    low_ref,
    norm_ref,
    own_norm_ref,
    low_own_ref,
    w_ref,
    up_ref,
    adjoint_ref,
    grads_ref,
    innov_ref,
    term_ref,
    place_ref,
    loss_scale,
):
    sources = innov_ref.shape[0]
    field_low = jnp.broadcast_to(field_ref[0:1, 0:128], (sources, 128))
    field_high = jnp.broadcast_to(field_ref[0:1, 128:256], (sources, 128))
    places, weights = [], []
    for pair in range(2):
        packed = slots_ref[pl.ds(pair, sources, stride=8), :].astype(jnp.int32)
        places += [packed & 1023, packed >> 10]
    predicted = jnp.zeros((sources, 128), F32)
    for k in range(4):
        lane = places[k] & 127
        picked = jnp.where(
            places[k] < 128,
            jnp.take_along_axis(field_low, lane, axis=1),
            jnp.take_along_axis(field_high, lane, axis=1),
        )
        weights.append(slots_ref[pl.ds(2 + k, sources, stride=8), :])
        predicted = predicted + weights[k] * picked
    innov = predicted - slots_ref[pl.ds(6, sources, stride=8), :]
    innov_ref[...] = innov
    for k in range(4):
        rows = slice(k * sources, (k + 1) * sources)
        term = weights[k] * innov
        high = term.astype(BF16).astype(F32)
        term_ref[0, rows, :] = high
        term_ref[1, rows, :] = term - high
        place_ref[0, rows, :] = places[k] >> 4
        place_ref[1, rows, :] = places[k] & 15

    digit = lax.broadcasted_iota(jnp.int32, (16, 128), 0)
    per_step = 32

    def add_rows(step, total):
        left, right = [], []
        for inner in range(per_step):
            at = pl.ds(step * per_step + inner, 1)
            left.append(jnp.where(digit == place_ref[0, at, :], 1.0, 0.0).astype(BF16))
            hit = digit == place_ref[1, at, :]
            terms = [jnp.where(hit, term_ref[i, at, :], 0.0) for i in range(2)]
            right.append(jnp.concatenate(terms, axis=0).astype(BF16))
        return total + mm(jnp.concatenate(left, axis=1), jnp.concatenate(right, axis=1), NT)

    total = lax.fori_loop(0, 4 * sources // per_step, add_rows, jnp.zeros((16, 32), F32))
    total = total[:, :16] + total[:, 16:]

    def cells(shape, axis):
        cell = lax.broadcasted_iota(jnp.int32, shape, axis)
        digits = lax.broadcasted_iota(jnp.int32, shape, 1 - axis)
        return cell // 16 == digits, cell % 16 == digits

    high, low = cells((OWN, 16), 0)
    column = exact(high.astype(F32), total)
    adjoint = jnp.sum(jnp.where(low, column, 0.0), axis=1, keepdims=True)
    high, low = cells((16, OWN), 1)
    row = jnp.sum(jnp.where(high, exact(total, low.astype(F32)), 0.0), axis=0, keepdims=True)
    adjoint_ref[...] = jnp.zeros_like(adjoint_ref)
    adjoint_ref[0:1, :OWN] = row

    factor = 0.5 * loss_scale
    g_query = gq_ref[...].astype(BF16)
    up = up_ref[...]
    grad_low = mm(g_query, up, NT)
    up_query = mm((low_own_ref[...] * adjoint).astype(BF16), g_query, TN)
    down_query = mm((grad_low * adjoint).astype(BF16), own_norm_ref[...], TN)

    weighted = [None] * 6
    for n in range(8):
        window = (n // 4) * 3 + (n % 4 + 1) // 2
        probs = probs_ref[n].astype(F32).reshape(HEADS, GROUP, WINDOW)
        part = jnp.sum(probs * adjoint[n * GROUP : (n + 1) * GROUP].reshape(1, GROUP, 1), axis=1)
        weighted[window] = part if weighted[window] is None else weighted[window] + part
    head = lax.broadcasted_iota(jnp.int32, (HEADS, MODEL), 0)
    of_head = head == lax.broadcasted_iota(jnp.int32, (HEADS, MODEL), 1) // HEAD_DIM
    w_masked = jnp.where(of_head, jnp.broadcast_to(w_ref[0:1, :], (HEADS, MODEL)), 0.0)
    rank_head = exact(up.astype(F32), w_masked, NT)
    sums, down_value = jnp.zeros((HEADS, 16), F32), jnp.zeros((16, MODEL), F32)
    for window in range(6):
        keys = slice(window * WINDOW, (window + 1) * WINDOW)
        sums = sums + mm(weighted[window].astype(BF16), low_ref[keys, :])
        of_rank = exact(rank_head, weighted[window])
        down_value = down_value + mm(of_rank.astype(BF16), norm_ref[keys, :])
    up_value = exact(sums, w_masked, TN)

    parts = (up_query[:8], up_value[8:], down_query[:8], down_value[8:])
    for m, part in enumerate(parts):
        part = part * factor
        for q in range(4):
            grads_ref[pl.ds(q * 32 + m, 8, stride=4), :] = part[:, 128 * q : 128 * (q + 1)]


def core_kernel(
    own_ref,
    near_lon_ref,
    far_lon_ref,
    near_lat_ref,
    far_lat_ref,
    qkv_hbm,
    wo_hbm,
    down_ref,
    up_ref,
    readout_ref,
    bias_hbm,
    slots_hbm,
    block_ref,
    adjoint_ref,
    grads_ref,
    innov_ref,
    field_ref,
    probs_ref,
    gq_ref,
    low_ref,
    norm_ref,
    own_norm_ref,
    low_own_ref,
    w_ref,
    k_ref,
    v_ref,
    q_ref,
    att_ref,
    qkv_ref,
    wo_ref,
    bias_ref,
    copy_sems,
    term_ref,
    place_ref,
    slots_ref,
    loss_scale,
    lat_count,
):
    slot_load = pltpu.make_async_copy(slots_hbm, slots_ref, copy_sems.at[3])
    slot_load.start()
    forward_part(
        lat_count,
            own_ref,
        near_lon_ref,
        far_lon_ref,
        near_lat_ref,
        far_lat_ref,
        qkv_hbm,
        wo_hbm,
        down_ref,
        up_ref,
        readout_ref,
        bias_hbm,
        block_ref,
        field_ref,
        probs_ref,
        gq_ref,
        low_ref,
        norm_ref,
        own_norm_ref,
        low_own_ref,
        w_ref,
        k_ref,
        v_ref,
        q_ref,
        att_ref,
        qkv_ref,
        wo_ref,
        bias_ref,
        copy_sems,
    )
    slot_load.wait()
    observe_part(
        slots_ref,
        field_ref,
        probs_ref,
        gq_ref,
        low_ref,
        norm_ref,
        own_norm_ref,
        low_own_ref,
        w_ref,
        up_ref,
        adjoint_ref,
        grads_ref,
        innov_ref,
        term_ref,
        place_ref,
        loss_scale,
    )


def core(own, halos, qkv, wo, down, up, readout, bias, slots, loss_scale, lat_count):
    sources = slots.shape[0] // 8
    shape = jax.ShapeDtypeStruct
    vmem, far = pl.BlockSpec(memory_space=pltpu.VMEM), pl.BlockSpec(memory_space=pl.ANY)
    return pl.pallas_call(
        functools.partial(core_kernel, loss_scale=loss_scale, lat_count=lat_count),
        in_specs=[vmem] * 5 + [far] * 2 + [vmem] * 3 + [far] * 2,
        out_specs=[vmem] * 4,
        out_shape=[
            shape((OWN, MODEL), BF16),
            shape((8, 256), F32),
            shape((128, 128), F32),
            shape((sources, 128), F32),
        ],
        scratch_shapes=[
            pltpu.VMEM((8, 256), F32),
            pltpu.VMEM((8, HEADS * GROUP, WINDOW), BF16),
            pltpu.VMEM((OWN, MODEL), F32),
            pltpu.VMEM((6 * WINDOW, 16), BF16),
            pltpu.VMEM((6 * WINDOW, MODEL), BF16),
            pltpu.VMEM((OWN, MODEL), BF16),
            pltpu.VMEM((OWN, 16), F32),
            pltpu.VMEM((8, MODEL), F32),
            pltpu.VMEM((6 * WINDOW, MODEL), BF16),
            pltpu.VMEM((6 * WINDOW, MODEL), BF16),
            pltpu.VMEM((OWN, MODEL), F32),
            pltpu.VMEM((OWN, MODEL), F32),
            pltpu.VMEM((MODEL, 3 * MODEL), BF16),
            pltpu.VMEM((MODEL, MODEL), BF16),
            pltpu.VMEM((4, HEADS, GROUP, WINDOW), F32),
            pltpu.SemaphoreType.DMA((4,)),
            pltpu.VMEM((2, 4 * sources, 128), F32),
            pltpu.VMEM((2, 4 * sources, 128), jnp.int32),
            pltpu.VMEM((sources * 8, 128), F32),
        ],
        compiler_params=pltpu.CompilerParams(vmem_limit_bytes=58 * 1024 * 1024),
        cost_estimate=pl.CostEstimate(
            flops=3 * 10**9, bytes_accessed=8 * 10**6, transcendentals=4 * 10**5
        ),
        name="window_and_observe",
    )(own, *halos, qkv, wo, down, up, readout, bias, slots)


def paired(value, axis, odd_first):
    count = lax.axis_size(axis)
    if odd_first:
        pairs = [(i, (i + 1) % count if i % 2 else (i - 1) % count) for i in range(count)]
    else:
        pairs = [(i, i ^ 1) for i in range(count)]
    return lax.ppermute(value, axis, pairs)


def shards(
    tokens,
    query_key_value_weight,
    output_weight,
    adapter_down_map,
    adapter_up_map,
    relative_position_bias,
    readout,
    observation_index,
    observation_weight,
    observation_value,
    observation_count,
):
    lat_count, lon_count = lax.axis_size("lat"), lax.axis_size("lon")
    lat, lon = lax.axis_index("lat"), lax.axis_index("lon")
    even_lat, even_lon = lat % 2 == 0, lon % 2 == 0

    own = tokens.reshape(4, 3, 2, 6, MODEL).transpose(2, 0, 1, 3, 4).reshape(2, 4, LIVE, MODEL)
    own = lax.optimization_barrier(own)
    near_send, far_send, observation_index = lax.optimization_barrier(
        (
            jnp.where(even_lon, own[1], own[0]),
            jnp.where(even_lon, own[0], own[1]),
            observation_index,
        )
    )
    near_lon = paired(near_send, "lon", False)
    far_lon = paired(far_send, "lon", True)

    slots = packed_slots(
        observation_index.reshape(lon_count * 4, 128),
        observation_weight.reshape(lon_count * 4, 128),
        observation_value.reshape(lon_count, 128),
        observation_count.reshape(1, lon_count),
    ).reshape(lon_count, 8, 128)

    left = jnp.where(even_lon, far_lon, near_lon)
    right = jnp.where(even_lon, near_lon, far_lon)
    top = jnp.stack([left[0], own[0, 0], own[1, 0], right[0]])
    bottom = jnp.stack([left[3], own[0, 3], own[1, 3], right[3]])
    near_send = jnp.where(even_lat, bottom, top)
    far_send = jnp.where(even_lat, top, bottom)
    near_send, far_send, bias, readout = lax.optimization_barrier(
        (near_send, far_send, relative_position_bias, readout)
    )
    near_lat = paired(near_send, "lat", False)
    far_lat = paired(far_send, "lat", True)
    slots = lax.all_to_all(slots, "lon", 0, 0, tiled=True).reshape(lon_count * 8, 128)

    down_rows = adapter_down_map.reshape(16, MODEL)
    up_rows = adapter_up_map.reshape(16, MODEL)
    loss_scale = 1.0 / math.sqrt(lat_count * lon_count)
    block, adjoint, grads, innov = core(
        own,
        (near_lon, far_lon, near_lat, far_lat),
        query_key_value_weight,
        output_weight,
        down_rows,
        up_rows,
        readout.reshape(1, MODEL),
        ordered_bias(bias),
        slots,
        loss_scale,
        lat_count,
    )
    block = block.reshape(2, 4, GROUP, MODEL)[:, :, :LIVE].reshape(2, 4, 3, 6, MODEL)
    block_out = block.transpose(1, 2, 0, 3, 4).reshape(12, 12, MODEL)

    planes = [[i for i in range(lon_count) if (i // 2) % 2 == h] for h in range(2)]
    columns = [
        [a * lon_count + plane * 4 + h * 2 + c for h in range(2) for a in range(lat_count)]
        for plane in range(lon_count // 4)
        for c in range(2)
    ]
    chunks = lax.all_to_all(
        grads.reshape(32, 4, 128), "lon", 0, 0, axis_index_groups=planes, tiled=True
    )
    chunk = jnp.sum(chunks, axis=0).reshape(2, 1, 2, 128)
    adjoint_row = adjoint[0].reshape(1, 1, 2, 128)
    chunk = jnp.concatenate(
        [
            jnp.broadcast_to(chunk, (2, lat_count, 2, 128)),
            jnp.broadcast_to(adjoint_row, (2, lat_count, 2, 128)),
        ],
        axis=2,
    ).reshape(2 * lat_count, 4, 128)
    along = lax.all_to_all(chunk, ("lat", "lon"), 0, 0, axis_index_groups=columns, tiled=True)
    half = jnp.sum(along[:, :2], axis=0)
    below = lax.dynamic_index_in_dim(
        along, ((lon // 2) % 2) * lat_count + (lat + 1) % lat_count, 0, keepdims=False
    )[2:]
    below = below.reshape(256)[:OWN].reshape(2, 4, GROUP)
    here = adjoint[0, :OWN].reshape(2, 4, GROUP)
    moved = jnp.concatenate([here[:, 1:], below[:, :1]], axis=1)
    edge = jnp.pad(moved[0].reshape(1, 1, 4 * GROUP), ((0, 0), (0, 0), (0, 128 - 4 * GROUP)))
    last = jnp.concatenate(
        [
            jnp.broadcast_to(half[None], (lon_count, 2, 128)),
            innov[:, None, :],
            jnp.broadcast_to(edge, (lon_count, 1, 128)),
        ],
        axis=1,
    )
    final = lax.all_to_all(last, "lon", 0, 0, tiled=True)
    innovation = final[:, 2][None, None]
    beside = lax.dynamic_index_in_dim(final[:, 3], (lon + 1) % lon_count, 0, keepdims=False)
    beside = beside[: 4 * GROUP].reshape(4, GROUP)
    rolled = jnp.stack([moved[1], beside])[:, :, :LIVE].reshape(2, 4, 3, 6)
    rolled_adjoint = rolled.transpose(1, 2, 0, 3).reshape(12, 12)
    parts = final[:, :2].reshape(lon_count // 4, 2, 2, 2, 128)

    def whole(part):
        part = part.reshape(4, 8, 2, 128)
        return part.transpose(2, 1, 0, 3).reshape(2, 8, MODEL)

    return block_out, innovation, rolled_adjoint, whole(parts[:, 1]), whole(parts[:, 0])


def solution(mesh):
    return jax.shard_map(
        shards,
        mesh=mesh,
        in_specs=(
            P("lat", "lon", None),
            P(),
            P(),
            P(),
            P(),
            P(),
            P(),
            P("lat", "lon", None, None, None),
            P("lat", "lon", None, None, None),
            P("lat", "lon", None, None),
            P("lat", "lon", None),
        ),
        out_specs=(P("lat", "lon", None), P("lat", "lon", None, None), P("lat", "lon"), P(), P()),
        check_vma=False,
    )
```

```python
import functools
import math

import jax
import jax.numpy as jnp
from jax import lax
from jax.experimental import pallas as pl
from jax.experimental.pallas import tpu as pltpu
from jax.sharding import PartitionSpec as P

F32 = jnp.float32
BF16 = jnp.bfloat16
HEADS = 16
HEAD_DIM = 32
MODEL = 512
GROUP = 24
WINDOW = 4 * GROUP
LIVE = 18
OWN = 8 * GROUP
NORM_EPS = 1e-05
NEG = -1e30
NT = (((1,), (1,)), ((), ()))
TN = (((0,), (0,)), ((), ()))
NN = (((1,), (0,)), ((), ()))


def mm(a, b, dims=NN, precision=None):
    return lax.dot_general(a, b, dims, precision=precision, preferred_element_type=F32)


def exact(a, b, dims=NN):
    return mm(a, b, dims, precision=lax.Precision.HIGHEST)


def bias_kernel(bias_ref, out_ref, wide_ref):
    shape = (72, WINDOW)
    lane = lax.broadcasted_iota(jnp.int32, shape, 1)
    row = lane % GROUP
    column = 12 * (3 * ((lane // GROUP) % 2) + row // 6) + 6 * (lane // (2 * GROUP)) + row % 6
    hit = (column == lax.broadcasted_iota(jnp.int32, shape, 0)) & (row < LIVE)
    wide = exact(bias_ref[...], hit.astype(F32))
    lanes = lax.broadcasted_iota(jnp.int32, (1, WINDOW), 1)
    wide = wide + jnp.where(lanes % GROUP < LIVE, 0.0, NEG)
    wide_ref[...] = wide.reshape(HEADS, 72, WINDOW)
    out_ref[...] = jnp.zeros_like(out_ref)
    for parity in range(2):
        for half in range(2):
            for m in range(3):
                start = 12 * (3 * (1 - parity) + m) + 6 * (1 - half)
                out_ref[parity * 2 + half, :, 6 * m : 6 * m + 6, :] = wide_ref[:, start : start + 6, :]


def ordered_bias(bias):
    return pl.pallas_call(
        bias_kernel,
        out_shape=jax.ShapeDtypeStruct((4, HEADS, GROUP, WINDOW), F32),
        scratch_shapes=[pltpu.VMEM((HEADS, 72, WINDOW), F32)],
        cost_estimate=pl.CostEstimate(flops=2 * 10**10, bytes_accessed=2 * 10**6, transcendentals=0),
        name="ordered_bias",
    )(bias.reshape(HEADS * 72, 72))


def slots_kernel(index_ref, weight_ref, value_ref, count_ref, out_ref):
    strips = value_ref.shape[0]
    square = (strips, strips)
    own_lane = lax.broadcasted_iota(jnp.int32, square, 0) == lax.broadcasted_iota(jnp.int32, square, 1)
    counts = jnp.broadcast_to(count_ref[...].astype(F32), square)
    counts = jnp.sum(jnp.where(own_lane, counts, 0.0), axis=1, keepdims=True).astype(jnp.int32)
    live = lax.broadcasted_iota(jnp.int32, (strips, 128), 1) < counts
    places = []
    for k in range(4):
        cell = index_ref[pl.ds(k, strips, stride=4), :]
        row = (cell * 171) >> 11
        col = cell - 12 * row
        group = (row * 11) >> 5
        half = (col >= 6).astype(jnp.int32)
        places.append((half * 4 + group) * GROUP + (row - 3 * group) * 6 + col - 6 * half)
        weight = weight_ref[pl.ds(k, strips, stride=4), :]
        out_ref[pl.ds(2 + k, strips, stride=8), :] = jnp.where(live, weight, 0.0)
    for pair in range(2):
        packed = places[2 * pair] + 1024 * places[2 * pair + 1]
        out_ref[pl.ds(pair, strips, stride=8), :] = packed.astype(F32)
    out_ref[pl.ds(6, strips, stride=8), :] = jnp.where(live, value_ref[...], 0.0)
    out_ref[pl.ds(7, strips, stride=8), :] = jnp.zeros((strips, 128), F32)


def packed_slots(index, weight, value, count):
    return pl.pallas_call(
        slots_kernel,
        out_shape=jax.ShapeDtypeStruct((value.shape[0] * 8, 128), F32),
        cost_estimate=pl.CostEstimate(flops=10**6, bytes_accessed=5 * 10**5, transcendentals=0),
        name="packed_slots",
    )(index, weight, value, count)


def forward_part(
    lat_count,
    own_ref,
    near_lon_ref,
    far_lon_ref,
    near_lat_ref,
    far_lat_ref,
    qkv_hbm,
    wo_hbm,
    down_ref,
    up_ref,
    readout_ref,
    bias_hbm,
    block_ref,
    field_ref,
    probs_ref,
    gq_ref,
    low_ref,
    norm_ref,
    own_norm_ref,
    low_own_ref,
    w_ref,
    k_ref,
    v_ref,
    q_ref,
    att_ref,
    qkv_ref,
    wo_ref,
    bias_ref,
    copy_sems,
):
    loads = [
        pltpu.make_async_copy(source, target, copy_sems.at[i])
        for i, (source, target) in enumerate(
            ((qkv_hbm, qkv_ref), (bias_hbm, bias_ref), (wo_hbm, wo_ref))
        )
    ]
    for load in loads:
        load.start()
    lat = lax.axis_index("lat")
    even_lon = lax.axis_index("lon") % 2 == 0
    even_lat = lat % 2 == 0
    first = (lat == 0).astype(F32)
    last = (lat == lat_count - 1).astype(F32)

    def padded(x):
        return jnp.concatenate([x, jnp.zeros((GROUP - LIVE, MODEL), F32)], axis=0)

    def pick(cond, a, b):
        return jnp.where(cond, a.astype(F32), b.astype(F32))

    def piece(strip, group):
        if group == 0:
            return pick(even_lat, far_lat_ref[strip], near_lat_ref[strip])
        if group == 5:
            return pick(even_lat, near_lat_ref[strip], far_lat_ref[strip])
        if strip == 0:
            return pick(even_lon, far_lon_ref[group - 1], near_lon_ref[group - 1])
        if strip == 3:
            return pick(even_lon, near_lon_ref[group - 1], far_lon_ref[group - 1])
        return own_ref[strip - 1, group - 1].astype(F32)

    for strip in range(4):
        rows = []
        for pair in range(3):
            x = jnp.concatenate([padded(piece(strip, 2 * pair + i)) for i in range(2)], axis=0)
            center = x - jnp.mean(x, axis=1, keepdims=True)
            spread = jnp.mean(center * center, axis=1, keepdims=True)
            y = center * lax.rsqrt(spread + NORM_EPS)
            at = ((strip // 2) * 3 + pair) * WINDOW + (strip % 2) * 2 * GROUP
            norm_ref[at : at + 2 * GROUP, :] = y.astype(BF16)
            rows.append(y)
        if strip in (1, 2):
            mine = jnp.concatenate([rows[0][GROUP:], rows[1], rows[2][:GROUP]], axis=0)
            own_norm_ref[(strip - 1) * 4 * GROUP : strip * 4 * GROUP, :] = mine.astype(BF16)

    normed = norm_ref[...]
    for load in loads:
        load.wait()
    rank_row = lax.broadcasted_iota(jnp.int32, (16, MODEL), 0)
    up_half = 0.5 * up_ref[...].astype(F32)
    up_query = jnp.where(rank_row < 8, up_half, 0.0).astype(BF16)
    up_value = jnp.where(rank_row >= 8, up_half, 0.0).astype(BF16)
    low = mm(normed, down_ref[...], NT).astype(BF16)
    low_ref[...] = low
    k_ref[...] = mm(normed, qkv_ref[:, MODEL : 2 * MODEL]).astype(BF16)
    v_ref[...] = (mm(normed, qkv_ref[:, 2 * MODEL :]) + mm(low, up_value)).astype(BF16)
    normed_own = own_norm_ref[...]
    low_own = mm(normed_own, down_ref[...], NT).astype(BF16)
    low_own_ref[...] = low_own.astype(F32)
    query = mm(normed_own, qkv_ref[:, :MODEL]) + mm(low_own, up_query)
    q_ref[...] = query.astype(BF16).astype(F32)

    readout = jnp.broadcast_to(readout_ref[...].astype(F32), (8, MODEL)).astype(BF16)
    w_row = mm(readout, wo_ref[...], NT)
    w_ref[...] = w_row

    scale = 1.0 / math.sqrt(HEAD_DIM)
    head_of = lax.broadcasted_iota(jnp.int32, (8, 1, 256), 2) // HEAD_DIM
    head_mask = head_of == lax.broadcasted_iota(jnp.int32, (8, 1, 256), 0)
    lane_part = (lax.broadcasted_iota(jnp.int32, (1, WINDOW), 1) // GROUP) % 2
    masked_first = jnp.where(lane_part == 0, NEG * first, 0.0)
    masked_last = jnp.where(lane_part == 1, NEG * last, 0.0)

    ones = jnp.ones((WINDOW, WINDOW), BF16)

    def fold(rows):
        return jnp.sum(jnp.where(head_mask, rows.reshape(8, GROUP, 256), 0.0), axis=0)

    for n in range(8):
        half, row = n // 4, n % 4
        window = half * 3 + (row + 1) // 2
        keys = slice(window * WINDOW, (window + 1) * WINDOW)
        for part in range(2):
            cols = slice(256 * part, 256 * (part + 1))
            k_win, v_win = k_ref[keys, cols], v_ref[keys, cols]
            q_own = q_ref[n * GROUP : (n + 1) * GROUP, cols]
            lhs = jnp.where(head_mask, q_own[None], 0.0).reshape(8 * GROUP, 256).astype(BF16)
            bias = bias_ref[(row % 2) * 2 + half, 8 * part : 8 * part + 8].reshape(8 * GROUP, WINDOW)
            scores = mm(lhs, k_win, NT) * scale + bias
            if row == 0:
                scores = scores + masked_first
            if row == 3:
                scores = scores + masked_last
            raised = jnp.exp(scores - jnp.max(scores, axis=1, keepdims=True))
            probs = raised * (1.0 / jnp.sum(raised, axis=1, keepdims=True))
            probs_bf = probs.astype(BF16)
            probs_ref[n, 8 * GROUP * part : 8 * GROUP * (part + 1), :] = probs_bf
            att_ref[n * GROUP : (n + 1) * GROUP, cols] = fold(mm(probs_bf, v_win))
            w_masked = jnp.where(head_mask[:, 0, :], w_row[:, cols], 0.0)
            w_high = w_masked.astype(BF16).astype(F32)
            w_pair = jnp.concatenate([w_high, w_masked - w_high], axis=0).astype(BF16)
            v_pair = mm(w_pair, v_win, NT)
            v_w = (v_pair[:8] + v_pair[8:]).reshape(8, 1, WINDOW)
            v_w = jnp.broadcast_to(v_w, (8, GROUP, WINDOW)).reshape(8 * GROUP, WINDOW)
            share = probs * v_w
            share_high = share.astype(BF16)
            share_low = (share - share_high.astype(F32)).astype(BF16)
            mean = jnp.sum(share, axis=1, keepdims=True)
            slope = (probs * (v_w - mean) * scale).astype(BF16)
            gq_ref[n * GROUP : (n + 1) * GROUP, cols] = fold(mm(slope, k_win))

    x_own = [padded(own_ref[n // 4, n % 4].astype(F32)) for n in range(8)]
    x_own = jnp.concatenate(x_own, axis=0)
    out = (x_own + mm(att_ref[...].astype(BF16), wo_ref[...])).astype(BF16)
    block_ref[...] = out
    field_ref[...] = jnp.zeros_like(field_ref)
    field_ref[:, :OWN] = mm(readout, out, NT)


def observe_part(
    slots_ref,
    field_ref,
    probs_ref,
    gq_ref,
    low_ref,
    norm_ref,
    own_norm_ref,
    low_own_ref,
    w_ref,
    up_ref,
    adjoint_ref,
    grads_ref,
    innov_ref,
    term_ref,
    place_ref,
    loss_scale,
):
    sources = innov_ref.shape[0]
    field_low = jnp.broadcast_to(field_ref[0:1, 0:128], (sources, 128))
    field_high = jnp.broadcast_to(field_ref[0:1, 128:256], (sources, 128))
    places, weights = [], []
    for pair in range(2):
        packed = slots_ref[pl.ds(pair, sources, stride=8), :].astype(jnp.int32)
        places += [packed & 1023, packed >> 10]
    predicted = jnp.zeros((sources, 128), F32)
    for k in range(4):
        lane = places[k] & 127
        picked = jnp.where(
            places[k] < 128,
            jnp.take_along_axis(field_low, lane, axis=1),
            jnp.take_along_axis(field_high, lane, axis=1),
        )
        weights.append(slots_ref[pl.ds(2 + k, sources, stride=8), :])
        predicted = predicted + weights[k] * picked
    innov = predicted - slots_ref[pl.ds(6, sources, stride=8), :]
    innov_ref[...] = innov
    for k in range(4):
        rows = slice(k * sources, (k + 1) * sources)
        term = weights[k] * innov
        high = term.astype(BF16).astype(F32)
        term_ref[0, rows, :] = high
        term_ref[1, rows, :] = term - high
        place_ref[0, rows, :] = places[k] >> 4
        place_ref[1, rows, :] = places[k] & 15

    digit = lax.broadcasted_iota(jnp.int32, (16, 128), 0)
    per_step = 32

    def add_rows(step, total):
        left, right = [], []
        for inner in range(per_step):
            at = pl.ds(step * per_step + inner, 1)
            left.append(jnp.where(digit == place_ref[0, at, :], 1.0, 0.0).astype(BF16))
            hit = digit == place_ref[1, at, :]
            terms = [jnp.where(hit, term_ref[i, at, :], 0.0) for i in range(2)]
            right.append(jnp.concatenate(terms, axis=0).astype(BF16))
        return total + mm(jnp.concatenate(left, axis=1), jnp.concatenate(right, axis=1), NT)

    total = lax.fori_loop(0, 4 * sources // per_step, add_rows, jnp.zeros((16, 32), F32))
    total = total[:, :16] + total[:, 16:]

    def cells(shape, axis):
        cell = lax.broadcasted_iota(jnp.int32, shape, axis)
        digits = lax.broadcasted_iota(jnp.int32, shape, 1 - axis)
        return cell // 16 == digits, cell % 16 == digits

    high, low = cells((OWN, 16), 0)
    column = exact(high.astype(F32), total)
    adjoint = jnp.sum(jnp.where(low, column, 0.0), axis=1, keepdims=True)
    high, low = cells((16, OWN), 1)
    row = jnp.sum(jnp.where(high, exact(total, low.astype(F32)), 0.0), axis=0, keepdims=True)
    adjoint_ref[...] = jnp.zeros_like(adjoint_ref)
    adjoint_ref[0:1, :OWN] = row

    factor = 0.5 * loss_scale
    g_query = gq_ref[...].astype(BF16)
    up = up_ref[...]
    grad_low = mm(g_query, up, NT)
    up_query = mm((low_own_ref[...] * adjoint).astype(BF16), g_query, TN)
    down_query = mm((grad_low * adjoint).astype(BF16), own_norm_ref[...], TN)

    weighted = [None] * 6
    for n in range(8):
        window = (n // 4) * 3 + (n % 4 + 1) // 2
        probs = probs_ref[n].astype(F32).reshape(HEADS, GROUP, WINDOW)
        part = jnp.sum(probs * adjoint[n * GROUP : (n + 1) * GROUP].reshape(1, GROUP, 1), axis=1)
        weighted[window] = part if weighted[window] is None else weighted[window] + part
    head = lax.broadcasted_iota(jnp.int32, (HEADS, MODEL), 0)
    of_head = head == lax.broadcasted_iota(jnp.int32, (HEADS, MODEL), 1) // HEAD_DIM
    w_masked = jnp.where(of_head, jnp.broadcast_to(w_ref[0:1, :], (HEADS, MODEL)), 0.0)
    rank_head = exact(up.astype(F32), w_masked, NT)
    sums, down_value = jnp.zeros((HEADS, 16), F32), jnp.zeros((16, MODEL), F32)
    for window in range(6):
        keys = slice(window * WINDOW, (window + 1) * WINDOW)
        sums = sums + mm(weighted[window].astype(BF16), low_ref[keys, :])
        of_rank = exact(rank_head, weighted[window])
        down_value = down_value + mm(of_rank.astype(BF16), norm_ref[keys, :])
    up_value = exact(sums, w_masked, TN)

    parts = (up_query[:8], up_value[8:], down_query[:8], down_value[8:])
    for m, part in enumerate(parts):
        part = part * factor
        for q in range(4):
            grads_ref[pl.ds(q * 32 + m, 8, stride=4), :] = part[:, 128 * q : 128 * (q + 1)]


def core_kernel(
    own_ref,
    near_lon_ref,
    far_lon_ref,
    near_lat_ref,
    far_lat_ref,
    qkv_hbm,
    wo_hbm,
    down_ref,
    up_ref,
    readout_ref,
    bias_hbm,
    slots_hbm,
    block_ref,
    adjoint_ref,
    grads_ref,
    innov_ref,
    field_ref,
    probs_ref,
    gq_ref,
    low_ref,
    norm_ref,
    own_norm_ref,
    low_own_ref,
    w_ref,
    k_ref,
    v_ref,
    q_ref,
    att_ref,
    qkv_ref,
    wo_ref,
    bias_ref,
    copy_sems,
    term_ref,
    place_ref,
    slots_ref,
    loss_scale,
    lat_count,
):
    slot_load = pltpu.make_async_copy(slots_hbm, slots_ref, copy_sems.at[3])
    slot_load.start()
    forward_part(
        lat_count,
            own_ref,
        near_lon_ref,
        far_lon_ref,
        near_lat_ref,
        far_lat_ref,
        qkv_hbm,
        wo_hbm,
        down_ref,
        up_ref,
        readout_ref,
        bias_hbm,
        block_ref,
        field_ref,
        probs_ref,
        gq_ref,
        low_ref,
        norm_ref,
        own_norm_ref,
        low_own_ref,
        w_ref,
        k_ref,
        v_ref,
        q_ref,
        att_ref,
        qkv_ref,
        wo_ref,
        bias_ref,
        copy_sems,
    )
    slot_load.wait()
    observe_part(
        slots_ref,
        field_ref,
        probs_ref,
        gq_ref,
        low_ref,
        norm_ref,
        own_norm_ref,
        low_own_ref,
        w_ref,
        up_ref,
        adjoint_ref,
        grads_ref,
        innov_ref,
        term_ref,
        place_ref,
        loss_scale,
    )


def core(own, halos, qkv, wo, down, up, readout, bias, slots, loss_scale, lat_count):
    sources = slots.shape[0] // 8
    shape = jax.ShapeDtypeStruct
    vmem, far = pl.BlockSpec(memory_space=pltpu.VMEM), pl.BlockSpec(memory_space=pl.ANY)
    return pl.pallas_call(
        functools.partial(core_kernel, loss_scale=loss_scale, lat_count=lat_count),
        in_specs=[vmem] * 5 + [far] * 2 + [vmem] * 3 + [far] * 2,
        out_specs=[vmem] * 4,
        out_shape=[
            shape((OWN, MODEL), BF16),
            shape((8, 256), F32),
            shape((128, 128), F32),
            shape((sources, 128), F32),
        ],
        scratch_shapes=[
            pltpu.VMEM((8, 256), F32),
            pltpu.VMEM((8, HEADS * GROUP, WINDOW), BF16),
            pltpu.VMEM((OWN, MODEL), F32),
            pltpu.VMEM((6 * WINDOW, 16), BF16),
            pltpu.VMEM((6 * WINDOW, MODEL), BF16),
            pltpu.VMEM((OWN, MODEL), BF16),
            pltpu.VMEM((OWN, 16), F32),
            pltpu.VMEM((8, MODEL), F32),
            pltpu.VMEM((6 * WINDOW, MODEL), BF16),
            pltpu.VMEM((6 * WINDOW, MODEL), BF16),
            pltpu.VMEM((OWN, MODEL), F32),
            pltpu.VMEM((OWN, MODEL), F32),
            pltpu.VMEM((MODEL, 3 * MODEL), BF16),
            pltpu.VMEM((MODEL, MODEL), BF16),
            pltpu.VMEM((4, HEADS, GROUP, WINDOW), F32),
            pltpu.SemaphoreType.DMA((4,)),
            pltpu.VMEM((2, 4 * sources, 128), F32),
            pltpu.VMEM((2, 4 * sources, 128), jnp.int32),
            pltpu.VMEM((sources * 8, 128), F32),
        ],
        compiler_params=pltpu.CompilerParams(vmem_limit_bytes=58 * 1024 * 1024),
        cost_estimate=pl.CostEstimate(
            flops=3 * 10**9, bytes_accessed=8 * 10**6, transcendentals=4 * 10**5
        ),
        name="window_and_observe",
    )(own, *halos, qkv, wo, down, up, readout, bias, slots)


def paired(value, axis, odd_first):
    count = lax.axis_size(axis)
    if odd_first:
        pairs = [(i, (i + 1) % count if i % 2 else (i - 1) % count) for i in range(count)]
    else:
        pairs = [(i, i ^ 1) for i in range(count)]
    return lax.ppermute(value, axis, pairs)


def shards(
    tokens,
    query_key_value_weight,
    output_weight,
    adapter_down_map,
    adapter_up_map,
    relative_position_bias,
    readout,
    observation_index,
    observation_weight,
    observation_value,
    observation_count,
):
    lat_count, lon_count = lax.axis_size("lat"), lax.axis_size("lon")
    lat, lon = lax.axis_index("lat"), lax.axis_index("lon")
    even_lat, even_lon = lat % 2 == 0, lon % 2 == 0

    own = tokens.reshape(4, 3, 2, 6, MODEL).transpose(2, 0, 1, 3, 4).reshape(2, 4, LIVE, MODEL)
    own = lax.optimization_barrier(own)
    near_send, far_send, observation_index = lax.optimization_barrier(
        (
            jnp.where(even_lon, own[1], own[0]),
            jnp.where(even_lon, own[0], own[1]),
            observation_index,
        )
    )
    near_lon = paired(near_send, "lon", False)
    far_lon = paired(far_send, "lon", True)

    slots = packed_slots(
        observation_index.reshape(lon_count * 4, 128),
        observation_weight.reshape(lon_count * 4, 128),
        observation_value.reshape(lon_count, 128),
        observation_count.reshape(1, lon_count),
    ).reshape(lon_count, 8, 128)

    left = jnp.where(even_lon, far_lon, near_lon)
    right = jnp.where(even_lon, near_lon, far_lon)
    top = jnp.stack([left[0], own[0, 0], own[1, 0], right[0]])
    bottom = jnp.stack([left[3], own[0, 3], own[1, 3], right[3]])
    near_send = jnp.where(even_lat, bottom, top)
    far_send = jnp.where(even_lat, top, bottom)
    near_send, far_send, bias, readout = lax.optimization_barrier(
        (near_send, far_send, relative_position_bias, readout)
    )
    near_lat = paired(near_send, "lat", False)
    far_lat = paired(far_send, "lat", True)
    slots = lax.all_to_all(slots, "lon", 0, 0, tiled=True).reshape(lon_count * 8, 128)

    down_rows = adapter_down_map.reshape(16, MODEL)
    up_rows = adapter_up_map.reshape(16, MODEL)
    loss_scale = 1.0 / math.sqrt(lat_count * lon_count)
    block, adjoint, grads, innov = core(
        own,
        (near_lon, far_lon, near_lat, far_lat),
        query_key_value_weight,
        output_weight,
        down_rows,
        up_rows,
        readout.reshape(1, MODEL),
        ordered_bias(bias),
        slots,
        loss_scale,
        lat_count,
    )
    block = block.reshape(2, 4, GROUP, MODEL)[:, :, :LIVE].reshape(2, 4, 3, 6, MODEL)
    block_out = block.transpose(1, 2, 0, 3, 4).reshape(12, 12, MODEL)

    members = lon_count // 2
    plane = (lon // 2) % 2
    planes = [[i for i in range(lon_count) if (i // 2) % 2 == h] for h in range(2)]
    columns = [
        [a * lon_count + at * 4 + h * 2 + c for h in range(2) for a in range(lat_count)]
        for at in range(members // 2)
        for c in range(2)
    ]

    def by_plane(rows):
        split = rows.reshape(members // 2, 2, 2, 128)
        low, high = split[:, 0].reshape(members, 128), split[:, 1].reshape(members, 128)
        return jnp.where(plane == 0, low, high), jnp.where(plane == 0, high, low)

    chunks = lax.all_to_all(
        grads.reshape(members, 4, 128), "lon", 0, 0, axis_index_groups=planes, tiled=True
    )
    mine, other = by_plane(innov)
    other = lax.ppermute(other, "lon", [(i, i ^ 2) for i in range(lon_count)])

    chunk = jnp.concatenate([jnp.sum(chunks, axis=0), adjoint[:1, :128]], axis=0)
    along = lax.all_to_all(
        jnp.broadcast_to(chunk[None], (2 * lat_count, 5, 128)),
        ("lat", "lon"),
        0,
        0,
        axis_index_groups=columns,
        tiled=True,
    )
    total = jnp.sum(along[:, :4], axis=0)
    edges = along[:, 4]
    below_at = (lat + 1) % lat_count

    def edge_of(h, a):
        return lax.dynamic_index_in_dim(edges, h * lat_count + a, 0, keepdims=False)

    def moved_up(here, below):
        kept = here[: 4 * GROUP].reshape(4, GROUP)[1:]
        return jnp.concatenate([kept.reshape(3 * GROUP), below[:GROUP]])

    below = edge_of(plane, below_at)
    edge = moved_up(adjoint[0], below)
    twin_edge = moved_up(edge_of(1 - plane, lat), edge_of(1 - plane, below_at))
    shared = jnp.concatenate(
        [total, jnp.pad(jnp.stack([edge, twin_edge]), ((0, 0), (0, 128 - 4 * GROUP)))], axis=0
    )
    final = jnp.concatenate(
        [jnp.broadcast_to(shared[None], (members, 6, 128)), mine[:, None], other[:, None]], axis=1
    )
    final = lax.all_to_all(final, "lon", 0, 0, axis_index_groups=planes, tiled=True)

    near, far = final[:, 6].reshape(-1, 2, 128), final[:, 7].reshape(-1, 2, 128)
    low, high = jnp.where(plane == 0, near, far), jnp.where(plane == 0, far, near)
    innovation = jnp.stack([low, high], axis=1).reshape(1, 1, lon_count, 128)

    member = lon // 4 * 2 + lon % 2
    across = (member - 1 + 2 * plane) % members
    beside = lax.dynamic_index_in_dim(
        final[:, 4:6].reshape(2 * members, 128),
        jnp.where(lon % 2 == 0, 2 * (member + 1), 2 * across + 1),
        0,
        keepdims=False,
    )
    kept = adjoint[0, 4 * GROUP : OWN]
    moved = jnp.concatenate([kept[GROUP:], below[4 * GROUP : 5 * GROUP]])
    rolled = jnp.stack([moved, beside[: 4 * GROUP]]).reshape(2, 4, GROUP)[:, :, :LIVE]
    rolled_adjoint = rolled.reshape(2, 4, 3, 6).transpose(1, 2, 0, 3).reshape(12, 12)

    def whole(part):
        return part.reshape(4, 8, 2, 128).transpose(2, 1, 0, 3).reshape(2, 8, MODEL)

    return block_out, innovation, rolled_adjoint, whole(final[:, 2:4]), whole(final[:, 0:2])


def solution(mesh):
    return jax.shard_map(
        shards,
        mesh=mesh,
        in_specs=(
            P("lat", "lon", None),
            P(),
            P(),
            P(),
            P(),
            P(),
            P(),
            P("lat", "lon", None, None, None),
            P("lat", "lon", None, None, None),
            P("lat", "lon", None, None),
            P("lat", "lon", None),
        ),
        out_specs=(P("lat", "lon", None), P("lat", "lon", None, None), P("lat", "lon"), P(), P()),
        check_vma=False,
    )
```

```python
import functools
import math

import jax
import jax.numpy as jnp
from jax import lax
from jax.experimental import pallas as pl
from jax.experimental.pallas import tpu as pltpu
from jax.sharding import PartitionSpec as P

F32 = jnp.float32
BF16 = jnp.bfloat16
HEADS = 16
HEAD_DIM = 32
MODEL = 512
GROUP = 24
WINDOW = 4 * GROUP
LIVE = 18
OWN = 8 * GROUP
NORM_EPS = 1e-05
NEG = -1e30
NT = (((1,), (1,)), ((), ()))
TN = (((0,), (0,)), ((), ()))
NN = (((1,), (0,)), ((), ()))


def mm(a, b, dims=NN, precision=None):
    return lax.dot_general(a, b, dims, precision=precision, preferred_element_type=F32)


def exact(a, b, dims=NN):
    return mm(a, b, dims, precision=lax.Precision.HIGHEST)


def bias_kernel(bias_ref, out_ref, wide_ref):
    shape = (72, WINDOW)
    lane = lax.broadcasted_iota(jnp.int32, shape, 1)
    row = lane % GROUP
    column = 12 * (3 * ((lane // GROUP) % 2) + row // 6) + 6 * (lane // (2 * GROUP)) + row % 6
    hit = (column == lax.broadcasted_iota(jnp.int32, shape, 0)) & (row < LIVE)
    wide = exact(bias_ref[...], hit.astype(F32))
    lanes = lax.broadcasted_iota(jnp.int32, (1, WINDOW), 1)
    wide = wide + jnp.where(lanes % GROUP < LIVE, 0.0, NEG)
    wide_ref[...] = wide.reshape(HEADS, 72, WINDOW)
    out_ref[...] = jnp.zeros_like(out_ref)
    for parity in range(2):
        for half in range(2):
            for m in range(3):
                start = 12 * (3 * (1 - parity) + m) + 6 * (1 - half)
                out_ref[parity * 2 + half, :, 6 * m : 6 * m + 6, :] = wide_ref[:, start : start + 6, :]


def ordered_bias(bias):
    return pl.pallas_call(
        bias_kernel,
        out_shape=jax.ShapeDtypeStruct((4, HEADS, GROUP, WINDOW), F32),
        scratch_shapes=[pltpu.VMEM((HEADS, 72, WINDOW), F32)],
        cost_estimate=pl.CostEstimate(flops=2 * 10**10, bytes_accessed=2 * 10**6, transcendentals=0),
        name="ordered_bias",
    )(bias.reshape(HEADS * 72, 72))


def slots_kernel(index_ref, weight_ref, value_ref, count_ref, out_ref):
    strips = value_ref.shape[0]
    square = (strips, strips)
    own_lane = lax.broadcasted_iota(jnp.int32, square, 0) == lax.broadcasted_iota(jnp.int32, square, 1)
    counts = jnp.broadcast_to(count_ref[...].astype(F32), square)
    counts = jnp.sum(jnp.where(own_lane, counts, 0.0), axis=1, keepdims=True).astype(jnp.int32)
    live = lax.broadcasted_iota(jnp.int32, (strips, 128), 1) < counts
    places = []
    for k in range(4):
        cell = index_ref[pl.ds(k, strips, stride=4), :]
        row = (cell * 171) >> 11
        col = cell - 12 * row
        group = (row * 11) >> 5
        half = (col >= 6).astype(jnp.int32)
        places.append((half * 4 + group) * GROUP + (row - 3 * group) * 6 + col - 6 * half)
        weight = weight_ref[pl.ds(k, strips, stride=4), :]
        out_ref[pl.ds(2 + k, strips, stride=8), :] = jnp.where(live, weight, 0.0)
    for pair in range(2):
        packed = places[2 * pair] + 1024 * places[2 * pair + 1]
        out_ref[pl.ds(pair, strips, stride=8), :] = packed.astype(F32)
    out_ref[pl.ds(6, strips, stride=8), :] = jnp.where(live, value_ref[...], 0.0)
    out_ref[pl.ds(7, strips, stride=8), :] = jnp.zeros((strips, 128), F32)


def packed_slots(index, weight, value, count):
    return pl.pallas_call(
        slots_kernel,
        out_shape=jax.ShapeDtypeStruct((value.shape[0] * 8, 128), F32),
        cost_estimate=pl.CostEstimate(flops=10**6, bytes_accessed=5 * 10**5, transcendentals=0),
        name="packed_slots",
    )(index, weight, value, count)


def forward_part(
    lat_count,
    own_ref,
    near_lon_ref,
    far_lon_ref,
    near_lat_ref,
    far_lat_ref,
    qkv_hbm,
    wo_hbm,
    down_ref,
    up_ref,
    readout_ref,
    bias_hbm,
    block_ref,
    field_ref,
    probs_ref,
    gq_ref,
    low_ref,
    norm_ref,
    own_norm_ref,
    low_own_ref,
    w_ref,
    k_ref,
    v_ref,
    q_ref,
    att_ref,
    qkv_ref,
    wo_ref,
    bias_ref,
    copy_sems,
):
    loads = [
        pltpu.make_async_copy(source, target, copy_sems.at[i])
        for i, (source, target) in enumerate(
            ((qkv_hbm, qkv_ref), (bias_hbm, bias_ref), (wo_hbm, wo_ref))
        )
    ]
    for load in loads:
        load.start()
    lat = lax.axis_index("lat")
    even_lon = lax.axis_index("lon") % 2 == 0
    even_lat = lat % 2 == 0
    first = (lat == 0).astype(F32)
    last = (lat == lat_count - 1).astype(F32)

    def padded(x):
        return jnp.concatenate([x, jnp.zeros((GROUP - LIVE, MODEL), F32)], axis=0)

    def pick(cond, a, b):
        return jnp.where(cond, a.astype(F32), b.astype(F32))

    def piece(strip, group):
        if group == 0:
            return pick(even_lat, far_lat_ref[strip], near_lat_ref[strip])
        if group == 5:
            return pick(even_lat, near_lat_ref[strip], far_lat_ref[strip])
        if strip == 0:
            return pick(even_lon, far_lon_ref[group - 1], near_lon_ref[group - 1])
        if strip == 3:
            return pick(even_lon, near_lon_ref[group - 1], far_lon_ref[group - 1])
        return own_ref[strip - 1, group - 1].astype(F32)

    for strip in range(4):
        rows = []
        for pair in range(3):
            x = jnp.concatenate([padded(piece(strip, 2 * pair + i)) for i in range(2)], axis=0)
            center = x - jnp.mean(x, axis=1, keepdims=True)
            spread = jnp.mean(center * center, axis=1, keepdims=True)
            y = center * lax.rsqrt(spread + NORM_EPS)
            at = ((strip // 2) * 3 + pair) * WINDOW + (strip % 2) * 2 * GROUP
            norm_ref[at : at + 2 * GROUP, :] = y.astype(BF16)
            rows.append(y)
        if strip in (1, 2):
            mine = jnp.concatenate([rows[0][GROUP:], rows[1], rows[2][:GROUP]], axis=0)
            own_norm_ref[(strip - 1) * 4 * GROUP : strip * 4 * GROUP, :] = mine.astype(BF16)

    normed = norm_ref[...]
    for load in loads:
        load.wait()
    rank_row = lax.broadcasted_iota(jnp.int32, (16, MODEL), 0)
    up_half = 0.5 * up_ref[...].astype(F32)
    up_query = jnp.where(rank_row < 8, up_half, 0.0).astype(BF16)
    up_value = jnp.where(rank_row >= 8, up_half, 0.0).astype(BF16)
    low = mm(normed, down_ref[...], NT).astype(BF16)
    low_ref[...] = low
    k_ref[...] = mm(normed, qkv_ref[:, MODEL : 2 * MODEL]).astype(BF16)
    v_ref[...] = (mm(normed, qkv_ref[:, 2 * MODEL :]) + mm(low, up_value)).astype(BF16)
    normed_own = own_norm_ref[...]
    low_own = mm(normed_own, down_ref[...], NT).astype(BF16)
    low_own_ref[...] = low_own.astype(F32)
    query = mm(normed_own, qkv_ref[:, :MODEL]) + mm(low_own, up_query)
    q_ref[...] = query.astype(BF16).astype(F32)

    readout = jnp.broadcast_to(readout_ref[...].astype(F32), (8, MODEL)).astype(BF16)
    w_row = mm(readout, wo_ref[...], NT)
    w_ref[...] = w_row

    scale = 1.0 / math.sqrt(HEAD_DIM)
    head_of = lax.broadcasted_iota(jnp.int32, (8, 1, 256), 2) // HEAD_DIM
    head_mask = head_of == lax.broadcasted_iota(jnp.int32, (8, 1, 256), 0)
    lane_part = (lax.broadcasted_iota(jnp.int32, (1, WINDOW), 1) // GROUP) % 2
    masked_first = jnp.where(lane_part == 0, NEG * first, 0.0)
    masked_last = jnp.where(lane_part == 1, NEG * last, 0.0)

    ones = jnp.ones((WINDOW, WINDOW), BF16)

    def fold(rows):
        return jnp.sum(jnp.where(head_mask, rows.reshape(8, GROUP, 256), 0.0), axis=0)

    for n in range(8):
        half, row = n // 4, n % 4
        window = half * 3 + (row + 1) // 2
        keys = slice(window * WINDOW, (window + 1) * WINDOW)
        for part in range(2):
            cols = slice(256 * part, 256 * (part + 1))
            k_win, v_win = k_ref[keys, cols], v_ref[keys, cols]
            q_own = q_ref[n * GROUP : (n + 1) * GROUP, cols]
            lhs = jnp.where(head_mask, q_own[None], 0.0).reshape(8 * GROUP, 256).astype(BF16)
            bias = bias_ref[(row % 2) * 2 + half, 8 * part : 8 * part + 8].reshape(8 * GROUP, WINDOW)
            scores = mm(lhs, k_win, NT) * scale + bias
            if row == 0:
                scores = scores + masked_first
            if row == 3:
                scores = scores + masked_last
            raised = jnp.exp(scores - jnp.max(scores, axis=1, keepdims=True))
            probs = raised * (1.0 / jnp.sum(raised, axis=1, keepdims=True))
            probs_bf = probs.astype(BF16)
            probs_ref[n, 8 * GROUP * part : 8 * GROUP * (part + 1), :] = probs_bf
            att_ref[n * GROUP : (n + 1) * GROUP, cols] = fold(mm(probs_bf, v_win))
            w_masked = jnp.where(head_mask[:, 0, :], w_row[:, cols], 0.0)
            w_high = w_masked.astype(BF16).astype(F32)
            w_pair = jnp.concatenate([w_high, w_masked - w_high], axis=0).astype(BF16)
            v_pair = mm(w_pair, v_win, NT)
            v_w = (v_pair[:8] + v_pair[8:]).reshape(8, 1, WINDOW)
            v_w = jnp.broadcast_to(v_w, (8, GROUP, WINDOW)).reshape(8 * GROUP, WINDOW)
            share = probs * v_w
            share_high = share.astype(BF16)
            share_low = (share - share_high.astype(F32)).astype(BF16)
            mean = jnp.sum(share, axis=1, keepdims=True)
            slope = (probs * (v_w - mean) * scale).astype(BF16)
            gq_ref[n * GROUP : (n + 1) * GROUP, cols] = fold(mm(slope, k_win))

    x_own = [padded(own_ref[n // 4, n % 4].astype(F32)) for n in range(8)]
    x_own = jnp.concatenate(x_own, axis=0)
    out = (x_own + mm(att_ref[...].astype(BF16), wo_ref[...])).astype(BF16)
    block_ref[...] = out
    field_ref[...] = jnp.zeros_like(field_ref)
    field_ref[:, :OWN] = mm(readout, out, NT)


def observe_part(
    slots_ref,
    field_ref,
    probs_ref,
    gq_ref,
    low_ref,
    norm_ref,
    own_norm_ref,
    low_own_ref,
    w_ref,
    up_ref,
    adjoint_ref,
    edge_ref,
    grads_ref,
    mine_ref,
    other_ref,
    innov_ref,
    term_ref,
    place_ref,
    loss_scale,
):
    sources = innov_ref.shape[0]
    field_low = jnp.broadcast_to(field_ref[0:1, 0:128], (sources, 128))
    field_high = jnp.broadcast_to(field_ref[0:1, 128:256], (sources, 128))
    places, weights = [], []
    for pair in range(2):
        packed = slots_ref[pl.ds(pair, sources, stride=8), :].astype(jnp.int32)
        places += [packed & 1023, packed >> 10]
    predicted = jnp.zeros((sources, 128), F32)
    for k in range(4):
        lane = places[k] & 127
        picked = jnp.where(
            places[k] < 128,
            jnp.take_along_axis(field_low, lane, axis=1),
            jnp.take_along_axis(field_high, lane, axis=1),
        )
        weights.append(slots_ref[pl.ds(2 + k, sources, stride=8), :])
        predicted = predicted + weights[k] * picked
    innov = predicted - slots_ref[pl.ds(6, sources, stride=8), :]
    innov_ref[...] = innov
    for k in range(4):
        rows = slice(k * sources, (k + 1) * sources)
        term = weights[k] * innov
        high = term.astype(BF16).astype(F32)
        term_ref[0, rows, :] = high
        term_ref[1, rows, :] = term - high
        place_ref[0, rows, :] = places[k] >> 4
        place_ref[1, rows, :] = places[k] & 15

    digit = lax.broadcasted_iota(jnp.int32, (16, 128), 0)
    per_step = 32

    def add_rows(step, total):
        left, right = [], []
        for inner in range(per_step):
            at = pl.ds(step * per_step + inner, 1)
            left.append(jnp.where(digit == place_ref[0, at, :], 1.0, 0.0).astype(BF16))
            hit = digit == place_ref[1, at, :]
            terms = [jnp.where(hit, term_ref[i, at, :], 0.0) for i in range(2)]
            right.append(jnp.concatenate(terms, axis=0).astype(BF16))
        return total + mm(jnp.concatenate(left, axis=1), jnp.concatenate(right, axis=1), NT)

    total = lax.fori_loop(0, 4 * sources // per_step, add_rows, jnp.zeros((16, 32), F32))
    total = total[:, :16] + total[:, 16:]

    def cells(shape, axis):
        cell = lax.broadcasted_iota(jnp.int32, shape, axis)
        digits = lax.broadcasted_iota(jnp.int32, shape, 1 - axis)
        return cell // 16 == digits, cell % 16 == digits

    high, low = cells((OWN, 16), 0)
    column = exact(high.astype(F32), total)
    adjoint = jnp.sum(jnp.where(low, column, 0.0), axis=1, keepdims=True)
    high, low = cells((16, OWN), 1)
    row = jnp.sum(jnp.where(high, exact(total, low.astype(F32)), 0.0), axis=0, keepdims=True)
    adjoint_ref[...] = jnp.concatenate([row, jnp.zeros((1, 256 - OWN), F32)], axis=1)
    edge_ref[...] = row[:, :128]
    low_plane = (lax.axis_index("lon") // 2) % 2 == 0
    for side in range(2):
        by_plane = [innov_ref[pl.ds(2 * h + side, sources // 4, stride=4), :] for h in range(2)]
        place = pl.ds(side, sources // 4, stride=2)
        mine_ref[place, :] = jnp.where(low_plane, by_plane[0], by_plane[1])
        other_ref[place, :] = jnp.where(low_plane, by_plane[1], by_plane[0])

    factor = 0.5 * loss_scale
    g_query = gq_ref[...].astype(BF16)
    up = up_ref[...]
    grad_low = mm(g_query, up, NT)
    up_query = mm((low_own_ref[...] * adjoint).astype(BF16), g_query, TN)
    down_query = mm((grad_low * adjoint).astype(BF16), own_norm_ref[...], TN)

    weighted = [None] * 6
    for n in range(8):
        window = (n // 4) * 3 + (n % 4 + 1) // 2
        probs = probs_ref[n].astype(F32).reshape(HEADS, GROUP, WINDOW)
        part = jnp.sum(probs * adjoint[n * GROUP : (n + 1) * GROUP].reshape(1, GROUP, 1), axis=1)
        weighted[window] = part if weighted[window] is None else weighted[window] + part
    head = lax.broadcasted_iota(jnp.int32, (HEADS, MODEL), 0)
    of_head = head == lax.broadcasted_iota(jnp.int32, (HEADS, MODEL), 1) // HEAD_DIM
    w_masked = jnp.where(of_head, jnp.broadcast_to(w_ref[0:1, :], (HEADS, MODEL)), 0.0)
    rank_head = exact(up.astype(F32), w_masked, NT)
    sums, down_value = jnp.zeros((HEADS, 16), F32), jnp.zeros((16, MODEL), F32)
    for window in range(6):
        keys = slice(window * WINDOW, (window + 1) * WINDOW)
        sums = sums + mm(weighted[window].astype(BF16), low_ref[keys, :])
        of_rank = exact(rank_head, weighted[window])
        down_value = down_value + mm(of_rank.astype(BF16), norm_ref[keys, :])
    up_value = exact(sums, w_masked, TN)

    parts = (up_query[:8], up_value[8:], down_query[:8], down_value[8:])
    for m, part in enumerate(parts):
        part = part * factor
        for q in range(4):
            grads_ref[pl.ds(q * 32 + m, 8, stride=4), :] = part[:, 128 * q : 128 * (q + 1)]


def core_kernel(
    own_ref,
    near_lon_ref,
    far_lon_ref,
    far_lat_ref,
    near_lat_ref,
    qkv_hbm,
    wo_hbm,
    down_ref,
    up_ref,
    readout_ref,
    bias_hbm,
    slots_hbm,
    block_ref,
    adjoint_ref,
    edge_ref,
    grads_ref,
    mine_ref,
    other_ref,
    field_ref,
    probs_ref,
    gq_ref,
    low_ref,
    norm_ref,
    own_norm_ref,
    low_own_ref,
    w_ref,
    k_ref,
    v_ref,
    q_ref,
    att_ref,
    qkv_ref,
    wo_ref,
    bias_ref,
    copy_sems,
    innov_ref,
    term_ref,
    place_ref,
    slots_ref,
    loss_scale,
    lat_count,
):
    slot_load = pltpu.make_async_copy(slots_hbm, slots_ref, copy_sems.at[3])
    slot_load.start()
    forward_part(
        lat_count,
        own_ref,
        near_lon_ref,
        far_lon_ref,
        near_lat_ref,
        far_lat_ref,
        qkv_hbm,
        wo_hbm,
        down_ref,
        up_ref,
        readout_ref,
        bias_hbm,
        block_ref,
        field_ref,
        probs_ref,
        gq_ref,
        low_ref,
        norm_ref,
        own_norm_ref,
        low_own_ref,
        w_ref,
        k_ref,
        v_ref,
        q_ref,
        att_ref,
        qkv_ref,
        wo_ref,
        bias_ref,
        copy_sems,
    )
    slot_load.wait()
    observe_part(
        slots_ref,
        field_ref,
        probs_ref,
        gq_ref,
        low_ref,
        norm_ref,
        own_norm_ref,
        low_own_ref,
        w_ref,
        up_ref,
        adjoint_ref,
        edge_ref,
        grads_ref,
        mine_ref,
        other_ref,
        innov_ref,
        term_ref,
        place_ref,
        loss_scale,
    )


def core(own, halos, qkv, wo, down, up, readout, bias, slots, loss_scale, lat_count):
    sources = slots.shape[0] // 8
    shape = jax.ShapeDtypeStruct
    vmem, far = pl.BlockSpec(memory_space=pltpu.VMEM), pl.BlockSpec(memory_space=pl.ANY)
    return pl.pallas_call(
        functools.partial(core_kernel, loss_scale=loss_scale, lat_count=lat_count),
        in_specs=[vmem] * 5 + [far] * 2 + [vmem] * 3 + [far] * 2,
        out_specs=[vmem] * 6,
        out_shape=[
            shape((OWN, MODEL), BF16),
            shape((1, 256), F32),
            shape((1, 128), F32),
            shape((128, 128), F32),
            shape((sources // 2, 128), F32),
            shape((sources // 2, 128), F32),
        ],
        scratch_shapes=[
            pltpu.VMEM((8, 256), F32),
            pltpu.VMEM((8, HEADS * GROUP, WINDOW), BF16),
            pltpu.VMEM((OWN, MODEL), F32),
            pltpu.VMEM((6 * WINDOW, 16), BF16),
            pltpu.VMEM((6 * WINDOW, MODEL), BF16),
            pltpu.VMEM((OWN, MODEL), BF16),
            pltpu.VMEM((OWN, 16), F32),
            pltpu.VMEM((8, MODEL), F32),
            pltpu.VMEM((6 * WINDOW, MODEL), BF16),
            pltpu.VMEM((6 * WINDOW, MODEL), BF16),
            pltpu.VMEM((OWN, MODEL), F32),
            pltpu.VMEM((OWN, MODEL), F32),
            pltpu.VMEM((MODEL, 3 * MODEL), BF16),
            pltpu.VMEM((MODEL, MODEL), BF16),
            pltpu.VMEM((4, HEADS, GROUP, WINDOW), F32),
            pltpu.SemaphoreType.DMA((4,)),
            pltpu.VMEM((sources, 128), F32),
            pltpu.VMEM((2, 4 * sources, 128), F32),
            pltpu.VMEM((2, 4 * sources, 128), jnp.int32),
            pltpu.VMEM((sources * 8, 128), F32),
        ],
        compiler_params=pltpu.CompilerParams(vmem_limit_bytes=58 * 1024 * 1024),
        cost_estimate=pl.CostEstimate(
            flops=3 * 10**9, bytes_accessed=8 * 10**6, transcendentals=4 * 10**5
        ),
        name="window_and_observe",
    )(own, *halos, qkv, wo, down, up, readout, bias, slots)


def finish_kernel(final_ref, moved_ref, up_ref, down_ref, innov_ref, rolled_ref, rows_ref):
    members = final_ref.shape[0] // 8
    rows_ref[...] = final_ref[...].astype(F32)
    for m, (ref, which) in enumerate(((up_ref, 0), (up_ref, 1), (down_ref, 0), (down_ref, 1))):
        for q in range(4):
            ref[which, :, 128 * q : 128 * (q + 1)] = rows_ref[pl.ds(q * 64 + m, 8, stride=8), :]
    lon = lax.axis_index("lon")
    plane, member = (lon // 2) % 2, lon // 4 * 2 + lon % 2
    for side in range(2):
        near, far = [rows_ref[pl.ds(8 * side + i, members // 2, stride=16), :] for i in (6, 7)]
        for h in range(2):
            innov_ref[pl.ds(2 * h + side, members // 2, stride=4), :] = jnp.where(plane == h, near, far)

    across = member - 1 + 2 * plane
    across = jnp.where(across >= members, 0, across)
    row = jnp.where(lon % 2 == 0, (member + 1) * 8 + 4, across * 8 + 5)
    lane = lax.broadcasted_iota(jnp.int32, (16, 128), 1)
    patch_row = lax.broadcasted_iota(jnp.int32, (16, 128), 0)
    source = (patch_row // 3 * GROUP + patch_row % 3 * 6 + lane % 6) & 127
    halves = [
        jnp.take_along_axis(jnp.broadcast_to(values, (16, 128)), source, axis=1)
        for values in (moved_ref[...], rows_ref[pl.ds(row, 1), :])
    ]
    rolled_ref[...] = jnp.where(lane < 6, halves[0], halves[1])[:12, :12]


def finish(final, moved):
    members = final.shape[0] // 8
    shape = jax.ShapeDtypeStruct
    return pl.pallas_call(
        finish_kernel,
        out_shape=[
            shape((2, 8, MODEL), F32),
            shape((2, 8, MODEL), F32),
            shape((2 * members, 128), F32),
            shape((12, 12), F32),
        ],
        scratch_shapes=[pltpu.VMEM((members * 8, 128), F32)],
        name="finish",
    )(final, moved)


def paired(value, axis, odd_first):
    count = lax.axis_size(axis)
    if odd_first:
        pairs = [(i, (i + 1) % count if i % 2 else (i - 1) % count) for i in range(count)]
    else:
        pairs = [(i, i ^ 1) for i in range(count)]
    return lax.ppermute(value, axis, pairs)


def shards(
    tokens,
    query_key_value_weight,
    output_weight,
    adapter_down_map,
    adapter_up_map,
    relative_position_bias,
    readout,
    observation_index,
    observation_weight,
    observation_value,
    observation_count,
):
    lat_count, lon_count = lax.axis_size("lat"), lax.axis_size("lon")
    lat, lon = lax.axis_index("lat"), lax.axis_index("lon")
    even_lat, even_lon = lat % 2 == 0, lon % 2 == 0

    own = tokens.reshape(4, 3, 2, 6, MODEL).transpose(2, 0, 1, 3, 4).reshape(2, 4, LIVE, MODEL)
    own = lax.optimization_barrier(own)
    near_send, far_send, observation_index = lax.optimization_barrier(
        (
            jnp.where(even_lon, own[1], own[0]),
            jnp.where(even_lon, own[0], own[1]),
            observation_index,
        )
    )
    far_lon = paired(far_send, "lon", True)

    slots = packed_slots(
        observation_index.reshape(lon_count * 4, 128),
        observation_weight.reshape(lon_count * 4, 128),
        observation_value.reshape(lon_count, 128),
        observation_count.reshape(1, lon_count),
    ).reshape(lon_count, 8, 128)
    near_send, slots = lax.optimization_barrier((near_send, slots))
    near_lon = paired(near_send, "lon", False)

    left = jnp.where(even_lon, far_lon, near_lon)
    right = jnp.where(even_lon, near_lon, far_lon)
    top = jnp.stack([left[0], own[0, 0], own[1, 0], right[0]])
    bottom = jnp.stack([left[3], own[0, 3], own[1, 3], right[3]])
    near_send, far_send, readout = lax.optimization_barrier(
        (jnp.where(even_lat, bottom, top), jnp.where(even_lat, top, bottom), readout)
    )
    far_send, readout, bias = lax.optimization_barrier(
        (far_send, readout.reshape(1, MODEL), relative_position_bias)
    )
    far_lat = paired(far_send, "lat", True)
    near_lat = paired(near_send, "lat", False)
    slots = lax.all_to_all(slots, "lon", 0, 0, tiled=True).reshape(lon_count * 8, 128)

    down_rows = adapter_down_map.reshape(16, MODEL)
    up_rows = adapter_up_map.reshape(16, MODEL)
    loss_scale = 1.0 / math.sqrt(lat_count * lon_count)
    block, adjoint, edge_row, grads, mine, other = core(
        own,
        (near_lon, far_lon, far_lat, near_lat),
        query_key_value_weight,
        output_weight,
        down_rows,
        up_rows,
        readout,
        ordered_bias(bias),
        slots,
        loss_scale,
        lat_count,
    )
    block = block.reshape(2, 4, GROUP, MODEL)[:, :, :LIVE].reshape(2, 4, 3, 6, MODEL)
    block_out = block.transpose(1, 2, 0, 3, 4).reshape(12, 12, MODEL)

    members = lon_count // 2
    plane = (lon // 2) % 2
    planes = [[i for i in range(lon_count) if (i // 2) % 2 == h] for h in range(2)]
    columns = [
        [a * lon_count + at * 4 + h * 2 + c for h in range(2) for a in range(lat_count)]
        for at in range(members // 2)
        for c in range(2)
    ]

    chunks = lax.all_to_all(
        grads.reshape(members, 4, 128), "lon", 0, 0, axis_index_groups=planes, tiled=True
    )
    other = lax.ppermute(other, "lon", [(i, i ^ 2) for i in range(lon_count)])

    chunk = jnp.concatenate([jnp.sum(chunks, axis=0), edge_row], axis=0)
    along = lax.all_to_all(
        jnp.broadcast_to(chunk[None], (2 * lat_count, 5, 128)),
        ("lat", "lon"),
        0,
        0,
        axis_index_groups=columns,
        tiled=True,
    )
    total = jnp.sum(along[:, :4], axis=0)
    edges = along[:, 4]
    below_at = (lat + 1) % lat_count

    def edge_of(h, a):
        return lax.dynamic_index_in_dim(edges, h * lat_count + a, 0, keepdims=False)

    def moved_up(here, below):
        kept = here[: 4 * GROUP].reshape(4, GROUP)[1:]
        return jnp.concatenate([kept.reshape(3 * GROUP), below[:GROUP]])

    below = edge_of(plane, below_at)
    edge = moved_up(adjoint[0], below)
    twin_edge = moved_up(edge_of(1 - plane, lat), edge_of(1 - plane, below_at))
    shared = jnp.concatenate(
        [total, jnp.pad(jnp.stack([edge, twin_edge]), ((0, 0), (0, 128 - 4 * GROUP)))], axis=0
    )
    final = jnp.concatenate(
        [jnp.broadcast_to(shared[None], (members, 6, 128)), mine[:, None], other[:, None]], axis=1
    )
    final = lax.all_to_all(
        final.astype(BF16), "lon", 0, 0, axis_index_groups=planes, tiled=True
    )

    kept = adjoint[0, 4 * GROUP : OWN]
    moved = jnp.concatenate([kept[GROUP:], below[4 * GROUP : 5 * GROUP], jnp.zeros((GROUP + 8,), F32)])
    up_gradient, down_gradient, innovation, rolled_adjoint = finish(
        final.reshape(members * 8, 128), moved.reshape(1, 128)
    )
    return block_out, innovation[None, None], rolled_adjoint, down_gradient, up_gradient


def solution(mesh):
    return jax.shard_map(
        shards,
        mesh=mesh,
        in_specs=(
            P("lat", "lon", None),
            P(),
            P(),
            P(),
            P(),
            P(),
            P(),
            P("lat", "lon", None, None, None),
            P("lat", "lon", None, None, None),
            P("lat", "lon", None, None),
            P("lat", "lon", None),
        ),
        out_specs=(P("lat", "lon", None), P("lat", "lon", None, None), P("lat", "lon"), P(), P()),
        check_vma=False,
    )
```

```python
import functools
import math

import jax
import jax.numpy as jnp
from jax import lax
from jax.experimental import pallas as pl
from jax.experimental.pallas import tpu as pltpu
from jax.sharding import PartitionSpec as P

F32 = jnp.float32
BF16 = jnp.bfloat16
HEADS = 16
HEAD_DIM = 32
MODEL = 512
GROUP = 24
WINDOW = 4 * GROUP
LIVE = 18
OWN = 8 * GROUP
NORM_EPS = 1e-05
NEG = -1e30
NT = (((1,), (1,)), ((), ()))
TN = (((0,), (0,)), ((), ()))
NN = (((1,), (0,)), ((), ()))


def mm(a, b, dims=NN, precision=None):
    return lax.dot_general(a, b, dims, precision=precision, preferred_element_type=F32)


def exact(a, b, dims=NN):
    return mm(a, b, dims, precision=lax.Precision.HIGHEST)


def bias_kernel(bias_ref, out_ref, wide_ref):
    shape = (72, WINDOW)
    lane = lax.broadcasted_iota(jnp.int32, shape, 1)
    row = lane % GROUP
    column = 12 * (3 * ((lane // GROUP) % 2) + row // 6) + 6 * (lane // (2 * GROUP)) + row % 6
    hit = (column == lax.broadcasted_iota(jnp.int32, shape, 0)) & (row < LIVE)
    wide = exact(bias_ref[...], hit.astype(F32))
    lanes = lax.broadcasted_iota(jnp.int32, (1, WINDOW), 1)
    wide = wide + jnp.where(lanes % GROUP < LIVE, 0.0, NEG)
    wide_ref[...] = wide.reshape(HEADS, 72, WINDOW)
    out_ref[...] = jnp.zeros_like(out_ref)
    for parity in range(2):
        for half in range(2):
            for m in range(3):
                start = 12 * (3 * (1 - parity) + m) + 6 * (1 - half)
                out_ref[parity * 2 + half, :, 6 * m : 6 * m + 6, :] = wide_ref[:, start : start + 6, :]


def ordered_bias(bias):
    return pl.pallas_call(
        bias_kernel,
        out_shape=jax.ShapeDtypeStruct((4, HEADS, GROUP, WINDOW), F32),
        scratch_shapes=[pltpu.VMEM((HEADS, 72, WINDOW), F32)],
        cost_estimate=pl.CostEstimate(flops=2 * 10**10, bytes_accessed=2 * 10**6, transcendentals=0),
        name="ordered_bias",
    )(bias.reshape(HEADS * 72, 72))


def slots_kernel(index_ref, weight_ref, value_ref, count_ref, out_ref):
    strips = value_ref.shape[0]
    square = (strips, strips)
    own_lane = lax.broadcasted_iota(jnp.int32, square, 0) == lax.broadcasted_iota(jnp.int32, square, 1)
    counts = jnp.broadcast_to(count_ref[...].astype(F32), square)
    counts = jnp.sum(jnp.where(own_lane, counts, 0.0), axis=1, keepdims=True).astype(jnp.int32)
    live = lax.broadcasted_iota(jnp.int32, (strips, 128), 1) < counts
    places = []
    for k in range(4):
        cell = index_ref[pl.ds(k, strips, stride=4), :]
        row = (cell * 171) >> 11
        col = cell - 12 * row
        group = (row * 11) >> 5
        half = (col >= 6).astype(jnp.int32)
        places.append((half * 4 + group) * GROUP + (row - 3 * group) * 6 + col - 6 * half)
        weight = weight_ref[pl.ds(k, strips, stride=4), :]
        out_ref[pl.ds(2 + k, strips, stride=8), :] = jnp.where(live, weight, 0.0)
    for pair in range(2):
        packed = places[2 * pair] + 1024 * places[2 * pair + 1]
        out_ref[pl.ds(pair, strips, stride=8), :] = packed.astype(F32)
    out_ref[pl.ds(6, strips, stride=8), :] = jnp.where(live, value_ref[...], 0.0)
    out_ref[pl.ds(7, strips, stride=8), :] = jnp.zeros((strips, 128), F32)


def packed_slots(index, weight, value, count):
    return pl.pallas_call(
        slots_kernel,
        out_shape=jax.ShapeDtypeStruct((value.shape[0] * 8, 128), F32),
        cost_estimate=pl.CostEstimate(flops=10**6, bytes_accessed=5 * 10**5, transcendentals=0),
        name="packed_slots",
    )(index, weight, value, count)


def forward_part(
    lat_count,
    own_ref,
    near_lon_ref,
    far_lon_ref,
    near_lat_ref,
    far_lat_ref,
    qkv_hbm,
    wo_hbm,
    down_ref,
    up_ref,
    readout_ref,
    bias_hbm,
    block_ref,
    field_ref,
    probs_ref,
    gq_ref,
    low_ref,
    norm_ref,
    own_norm_ref,
    low_own_ref,
    w_ref,
    k_ref,
    v_ref,
    q_ref,
    att_ref,
    qkv_ref,
    wo_ref,
    bias_ref,
    copy_sems,
):
    loads = [
        pltpu.make_async_copy(source, target, copy_sems.at[i])
        for i, (source, target) in enumerate(
            ((qkv_hbm, qkv_ref), (bias_hbm, bias_ref), (wo_hbm, wo_ref))
        )
    ]
    for load in loads:
        load.start()
    lat = lax.axis_index("lat")
    even_lon = lax.axis_index("lon") % 2 == 0
    even_lat = lat % 2 == 0
    first = (lat == 0).astype(F32)
    last = (lat == lat_count - 1).astype(F32)

    def pick(cond, a, b):
        return jnp.where(cond, a.astype(F32), b.astype(F32))

    gap = jnp.zeros((GROUP - LIVE, MODEL), F32)

    def piece(strip, group):
        rows = []
        for i in range(3):
            at = 3 * (group - 1) + i
            if group == 0:
                rows.append(pick(even_lat, far_lat_ref[strip, i], near_lat_ref[strip, i]))
            elif group == 5:
                rows.append(pick(even_lat, near_lat_ref[strip, i], far_lat_ref[strip, i]))
            elif strip == 0:
                rows.append(pick(even_lon, far_lon_ref[at], near_lon_ref[at]))
            elif strip == 3:
                rows.append(pick(even_lon, near_lon_ref[at], far_lon_ref[at]))
            else:
                rows.append(own_ref[at].astype(F32)[6 * (strip - 1) : 6 * strip])
        return jnp.concatenate(rows + [gap], axis=0)

    for strip in range(4):
        rows = []
        for pair in range(3):
            x = jnp.concatenate([piece(strip, 2 * pair + i) for i in range(2)], axis=0)
            center = x - jnp.mean(x, axis=1, keepdims=True)
            spread = jnp.mean(center * center, axis=1, keepdims=True)
            y = center * lax.rsqrt(spread + NORM_EPS)
            at = ((strip // 2) * 3 + pair) * WINDOW + (strip % 2) * 2 * GROUP
            norm_ref[at : at + 2 * GROUP, :] = y.astype(BF16)
            rows.append(y)
        if strip in (1, 2):
            mine = jnp.concatenate([rows[0][GROUP:], rows[1], rows[2][:GROUP]], axis=0)
            own_norm_ref[(strip - 1) * 4 * GROUP : strip * 4 * GROUP, :] = mine.astype(BF16)

    normed = norm_ref[...]
    for load in loads:
        load.wait()
    rank_row = lax.broadcasted_iota(jnp.int32, (16, MODEL), 0)
    up_half = 0.5 * up_ref[...].astype(F32)
    up_query = jnp.where(rank_row < 8, up_half, 0.0).astype(BF16)
    up_value = jnp.where(rank_row >= 8, up_half, 0.0).astype(BF16)
    low = mm(normed, down_ref[...], NT).astype(BF16)
    low_ref[...] = low
    k_ref[...] = mm(normed, qkv_ref[:, MODEL : 2 * MODEL]).astype(BF16)
    v_ref[...] = (mm(normed, qkv_ref[:, 2 * MODEL :]) + mm(low, up_value)).astype(BF16)
    normed_own = own_norm_ref[...]
    low_own = mm(normed_own, down_ref[...], NT).astype(BF16)
    low_own_ref[...] = low_own.astype(F32)
    query = mm(normed_own, qkv_ref[:, :MODEL]) + mm(low_own, up_query)
    q_ref[...] = query.astype(BF16).astype(F32)

    readout = jnp.broadcast_to(readout_ref[...].astype(F32), (8, MODEL)).astype(BF16)
    w_row = mm(readout, wo_ref[...], NT)
    w_ref[...] = w_row

    scale = 1.0 / math.sqrt(HEAD_DIM)
    head_of = lax.broadcasted_iota(jnp.int32, (8, 1, 256), 2) // HEAD_DIM
    head_mask = head_of == lax.broadcasted_iota(jnp.int32, (8, 1, 256), 0)
    lane_part = (lax.broadcasted_iota(jnp.int32, (1, WINDOW), 1) // GROUP) % 2
    masked_first = jnp.where(lane_part == 0, NEG * first, 0.0)
    masked_last = jnp.where(lane_part == 1, NEG * last, 0.0)

    ones = jnp.ones((WINDOW, WINDOW), BF16)

    def fold(rows):
        return jnp.sum(jnp.where(head_mask, rows.reshape(8, GROUP, 256), 0.0), axis=0)

    for n in range(8):
        half, row = n // 4, n % 4
        window = half * 3 + (row + 1) // 2
        keys = slice(window * WINDOW, (window + 1) * WINDOW)
        for part in range(2):
            cols = slice(256 * part, 256 * (part + 1))
            k_win, v_win = k_ref[keys, cols], v_ref[keys, cols]
            q_own = q_ref[n * GROUP : (n + 1) * GROUP, cols]
            lhs = jnp.where(head_mask, q_own[None], 0.0).reshape(8 * GROUP, 256).astype(BF16)
            bias = bias_ref[(row % 2) * 2 + half, 8 * part : 8 * part + 8].reshape(8 * GROUP, WINDOW)
            scores = mm(lhs, k_win, NT) * scale + bias
            if row == 0:
                scores = scores + masked_first
            if row == 3:
                scores = scores + masked_last
            raised = jnp.exp(scores - jnp.max(scores, axis=1, keepdims=True))
            probs = raised * (1.0 / jnp.sum(raised, axis=1, keepdims=True))
            probs_bf = probs.astype(BF16)
            probs_ref[n, 8 * GROUP * part : 8 * GROUP * (part + 1), :] = probs_bf
            att_ref[n * GROUP : (n + 1) * GROUP, cols] = fold(mm(probs_bf, v_win))
            w_masked = jnp.where(head_mask[:, 0, :], w_row[:, cols], 0.0)
            w_high = w_masked.astype(BF16).astype(F32)
            w_pair = jnp.concatenate([w_high, w_masked - w_high], axis=0).astype(BF16)
            v_pair = mm(w_pair, v_win, NT)
            v_w = (v_pair[:8] + v_pair[8:]).reshape(8, 1, WINDOW)
            v_w = jnp.broadcast_to(v_w, (8, GROUP, WINDOW)).reshape(8 * GROUP, WINDOW)
            share = probs * v_w
            share_high = share.astype(BF16)
            share_low = (share - share_high.astype(F32)).astype(BF16)
            mean = jnp.sum(share, axis=1, keepdims=True)
            slope = (probs * (v_w - mean) * scale).astype(BF16)
            gq_ref[n * GROUP : (n + 1) * GROUP, cols] = fold(mm(slope, k_win))

    x_own = jnp.concatenate([piece(1 + n // 4, 1 + n % 4) for n in range(8)], axis=0)
    out = (x_own + mm(att_ref[...].astype(BF16), wo_ref[...])).astype(BF16)
    wide = out.astype(F32)
    for row in range(12):
        starts = [(half * 4 + row // 3) * GROUP + 6 * (row % 3) for half in range(2)]
        pair = jnp.concatenate([wide[start : start + 6] for start in starts], axis=0)
        block_ref[row] = pair.astype(BF16)
    field_ref[...] = jnp.zeros_like(field_ref)
    field_ref[:, :OWN] = mm(readout, out, NT)


def observe_part(
    slots_ref,
    field_ref,
    probs_ref,
    gq_ref,
    low_ref,
    norm_ref,
    own_norm_ref,
    low_own_ref,
    w_ref,
    up_ref,
    adjoint_ref,
    edge_ref,
    grads_ref,
    mine_ref,
    other_ref,
    innov_ref,
    term_ref,
    place_ref,
    loss_scale,
):
    sources = innov_ref.shape[0]
    field_low = jnp.broadcast_to(field_ref[0:1, 0:128], (sources, 128))
    field_high = jnp.broadcast_to(field_ref[0:1, 128:256], (sources, 128))
    places, weights = [], []
    for pair in range(2):
        packed = slots_ref[pl.ds(pair, sources, stride=8), :].astype(jnp.int32)
        places += [packed & 1023, packed >> 10]
    predicted = jnp.zeros((sources, 128), F32)
    for k in range(4):
        lane = places[k] & 127
        picked = jnp.where(
            places[k] < 128,
            jnp.take_along_axis(field_low, lane, axis=1),
            jnp.take_along_axis(field_high, lane, axis=1),
        )
        weights.append(slots_ref[pl.ds(2 + k, sources, stride=8), :])
        predicted = predicted + weights[k] * picked
    innov = predicted - slots_ref[pl.ds(6, sources, stride=8), :]
    innov_ref[...] = innov
    for k in range(4):
        rows = slice(k * sources, (k + 1) * sources)
        term = weights[k] * innov
        high = term.astype(BF16).astype(F32)
        term_ref[0, rows, :] = high
        term_ref[1, rows, :] = term - high
        place_ref[0, rows, :] = places[k] >> 4
        place_ref[1, rows, :] = places[k] & 15

    digit = lax.broadcasted_iota(jnp.int32, (16, 128), 0)
    per_step = 32

    def add_rows(step, total):
        left, right = [], []
        for inner in range(per_step):
            at = pl.ds(step * per_step + inner, 1)
            left.append(jnp.where(digit == place_ref[0, at, :], 1.0, 0.0).astype(BF16))
            hit = digit == place_ref[1, at, :]
            terms = [jnp.where(hit, term_ref[i, at, :], 0.0) for i in range(2)]
            right.append(jnp.concatenate(terms, axis=0).astype(BF16))
        return total + mm(jnp.concatenate(left, axis=1), jnp.concatenate(right, axis=1), NT)

    total = lax.fori_loop(0, 4 * sources // per_step, add_rows, jnp.zeros((16, 32), F32))
    total = total[:, :16] + total[:, 16:]

    def cells(shape, axis):
        cell = lax.broadcasted_iota(jnp.int32, shape, axis)
        digits = lax.broadcasted_iota(jnp.int32, shape, 1 - axis)
        return cell // 16 == digits, cell % 16 == digits

    high, low = cells((OWN, 16), 0)
    column = exact(high.astype(F32), total)
    adjoint = jnp.sum(jnp.where(low, column, 0.0), axis=1, keepdims=True)
    high, low = cells((16, OWN), 1)
    row = jnp.sum(jnp.where(high, exact(total, low.astype(F32)), 0.0), axis=0, keepdims=True)
    adjoint_ref[...] = jnp.concatenate([row, jnp.zeros((1, 256 - OWN), F32)], axis=1)
    edge_ref[...] = row[:, :128]
    low_plane = (lax.axis_index("lon") // 2) % 2 == 0
    for side in range(2):
        by_plane = [innov_ref[pl.ds(2 * h + side, sources // 4, stride=4), :] for h in range(2)]
        place = pl.ds(side, sources // 4, stride=2)
        mine_ref[place, :] = jnp.where(low_plane, by_plane[0], by_plane[1])
        other_ref[place, :] = jnp.where(low_plane, by_plane[1], by_plane[0])

    factor = 0.5 * loss_scale
    g_query = gq_ref[...].astype(BF16)
    up = up_ref[...]
    grad_low = mm(g_query, up, NT)
    up_query = mm((low_own_ref[...] * adjoint).astype(BF16), g_query, TN)
    down_query = mm((grad_low * adjoint).astype(BF16), own_norm_ref[...], TN)

    weighted = [None] * 6
    for n in range(8):
        window = (n // 4) * 3 + (n % 4 + 1) // 2
        probs = probs_ref[n].astype(F32).reshape(HEADS, GROUP, WINDOW)
        part = jnp.sum(probs * adjoint[n * GROUP : (n + 1) * GROUP].reshape(1, GROUP, 1), axis=1)
        weighted[window] = part if weighted[window] is None else weighted[window] + part
    head = lax.broadcasted_iota(jnp.int32, (HEADS, MODEL), 0)
    of_head = head == lax.broadcasted_iota(jnp.int32, (HEADS, MODEL), 1) // HEAD_DIM
    w_masked = jnp.where(of_head, jnp.broadcast_to(w_ref[0:1, :], (HEADS, MODEL)), 0.0)
    rank_head = exact(up.astype(F32), w_masked, NT)
    sums, down_value = jnp.zeros((HEADS, 16), F32), jnp.zeros((16, MODEL), F32)
    for window in range(6):
        keys = slice(window * WINDOW, (window + 1) * WINDOW)
        sums = sums + mm(weighted[window].astype(BF16), low_ref[keys, :])
        of_rank = exact(rank_head, weighted[window])
        down_value = down_value + mm(of_rank.astype(BF16), norm_ref[keys, :])
    up_value = exact(sums, w_masked, TN)

    parts = (up_query[:8], up_value[8:], down_query[:8], down_value[8:])
    for m, part in enumerate(parts):
        part = part * factor
        for q in range(4):
            grads_ref[pl.ds(q * 32 + m, 8, stride=4), :] = part[:, 128 * q : 128 * (q + 1)]


def core_kernel(
    own_ref,
    near_lon_ref,
    far_lon_ref,
    far_lat_ref,
    near_lat_ref,
    qkv_hbm,
    wo_hbm,
    down_ref,
    up_ref,
    readout_ref,
    bias_hbm,
    slots_hbm,
    block_ref,
    adjoint_ref,
    edge_ref,
    grads_ref,
    mine_ref,
    other_ref,
    field_ref,
    probs_ref,
    gq_ref,
    low_ref,
    norm_ref,
    own_norm_ref,
    low_own_ref,
    w_ref,
    k_ref,
    v_ref,
    q_ref,
    att_ref,
    qkv_ref,
    wo_ref,
    bias_ref,
    copy_sems,
    innov_ref,
    term_ref,
    place_ref,
    slots_ref,
    loss_scale,
    lat_count,
):
    slot_load = pltpu.make_async_copy(slots_hbm, slots_ref, copy_sems.at[3])
    slot_load.start()
    forward_part(
        lat_count,
        own_ref,
        near_lon_ref,
        far_lon_ref,
        near_lat_ref,
        far_lat_ref,
        qkv_hbm,
        wo_hbm,
        down_ref,
        up_ref,
        readout_ref,
        bias_hbm,
        block_ref,
        field_ref,
        probs_ref,
        gq_ref,
        low_ref,
        norm_ref,
        own_norm_ref,
        low_own_ref,
        w_ref,
        k_ref,
        v_ref,
        q_ref,
        att_ref,
        qkv_ref,
        wo_ref,
        bias_ref,
        copy_sems,
    )
    slot_load.wait()
    observe_part(
        slots_ref,
        field_ref,
        probs_ref,
        gq_ref,
        low_ref,
        norm_ref,
        own_norm_ref,
        low_own_ref,
        w_ref,
        up_ref,
        adjoint_ref,
        edge_ref,
        grads_ref,
        mine_ref,
        other_ref,
        innov_ref,
        term_ref,
        place_ref,
        loss_scale,
    )


def core(own, halos, qkv, wo, down, up, readout, bias, slots, loss_scale, lat_count):
    sources = slots.shape[0] // 8
    shape = jax.ShapeDtypeStruct
    vmem, far = pl.BlockSpec(memory_space=pltpu.VMEM), pl.BlockSpec(memory_space=pl.ANY)
    return pl.pallas_call(
        functools.partial(core_kernel, loss_scale=loss_scale, lat_count=lat_count),
        in_specs=[vmem] * 5 + [far] * 2 + [vmem] * 3 + [far] * 2,
        out_specs=[vmem] * 6,
        out_shape=[
            shape((12, 12, MODEL), BF16),
            shape((1, 256), F32),
            shape((1, 128), F32),
            shape((128, 128), F32),
            shape((sources // 2, 128), F32),
            shape((sources // 2, 128), F32),
        ],
        scratch_shapes=[
            pltpu.VMEM((8, 256), F32),
            pltpu.VMEM((8, HEADS * GROUP, WINDOW), BF16),
            pltpu.VMEM((OWN, MODEL), F32),
            pltpu.VMEM((6 * WINDOW, 16), BF16),
            pltpu.VMEM((6 * WINDOW, MODEL), BF16),
            pltpu.VMEM((OWN, MODEL), BF16),
            pltpu.VMEM((OWN, 16), F32),
            pltpu.VMEM((8, MODEL), F32),
            pltpu.VMEM((6 * WINDOW, MODEL), BF16),
            pltpu.VMEM((6 * WINDOW, MODEL), BF16),
            pltpu.VMEM((OWN, MODEL), F32),
            pltpu.VMEM((OWN, MODEL), F32),
            pltpu.VMEM((MODEL, 3 * MODEL), BF16),
            pltpu.VMEM((MODEL, MODEL), BF16),
            pltpu.VMEM((4, HEADS, GROUP, WINDOW), F32),
            pltpu.SemaphoreType.DMA((4,)),
            pltpu.VMEM((sources, 128), F32),
            pltpu.VMEM((2, 4 * sources, 128), F32),
            pltpu.VMEM((2, 4 * sources, 128), jnp.int32),
            pltpu.VMEM((sources * 8, 128), F32),
        ],
        compiler_params=pltpu.CompilerParams(vmem_limit_bytes=58 * 1024 * 1024),
        cost_estimate=pl.CostEstimate(
            flops=3 * 10**9, bytes_accessed=8 * 10**6, transcendentals=4 * 10**5
        ),
        name="window_and_observe",
    )(own, *halos, qkv, wo, down, up, readout, bias, slots)


def finish_kernel(final_ref, moved_ref, up_ref, down_ref, innov_ref, rolled_ref):
    members = final_ref.shape[0] // 8
    for m, (ref, which) in enumerate(((up_ref, 0), (up_ref, 1), (down_ref, 0), (down_ref, 1))):
        for q in range(4):
            ref[which, :, 128 * q : 128 * (q + 1)] = final_ref[pl.ds(q * 64 + m, 8, stride=8), :]
    lon = lax.axis_index("lon")
    plane, member = (lon // 2) % 2, lon // 4 * 2 + lon % 2
    for side in range(2):
        near, far = [final_ref[pl.ds(8 * side + i, members // 2, stride=16), :] for i in (6, 7)]
        for h in range(2):
            innov_ref[pl.ds(2 * h + side, members // 2, stride=4), :] = jnp.where(plane == h, near, far)

    across = member - 1 + 2 * plane
    across = jnp.where(across >= members, 0, across)
    row = jnp.where(lon % 2 == 0, (member + 1) * 8 + 4, across * 8 + 5)
    lane = lax.broadcasted_iota(jnp.int32, (16, 128), 1)
    patch_row = lax.broadcasted_iota(jnp.int32, (16, 128), 0)
    source = (patch_row // 3 * GROUP + patch_row % 3 * 6 + lane % 6) & 127
    halves = [
        jnp.take_along_axis(jnp.broadcast_to(values, (16, 128)), source, axis=1)
        for values in (moved_ref[...], final_ref[pl.ds(row, 1), :])
    ]
    rolled_ref[...] = jnp.where(lane < 6, halves[0], halves[1])[:12, :12]


def finish(final, moved):
    members = final.shape[0] // 8
    shape = jax.ShapeDtypeStruct
    return pl.pallas_call(
        finish_kernel,
        out_shape=[
            shape((2, 8, MODEL), F32),
            shape((2, 8, MODEL), F32),
            shape((2 * members, 128), F32),
            shape((12, 12), F32),
        ],
        name="finish",
    )(final, moved)


def paired(value, axis, odd_first):
    count = lax.axis_size(axis)
    if odd_first:
        pairs = [(i, (i + 1) % count if i % 2 else (i - 1) % count) for i in range(count)]
    else:
        pairs = [(i, i ^ 1) for i in range(count)]
    return lax.ppermute(value, axis, pairs)


def shards(
    tokens,
    query_key_value_weight,
    output_weight,
    adapter_down_map,
    adapter_up_map,
    relative_position_bias,
    readout,
    observation_index,
    observation_weight,
    observation_value,
    observation_count,
):
    lat_count, lon_count = lax.axis_size("lat"), lax.axis_size("lon")
    lat, lon = lax.axis_index("lat"), lax.axis_index("lon")
    even_lat, even_lon = lat % 2 == 0, lon % 2 == 0

    own = (tokens[:, :6], tokens[:, 6:])
    near_send, far_send, observation_index = lax.optimization_barrier(
        (
            jnp.where(even_lon, own[1], own[0]),
            jnp.where(even_lon, own[0], own[1]),
            observation_index,
        )
    )
    far_lon = paired(far_send, "lon", True)

    slots = packed_slots(
        observation_index.reshape(lon_count * 4, 128),
        observation_weight.reshape(lon_count * 4, 128),
        observation_value.reshape(lon_count, 128),
        observation_count.reshape(1, lon_count),
    ).reshape(lon_count, 8, 128)
    near_send, slots = lax.optimization_barrier((near_send, slots))
    near_lon = paired(near_send, "lon", False)

    left = jnp.where(even_lon, far_lon, near_lon)
    right = jnp.where(even_lon, near_lon, far_lon)
    strips = (left, own[0], own[1], right)
    top = jnp.stack([strip[:3] for strip in strips])
    bottom = jnp.stack([strip[9:] for strip in strips])
    near_send, far_send, readout = lax.optimization_barrier(
        (jnp.where(even_lat, bottom, top), jnp.where(even_lat, top, bottom), readout)
    )
    far_send, readout, bias = lax.optimization_barrier(
        (far_send, readout.reshape(1, MODEL), relative_position_bias)
    )
    far_lat = paired(far_send, "lat", True)
    near_lat = paired(near_send, "lat", False)
    slots = lax.all_to_all(slots, "lon", 0, 0, tiled=True).reshape(lon_count * 8, 128)

    down_rows = adapter_down_map.reshape(16, MODEL)
    up_rows = adapter_up_map.reshape(16, MODEL)
    loss_scale = 1.0 / math.sqrt(lat_count * lon_count)
    block_out, adjoint, edge_row, grads, mine, other = core(
        tokens,
        (near_lon, far_lon, far_lat, near_lat),
        query_key_value_weight,
        output_weight,
        down_rows,
        up_rows,
        readout,
        ordered_bias(bias),
        slots,
        loss_scale,
        lat_count,
    )
    members = lon_count // 2
    plane = (lon // 2) % 2
    planes = [[i for i in range(lon_count) if (i // 2) % 2 == h] for h in range(2)]
    columns = [
        [a * lon_count + at * 4 + h * 2 + c for h in range(2) for a in range(lat_count)]
        for at in range(members // 2)
        for c in range(2)
    ]

    chunks = lax.all_to_all(
        grads.reshape(members, 4, 128), "lon", 0, 0, axis_index_groups=planes, tiled=True
    )
    other = lax.ppermute(other, "lon", [(i, i ^ 2) for i in range(lon_count)])

    chunk = jnp.concatenate([jnp.sum(chunks, axis=0), edge_row], axis=0)
    chunk, adjoint = lax.optimization_barrier((chunk, adjoint))
    along = lax.all_to_all(
        jnp.broadcast_to(chunk[None], (2 * lat_count, 5, 128)),
        ("lat", "lon"),
        0,
        0,
        axis_index_groups=columns,
        tiled=True,
    )
    total = jnp.sum(along[:, :4], axis=0)
    edges = along[:, 4]
    below_at = (lat + 1) % lat_count

    def edge_of(h, a):
        return lax.dynamic_index_in_dim(edges, h * lat_count + a, 0, keepdims=False)

    def moved_up(here, below):
        kept = here[: 4 * GROUP].reshape(4, GROUP)[1:]
        return jnp.concatenate([kept.reshape(3 * GROUP), below[:GROUP]])

    below = edge_of(plane, below_at)
    edge = moved_up(adjoint[0], below)
    twin_edge = moved_up(edge_of(1 - plane, lat), edge_of(1 - plane, below_at))
    shared = jnp.concatenate(
        [total, jnp.pad(jnp.stack([edge, twin_edge]), ((0, 0), (0, 128 - 4 * GROUP)))], axis=0
    )
    final = jnp.concatenate(
        [jnp.broadcast_to(shared[None], (members, 6, 128)), mine[:, None], other[:, None]], axis=1
    )
    final = lax.all_to_all(final, "lon", 0, 0, axis_index_groups=planes, tiled=True)

    kept = adjoint[0, 4 * GROUP : OWN]
    moved = jnp.concatenate([kept[GROUP:], below[4 * GROUP : 5 * GROUP], jnp.zeros((GROUP + 8,), F32)])
    up_gradient, down_gradient, innovation, rolled_adjoint = finish(
        final.reshape(members * 8, 128), moved.reshape(1, 128)
    )
    return block_out, innovation[None, None], rolled_adjoint, down_gradient, up_gradient


def solution(mesh):
    return jax.shard_map(
        shards,
        mesh=mesh,
        in_specs=(
            P("lat", "lon", None),
            P(),
            P(),
            P(),
            P(),
            P(),
            P(),
            P("lat", "lon", None, None, None),
            P("lat", "lon", None, None, None),
            P("lat", "lon", None, None),
            P("lat", "lon", None),
        ),
        out_specs=(P("lat", "lon", None), P("lat", "lon", None, None), P("lat", "lon"), P(), P()),
        check_vma=False,
    )
```

```python
import functools
import math

import jax
import jax.numpy as jnp
from jax import lax
from jax.experimental import pallas as pl
from jax.experimental.pallas import tpu as pltpu
from jax.sharding import PartitionSpec as P

F32 = jnp.float32
BF16 = jnp.bfloat16
HEADS = 16
HEAD_DIM = 32
MODEL = 512
GROUP = 24
WINDOW = 4 * GROUP
LIVE = 18
OWN = 8 * GROUP
NORM_EPS = 1e-05
NEG = -1e30
NT = (((1,), (1,)), ((), ()))
TN = (((0,), (0,)), ((), ()))
NN = (((1,), (0,)), ((), ()))


def mm(a, b, dims=NN, precision=None):
    return lax.dot_general(a, b, dims, precision=precision, preferred_element_type=F32)


def exact(a, b, dims=NN):
    return mm(a, b, dims, precision=lax.Precision.HIGHEST)


def bias_kernel(bias_ref, out_hbm, wide_ref, out_ref, sem):
    shape = (72, WINDOW)
    lane = lax.broadcasted_iota(jnp.int32, shape, 1)
    row = lane % GROUP
    column = 12 * (3 * ((lane // GROUP) % 2) + row // 6) + 6 * (lane // (2 * GROUP)) + row % 6
    hit = (column == lax.broadcasted_iota(jnp.int32, shape, 0)) & (row < LIVE)
    wide = exact(bias_ref[...], hit.astype(F32))
    lanes = lax.broadcasted_iota(jnp.int32, (1, WINDOW), 1)
    wide = wide + jnp.where(lanes % GROUP < LIVE, 0.0, NEG)
    wide_ref[...] = wide.reshape(HEADS, 72, WINDOW)
    out_ref[...] = jnp.zeros_like(out_ref)
    for parity in range(2):
        for half in range(2):
            for m in range(3):
                start = 12 * (3 * (1 - parity) + m) + 6 * (1 - half)
                out_ref[parity * 2 + half, :, 6 * m : 6 * m + 6, :] = wide_ref[:, start : start + 6, :]
    store = pltpu.make_async_copy(out_ref, out_hbm.at[pl.ds(0, 4)], sem)
    store.start()
    store.wait()


def ordered_bias(bias):
    return pl.pallas_call(
        bias_kernel,
        out_shape=jax.ShapeDtypeStruct((64, HEADS, GROUP, WINDOW), F32),
        out_specs=pl.BlockSpec(memory_space=pl.ANY),
        scratch_shapes=[
            pltpu.VMEM((HEADS, 72, WINDOW), F32),
            pltpu.VMEM((4, HEADS, GROUP, WINDOW), F32),
            pltpu.SemaphoreType.DMA,
        ],
        compiler_params=pltpu.CompilerParams(vmem_limit_bytes=58 * 1024 * 1024),
        cost_estimate=pl.CostEstimate(flops=2 * 10**10, bytes_accessed=2 * 10**6, transcendentals=0),
        name="ordered_bias",
    )(bias.reshape(HEADS * 72, 72))


def slots_kernel(index_ref, weight_ref, value_ref, count_ref, out_ref):
    strips = value_ref.shape[0]
    square = (strips, strips)
    own_lane = lax.broadcasted_iota(jnp.int32, square, 0) == lax.broadcasted_iota(jnp.int32, square, 1)
    counts = jnp.broadcast_to(count_ref[...].astype(F32), square)
    counts = jnp.sum(jnp.where(own_lane, counts, 0.0), axis=1, keepdims=True).astype(jnp.int32)
    live = lax.broadcasted_iota(jnp.int32, (strips, 128), 1) < counts
    places = []
    for k in range(4):
        cell = index_ref[pl.ds(k, strips, stride=4), :]
        row = (cell * 171) >> 11
        col = cell - 12 * row
        group = (row * 11) >> 5
        half = (col >= 6).astype(jnp.int32)
        places.append((half * 4 + group) * GROUP + (row - 3 * group) * 6 + col - 6 * half)
        weight = weight_ref[pl.ds(k, strips, stride=4), :]
        out_ref[pl.ds(2 + k, strips, stride=8), :] = jnp.where(live, weight, 0.0)
    for pair in range(2):
        packed = places[2 * pair] + 1024 * places[2 * pair + 1]
        out_ref[pl.ds(pair, strips, stride=8), :] = packed.astype(F32)
    out_ref[pl.ds(6, strips, stride=8), :] = jnp.where(live, value_ref[...], 0.0)
    out_ref[pl.ds(7, strips, stride=8), :] = jnp.zeros((strips, 128), F32)


def packed_slots(index, weight, value, count):
    return pl.pallas_call(
        slots_kernel,
        out_shape=jax.ShapeDtypeStruct((value.shape[0] * 8, 128), F32),
        cost_estimate=pl.CostEstimate(flops=10**6, bytes_accessed=5 * 10**5, transcendentals=0),
        name="packed_slots",
    )(index, weight, value, count)


def forward_part(
    bias_load,
    lat_count,
    own_ref,
    near_lon_ref,
    far_lon_ref,
    near_lat_ref,
    far_lat_ref,
    qkv_ref,
    wo_ref,
    down_ref,
    up_ref,
    readout_ref,
    bias_ref,
    block_ref,
    field_ref,
    probs_ref,
    gq_ref,
    low_ref,
    norm_ref,
    own_norm_ref,
    low_own_ref,
    w_ref,
    k_ref,
    v_ref,
    q_ref,
    att_ref,
):
    lat = lax.axis_index("lat")
    even_lon = lax.axis_index("lon") % 2 == 0
    even_lat = lat % 2 == 0
    first = (lat == 0).astype(F32)
    last = (lat == lat_count - 1).astype(F32)

    def pick(cond, a, b):
        return jnp.where(cond, a.astype(F32), b.astype(F32))

    gap = jnp.zeros((GROUP - LIVE, MODEL), F32)

    def piece(strip, group):
        rows = []
        for i in range(3):
            at = 3 * (group - 1) + i
            if group == 0:
                rows.append(pick(even_lat, far_lat_ref[strip, i], near_lat_ref[strip, i]))
            elif group == 5:
                rows.append(pick(even_lat, near_lat_ref[strip, i], far_lat_ref[strip, i]))
            elif strip == 0:
                rows.append(pick(even_lon, far_lon_ref[at], near_lon_ref[at]))
            elif strip == 3:
                rows.append(pick(even_lon, near_lon_ref[at], far_lon_ref[at]))
            else:
                rows.append(own_ref[at].astype(F32)[6 * (strip - 1) : 6 * strip])
        return jnp.concatenate(rows + [gap], axis=0)

    for strip in range(4):
        rows = []
        for pair in range(3):
            x = jnp.concatenate([piece(strip, 2 * pair + i) for i in range(2)], axis=0)
            center = x - jnp.mean(x, axis=1, keepdims=True)
            spread = jnp.mean(center * center, axis=1, keepdims=True)
            y = center * lax.rsqrt(spread + NORM_EPS)
            at = ((strip // 2) * 3 + pair) * WINDOW + (strip % 2) * 2 * GROUP
            norm_ref[at : at + 2 * GROUP, :] = y.astype(BF16)
            rows.append(y)
        if strip in (1, 2):
            mine = jnp.concatenate([rows[0][GROUP:], rows[1], rows[2][:GROUP]], axis=0)
            own_norm_ref[(strip - 1) * 4 * GROUP : strip * 4 * GROUP, :] = mine.astype(BF16)

    normed = norm_ref[...]
    rank_row = lax.broadcasted_iota(jnp.int32, (16, MODEL), 0)
    up_half = 0.5 * up_ref[...].astype(F32)
    up_query = jnp.where(rank_row < 8, up_half, 0.0).astype(BF16)
    up_value = jnp.where(rank_row >= 8, up_half, 0.0).astype(BF16)
    low = mm(normed, down_ref[...], NT).astype(BF16)
    low_ref[...] = low
    k_ref[...] = mm(normed, qkv_ref[:, MODEL : 2 * MODEL]).astype(BF16)
    v_ref[...] = (mm(normed, qkv_ref[:, 2 * MODEL :]) + mm(low, up_value)).astype(BF16)
    normed_own = own_norm_ref[...]
    low_own = mm(normed_own, down_ref[...], NT).astype(BF16)
    low_own_ref[...] = low_own.astype(F32)
    query = mm(normed_own, qkv_ref[:, :MODEL]) + mm(low_own, up_query)
    q_ref[...] = query.astype(BF16).astype(F32)

    readout = jnp.broadcast_to(readout_ref[...].astype(F32), (8, MODEL)).astype(BF16)
    w_row = mm(readout, wo_ref[...], NT)
    w_ref[...] = w_row

    scale = 1.0 / math.sqrt(HEAD_DIM)
    head_of = lax.broadcasted_iota(jnp.int32, (8, 1, 256), 2) // HEAD_DIM
    head_mask = head_of == lax.broadcasted_iota(jnp.int32, (8, 1, 256), 0)
    lane_part = (lax.broadcasted_iota(jnp.int32, (1, WINDOW), 1) // GROUP) % 2
    masked_first = jnp.where(lane_part == 0, NEG * first, 0.0)
    masked_last = jnp.where(lane_part == 1, NEG * last, 0.0)

    ones = jnp.ones((WINDOW, WINDOW), BF16)

    def fold(rows):
        return jnp.sum(jnp.where(head_mask, rows.reshape(8, GROUP, 256), 0.0), axis=0)

    bias_load.wait()
    for n in range(8):
        half, row = n // 4, n % 4
        window = half * 3 + (row + 1) // 2
        keys = slice(window * WINDOW, (window + 1) * WINDOW)
        for part in range(2):
            cols = slice(256 * part, 256 * (part + 1))
            k_win, v_win = k_ref[keys, cols], v_ref[keys, cols]
            q_own = q_ref[n * GROUP : (n + 1) * GROUP, cols]
            lhs = jnp.where(head_mask, q_own[None], 0.0).reshape(8 * GROUP, 256).astype(BF16)
            bias = bias_ref[(row % 2) * 2 + half, 8 * part : 8 * part + 8].reshape(8 * GROUP, WINDOW)
            scores = mm(lhs, k_win, NT) * scale + bias
            if row == 0:
                scores = scores + masked_first
            if row == 3:
                scores = scores + masked_last
            raised = jnp.exp(scores - jnp.max(scores, axis=1, keepdims=True))
            probs = raised * (1.0 / jnp.sum(raised, axis=1, keepdims=True))
            probs_bf = probs.astype(BF16)
            probs_ref[n, 8 * GROUP * part : 8 * GROUP * (part + 1), :] = probs_bf
            att_ref[n * GROUP : (n + 1) * GROUP, cols] = fold(mm(probs_bf, v_win))
            w_masked = jnp.where(head_mask[:, 0, :], w_row[:, cols], 0.0)
            w_high = w_masked.astype(BF16).astype(F32)
            w_pair = jnp.concatenate([w_high, w_masked - w_high], axis=0).astype(BF16)
            v_pair = mm(w_pair, v_win, NT)
            v_w = (v_pair[:8] + v_pair[8:]).reshape(8, 1, WINDOW)
            v_w = jnp.broadcast_to(v_w, (8, GROUP, WINDOW)).reshape(8 * GROUP, WINDOW)
            share = probs * v_w
            share_high = share.astype(BF16)
            share_low = (share - share_high.astype(F32)).astype(BF16)
            mean = jnp.sum(share, axis=1, keepdims=True)
            slope = (probs * (v_w - mean) * scale).astype(BF16)
            gq_ref[n * GROUP : (n + 1) * GROUP, cols] = fold(mm(slope, k_win))

    x_own = jnp.concatenate([piece(1 + n // 4, 1 + n % 4) for n in range(8)], axis=0)
    out = (x_own + mm(att_ref[...].astype(BF16), wo_ref[...])).astype(BF16)
    wide = out.astype(F32)
    for row in range(12):
        starts = [(half * 4 + row // 3) * GROUP + 6 * (row % 3) for half in range(2)]
        pair = jnp.concatenate([wide[start : start + 6] for start in starts], axis=0)
        block_ref[row] = pair.astype(BF16)
    field_ref[...] = jnp.zeros_like(field_ref)
    field_ref[:, :OWN] = mm(readout, out, NT)


def observe_part(
    slots_ref,
    field_ref,
    probs_ref,
    gq_ref,
    low_ref,
    norm_ref,
    own_norm_ref,
    low_own_ref,
    w_ref,
    up_ref,
    adjoint_ref,
    edge_ref,
    grads_ref,
    mine_ref,
    other_ref,
    innov_ref,
    term_ref,
    place_ref,
    loss_scale,
):
    sources = innov_ref.shape[0]
    field_low = jnp.broadcast_to(field_ref[0:1, 0:128], (sources, 128))
    field_high = jnp.broadcast_to(field_ref[0:1, 128:256], (sources, 128))
    places, weights = [], []
    for pair in range(2):
        packed = slots_ref[pl.ds(pair, sources, stride=8), :].astype(jnp.int32)
        places += [packed & 1023, packed >> 10]
    predicted = jnp.zeros((sources, 128), F32)
    for k in range(4):
        lane = places[k] & 127
        picked = jnp.where(
            places[k] < 128,
            jnp.take_along_axis(field_low, lane, axis=1),
            jnp.take_along_axis(field_high, lane, axis=1),
        )
        weights.append(slots_ref[pl.ds(2 + k, sources, stride=8), :])
        predicted = predicted + weights[k] * picked
    innov = predicted - slots_ref[pl.ds(6, sources, stride=8), :]
    innov_ref[...] = innov
    for k in range(4):
        rows = slice(k * sources, (k + 1) * sources)
        term = weights[k] * innov
        high = term.astype(BF16).astype(F32)
        term_ref[0, rows, :] = high
        term_ref[1, rows, :] = term - high
        place_ref[0, rows, :] = places[k] >> 4
        place_ref[1, rows, :] = places[k] & 15

    digit = lax.broadcasted_iota(jnp.int32, (16, 128), 0)
    per_step = 32

    def add_rows(step, total):
        left, right = [], []
        for inner in range(per_step):
            at = pl.ds(step * per_step + inner, 1)
            left.append(jnp.where(digit == place_ref[0, at, :], 1.0, 0.0).astype(BF16))
            hit = digit == place_ref[1, at, :]
            terms = [jnp.where(hit, term_ref[i, at, :], 0.0) for i in range(2)]
            right.append(jnp.concatenate(terms, axis=0).astype(BF16))
        return total + mm(jnp.concatenate(left, axis=1), jnp.concatenate(right, axis=1), NT)

    total = lax.fori_loop(0, 4 * sources // per_step, add_rows, jnp.zeros((16, 32), F32))
    total = total[:, :16] + total[:, 16:]

    def cells(shape, axis):
        cell = lax.broadcasted_iota(jnp.int32, shape, axis)
        digits = lax.broadcasted_iota(jnp.int32, shape, 1 - axis)
        return cell // 16 == digits, cell % 16 == digits

    high, low = cells((OWN, 16), 0)
    column = exact(high.astype(F32), total)
    adjoint = jnp.sum(jnp.where(low, column, 0.0), axis=1, keepdims=True)
    high, low = cells((16, OWN), 1)
    row = jnp.sum(jnp.where(high, exact(total, low.astype(F32)), 0.0), axis=0, keepdims=True)
    adjoint_ref[...] = jnp.concatenate([row, jnp.zeros((1, 256 - OWN), F32)], axis=1)
    edge_ref[...] = row[:, :128]
    low_plane = (lax.axis_index("lon") // 2) % 2 == 0
    for side in range(2):
        by_plane = [innov_ref[pl.ds(2 * h + side, sources // 4, stride=4), :] for h in range(2)]
        place = pl.ds(side, sources // 4, stride=2)
        mine_ref[place, :] = jnp.where(low_plane, by_plane[0], by_plane[1])
        other_ref[place, :] = jnp.where(low_plane, by_plane[1], by_plane[0])

    factor = 0.5 * loss_scale
    g_query = gq_ref[...].astype(BF16)
    up = up_ref[...]
    grad_low = mm(g_query, up, NT)
    up_query = mm((low_own_ref[...] * adjoint).astype(BF16), g_query, TN)
    down_query = mm((grad_low * adjoint).astype(BF16), own_norm_ref[...], TN)

    weighted = [None] * 6
    for n in range(8):
        window = (n // 4) * 3 + (n % 4 + 1) // 2
        probs = probs_ref[n].astype(F32).reshape(HEADS, GROUP, WINDOW)
        part = jnp.sum(probs * adjoint[n * GROUP : (n + 1) * GROUP].reshape(1, GROUP, 1), axis=1)
        weighted[window] = part if weighted[window] is None else weighted[window] + part
    head = lax.broadcasted_iota(jnp.int32, (HEADS, MODEL), 0)
    of_head = head == lax.broadcasted_iota(jnp.int32, (HEADS, MODEL), 1) // HEAD_DIM
    w_masked = jnp.where(of_head, jnp.broadcast_to(w_ref[0:1, :], (HEADS, MODEL)), 0.0)
    rank_head = exact(up.astype(F32), w_masked, NT)
    sums, down_value = jnp.zeros((HEADS, 16), F32), jnp.zeros((16, MODEL), F32)
    for window in range(6):
        keys = slice(window * WINDOW, (window + 1) * WINDOW)
        sums = sums + mm(weighted[window].astype(BF16), low_ref[keys, :])
        of_rank = exact(rank_head, weighted[window])
        down_value = down_value + mm(of_rank.astype(BF16), norm_ref[keys, :])
    up_value = exact(sums, w_masked, TN)

    parts = (up_query[:8], up_value[8:], down_query[:8], down_value[8:])
    for m, part in enumerate(parts):
        part = part * factor
        for q in range(4):
            grads_ref[pl.ds(q * 32 + m, 8, stride=4), :] = part[:, 128 * q : 128 * (q + 1)]


def core_kernel(
    own_ref,
    near_lon_ref,
    far_lon_ref,
    far_lat_ref,
    near_lat_ref,
    qkv_ref,
    wo_ref,
    down_ref,
    up_ref,
    readout_ref,
    bias_hbm,
    slots_ref,
    block_ref,
    adjoint_ref,
    edge_ref,
    grads_ref,
    mine_ref,
    other_ref,
    field_ref,
    probs_ref,
    gq_ref,
    low_ref,
    norm_ref,
    own_norm_ref,
    low_own_ref,
    w_ref,
    k_ref,
    v_ref,
    q_ref,
    att_ref,
    bias_ref,
    bias_sem,
    innov_ref,
    term_ref,
    place_ref,
    loss_scale,
    lat_count,
):
    bias_load = pltpu.make_async_copy(bias_hbm.at[pl.ds(0, 4)], bias_ref, bias_sem)
    bias_load.start()
    forward_part(
        bias_load,
        lat_count,
        own_ref,
        near_lon_ref,
        far_lon_ref,
        near_lat_ref,
        far_lat_ref,
        qkv_ref,
        wo_ref,
        down_ref,
        up_ref,
        readout_ref,
        bias_ref,
        block_ref,
        field_ref,
        probs_ref,
        gq_ref,
        low_ref,
        norm_ref,
        own_norm_ref,
        low_own_ref,
        w_ref,
        k_ref,
        v_ref,
        q_ref,
        att_ref,
    )
    observe_part(
        slots_ref,
        field_ref,
        probs_ref,
        gq_ref,
        low_ref,
        norm_ref,
        own_norm_ref,
        low_own_ref,
        w_ref,
        up_ref,
        adjoint_ref,
        edge_ref,
        grads_ref,
        mine_ref,
        other_ref,
        innov_ref,
        term_ref,
        place_ref,
        loss_scale,
    )


def core(own, halos, qkv, wo, down, up, readout, bias, slots, loss_scale, lat_count):
    sources = slots.shape[0] // 8
    shape = jax.ShapeDtypeStruct
    vmem = pl.BlockSpec(memory_space=pltpu.VMEM)
    return pl.pallas_call(
        functools.partial(core_kernel, loss_scale=loss_scale, lat_count=lat_count),
        in_specs=[vmem] * 10 + [pl.BlockSpec(memory_space=pl.ANY), vmem],
        out_specs=[vmem] * 6,
        out_shape=[
            shape((12, 12, MODEL), BF16),
            shape((1, 256), F32),
            shape((1, 128), F32),
            shape((128, 128), F32),
            shape((sources // 2, 128), F32),
            shape((sources // 2, 128), F32),
        ],
        scratch_shapes=[
            pltpu.VMEM((8, 256), F32),
            pltpu.VMEM((8, HEADS * GROUP, WINDOW), BF16),
            pltpu.VMEM((OWN, MODEL), F32),
            pltpu.VMEM((6 * WINDOW, 16), BF16),
            pltpu.VMEM((6 * WINDOW, MODEL), BF16),
            pltpu.VMEM((OWN, MODEL), BF16),
            pltpu.VMEM((OWN, 16), F32),
            pltpu.VMEM((8, MODEL), F32),
            pltpu.VMEM((6 * WINDOW, MODEL), BF16),
            pltpu.VMEM((6 * WINDOW, MODEL), BF16),
            pltpu.VMEM((OWN, MODEL), F32),
            pltpu.VMEM((OWN, MODEL), F32),
            pltpu.VMEM((4, HEADS, GROUP, WINDOW), F32),
            pltpu.SemaphoreType.DMA,
            pltpu.VMEM((sources, 128), F32),
            pltpu.VMEM((2, 4 * sources, 128), F32),
            pltpu.VMEM((2, 4 * sources, 128), jnp.int32),
        ],
        compiler_params=pltpu.CompilerParams(vmem_limit_bytes=49 * 1024 * 1024),
        cost_estimate=pl.CostEstimate(
            flops=3 * 10**9, bytes_accessed=8 * 10**6, transcendentals=4 * 10**5
        ),
        name="window_and_observe",
    )(own, *halos, qkv, wo, down, up, readout, bias, slots)


def finish_kernel(final_ref, moved_ref, up_ref, down_ref, innov_ref, rolled_ref):
    members = final_ref.shape[0] // 8
    for m, (ref, which) in enumerate(((up_ref, 0), (up_ref, 1), (down_ref, 0), (down_ref, 1))):
        for q in range(4):
            ref[which, :, 128 * q : 128 * (q + 1)] = final_ref[pl.ds(q * 64 + m, 8, stride=8), :]
    lon = lax.axis_index("lon")
    plane, member = (lon // 2) % 2, lon // 4 * 2 + lon % 2
    for side in range(2):
        near, far = [final_ref[pl.ds(8 * side + i, members // 2, stride=16), :] for i in (6, 7)]
        for h in range(2):
            innov_ref[pl.ds(2 * h + side, members // 2, stride=4), :] = jnp.where(plane == h, near, far)

    across = member - 1 + 2 * plane
    across = jnp.where(across >= members, 0, across)
    row = jnp.where(lon % 2 == 0, (member + 1) * 8 + 4, across * 8 + 5)
    lane = lax.broadcasted_iota(jnp.int32, (16, 128), 1)
    patch_row = lax.broadcasted_iota(jnp.int32, (16, 128), 0)
    source = (patch_row // 3 * GROUP + patch_row % 3 * 6 + lane % 6) & 127
    halves = [
        jnp.take_along_axis(jnp.broadcast_to(values, (16, 128)), source, axis=1)
        for values in (moved_ref[...], final_ref[pl.ds(row, 1), :])
    ]
    rolled_ref[...] = jnp.where(lane < 6, halves[0], halves[1])[:12, :12]


def finish(final, moved):
    members = final.shape[0] // 8
    shape = jax.ShapeDtypeStruct
    return pl.pallas_call(
        finish_kernel,
        out_shape=[
            shape((2, 8, MODEL), F32),
            shape((2, 8, MODEL), F32),
            shape((2 * members, 128), F32),
            shape((12, 12), F32),
        ],
        compiler_params=pltpu.CompilerParams(vmem_limit_bytes=4 * 1024 * 1024),
        cost_estimate=pl.CostEstimate(flops=10**4, bytes_accessed=10**5, transcendentals=0),
        name="finish",
    )(final, moved)


def paired(value, axis, odd_first):
    count = lax.axis_size(axis)
    if odd_first:
        pairs = [(i, (i + 1) % count if i % 2 else (i - 1) % count) for i in range(count)]
    else:
        pairs = [(i, i ^ 1) for i in range(count)]
    return lax.ppermute(value, axis, pairs)


def shards(
    tokens,
    query_key_value_weight,
    output_weight,
    adapter_down_map,
    adapter_up_map,
    relative_position_bias,
    readout,
    observation_index,
    observation_weight,
    observation_value,
    observation_count,
):
    lat_count, lon_count = lax.axis_size("lat"), lax.axis_size("lon")
    lat, lon = lax.axis_index("lat"), lax.axis_index("lon")
    even_lat, even_lon = lat % 2 == 0, lon % 2 == 0

    own = (tokens[:, :6], tokens[:, 6:])
    far_send, observation_index, own_later = lax.optimization_barrier(
        (jnp.where(even_lon, own[0], own[1]), observation_index, tokens)
    )
    near_send = jnp.where(even_lon, own_later[:, 6:], own_later[:, :6])
    far_lon = paired(far_send, "lon", True)

    slots = packed_slots(
        observation_index.reshape(lon_count * 4, 128),
        observation_weight.reshape(lon_count * 4, 128),
        observation_value.reshape(lon_count, 128),
        observation_count.reshape(1, lon_count),
    ).reshape(lon_count, 8, 128)
    near_send, slots = lax.optimization_barrier((near_send, slots))
    near_lon = paired(near_send, "lon", False)

    left = jnp.where(even_lon, far_lon, near_lon)
    right = jnp.where(even_lon, near_lon, far_lon)
    strips = (left, own[0], own[1], right)
    top = jnp.stack([strip[:3] for strip in strips])
    bottom = jnp.stack([strip[9:] for strip in strips])
    near_send, far_send, readout = lax.optimization_barrier(
        (jnp.where(even_lat, bottom, top), jnp.where(even_lat, top, bottom), readout)
    )
    far_send, readout, bias = lax.optimization_barrier(
        (far_send, readout.reshape(1, MODEL), relative_position_bias)
    )
    far_lat = paired(far_send, "lat", True)
    near_lat = paired(near_send, "lat", False)
    slots = lax.all_to_all(slots, "lon", 0, 0, tiled=True).reshape(lon_count * 8, 128)

    down_rows = adapter_down_map.reshape(16, MODEL)
    up_rows = adapter_up_map.reshape(16, MODEL)
    loss_scale = 1.0 / math.sqrt(lat_count * lon_count)
    block_out, adjoint, edge_row, grads, mine, other = core(
        tokens,
        (near_lon, far_lon, far_lat, near_lat),
        query_key_value_weight,
        output_weight,
        down_rows,
        up_rows,
        readout,
        ordered_bias(bias),
        slots,
        loss_scale,
        lat_count,
    )
    members = lon_count // 2
    plane = (lon // 2) % 2
    planes = [[i for i in range(lon_count) if (i // 2) % 2 == h] for h in range(2)]
    columns = [
        [a * lon_count + at * 4 + h * 2 + c for h in range(2) for a in range(lat_count)]
        for at in range(members // 2)
        for c in range(2)
    ]

    chunks = lax.all_to_all(
        grads.reshape(members, 4, 128), "lon", 0, 0, axis_index_groups=planes, tiled=True
    )
    other = lax.ppermute(other, "lon", [(i, i ^ 2) for i in range(lon_count)])

    chunk = jnp.concatenate([jnp.sum(chunks, axis=0), edge_row], axis=0)
    chunk, adjoint = lax.optimization_barrier((chunk, adjoint))
    along = lax.all_to_all(
        jnp.broadcast_to(chunk[None], (2 * lat_count, 5, 128)),
        ("lat", "lon"),
        0,
        0,
        axis_index_groups=columns,
        tiled=True,
    )
    total = jnp.sum(along[:, :4], axis=0)
    edges = along[:, 4]
    below_at = (lat + 1) % lat_count

    def edge_of(h, a):
        return lax.dynamic_index_in_dim(edges, h * lat_count + a, 0, keepdims=False)

    def moved_up(here, below):
        kept = here[: 4 * GROUP].reshape(4, GROUP)[1:]
        return jnp.concatenate([kept.reshape(3 * GROUP), below[:GROUP]])

    below = edge_of(plane, below_at)
    edge = moved_up(adjoint[0], below)
    twin_edge = moved_up(edge_of(1 - plane, lat), edge_of(1 - plane, below_at))
    shared = jnp.concatenate(
        [total, jnp.pad(jnp.stack([edge, twin_edge]), ((0, 0), (0, 128 - 4 * GROUP)))], axis=0
    )
    final = jnp.concatenate(
        [jnp.broadcast_to(shared[None], (members, 6, 128)), mine[:, None], other[:, None]], axis=1
    )
    final = lax.all_to_all(final, "lon", 0, 0, axis_index_groups=planes, tiled=True)

    kept = adjoint[0, 4 * GROUP : OWN]
    moved = jnp.concatenate([kept[GROUP:], below[4 * GROUP : 5 * GROUP], jnp.zeros((GROUP + 8,), F32)])
    up_gradient, down_gradient, innovation, rolled_adjoint = finish(
        final.reshape(members * 8, 128), moved.reshape(1, 128)
    )
    return block_out, innovation[None, None], rolled_adjoint, down_gradient, up_gradient


def solution(mesh):
    return jax.shard_map(
        shards,
        mesh=mesh,
        in_specs=(
            P("lat", "lon", None),
            P(),
            P(),
            P(),
            P(),
            P(),
            P(),
            P("lat", "lon", None, None, None),
            P("lat", "lon", None, None, None),
            P("lat", "lon", None, None),
            P("lat", "lon", None),
        ),
        out_specs=(P("lat", "lon", None), P("lat", "lon", None, None), P("lat", "lon"), P(), P()),
        check_vma=False,
    )
```

```python
import functools
import math

import jax
import jax.numpy as jnp
from jax import lax
from jax.experimental import pallas as pl
from jax.experimental.pallas import tpu as pltpu
from jax.sharding import PartitionSpec as P

F32 = jnp.float32
BF16 = jnp.bfloat16
HEADS = 16
HEAD_DIM = 32
MODEL = 512
GROUP = 24
WINDOW = 4 * GROUP
LIVE = 18
OWN = 8 * GROUP
NORM_EPS = 1e-05
NEG = -1e30
NT = (((1,), (1,)), ((), ()))
TN = (((0,), (0,)), ((), ()))
NN = (((1,), (0,)), ((), ()))


def mm(a, b, dims=NN, precision=None):
    return lax.dot_general(a, b, dims, precision=precision, preferred_element_type=F32)


def exact(a, b, dims=NN):
    return mm(a, b, dims, precision=lax.Precision.HIGHEST)


def bias_kernel(bias_ref, out_hbm, wide_ref, out_ref, sem):
    shape = (72, WINDOW)
    lane = lax.broadcasted_iota(jnp.int32, shape, 1)
    row = lane % GROUP
    column = 12 * (3 * ((lane // GROUP) % 2) + row // 6) + 6 * (lane // (2 * GROUP)) + row % 6
    hit = (column == lax.broadcasted_iota(jnp.int32, shape, 0)) & (row < LIVE)
    wide = exact(bias_ref[...], hit.astype(F32))
    lanes = lax.broadcasted_iota(jnp.int32, (1, WINDOW), 1)
    wide = wide + jnp.where(lanes % GROUP < LIVE, 0.0, NEG)
    wide_ref[...] = wide.reshape(HEADS, 72, WINDOW)
    out_ref[...] = jnp.zeros_like(out_ref)
    for parity in range(2):
        for half in range(2):
            for m in range(3):
                start = 12 * (3 * (1 - parity) + m) + 6 * (1 - half)
                out_ref[parity * 2 + half, :, 6 * m : 6 * m + 6, :] = wide_ref[:, start : start + 6, :]
    store = pltpu.make_async_copy(out_ref, out_hbm.at[pl.ds(0, 4)], sem)
    store.start()
    store.wait()


def ordered_bias(bias):
    return pl.pallas_call(
        bias_kernel,
        out_shape=jax.ShapeDtypeStruct((64, HEADS, GROUP, WINDOW), F32),
        out_specs=pl.BlockSpec(memory_space=pl.ANY),
        scratch_shapes=[
            pltpu.VMEM((HEADS, 72, WINDOW), F32),
            pltpu.VMEM((4, HEADS, GROUP, WINDOW), F32),
            pltpu.SemaphoreType.DMA,
        ],
        compiler_params=pltpu.CompilerParams(vmem_limit_bytes=58 * 1024 * 1024),
        cost_estimate=pl.CostEstimate(flops=2 * 10**10, bytes_accessed=2 * 10**6, transcendentals=0),
        name="ordered_bias",
    )(bias.reshape(HEADS * 72, 72))


def slots_kernel(index_ref, weight_ref, value_ref, count_ref, out_ref):
    strips = value_ref.shape[0]
    square = (strips, strips)
    own_lane = lax.broadcasted_iota(jnp.int32, square, 0) == lax.broadcasted_iota(jnp.int32, square, 1)
    counts = jnp.broadcast_to(count_ref[...].astype(F32), square)
    counts = jnp.sum(jnp.where(own_lane, counts, 0.0), axis=1, keepdims=True).astype(jnp.int32)
    live = lax.broadcasted_iota(jnp.int32, (strips, 128), 1) < counts
    places = []
    for k in range(4):
        cell = index_ref[pl.ds(k, strips, stride=4), :]
        row = (cell * 171) >> 11
        col = cell - 12 * row
        group = (row * 11) >> 5
        half = (col >= 6).astype(jnp.int32)
        places.append((half * 4 + group) * GROUP + (row - 3 * group) * 6 + col - 6 * half)
        weight = weight_ref[pl.ds(k, strips, stride=4), :]
        out_ref[pl.ds(2 + k, strips, stride=8), :] = jnp.where(live, weight, 0.0)
    for pair in range(2):
        packed = places[2 * pair] + 1024 * places[2 * pair + 1]
        out_ref[pl.ds(pair, strips, stride=8), :] = packed.astype(F32)
    out_ref[pl.ds(6, strips, stride=8), :] = jnp.where(live, value_ref[...], 0.0)
    out_ref[pl.ds(7, strips, stride=8), :] = jnp.zeros((strips, 128), F32)


def packed_slots(index, weight, value, count):
    return pl.pallas_call(
        slots_kernel,
        out_shape=jax.ShapeDtypeStruct((value.shape[0] * 8, 128), F32),
        cost_estimate=pl.CostEstimate(flops=10**6, bytes_accessed=5 * 10**5, transcendentals=0),
        name="packed_slots",
    )(index, weight, value, count)


def forward_part(
    bias_load,
    lat_count,
    own_ref,
    near_lon_ref,
    far_lon_ref,
    near_lat_ref,
    far_lat_ref,
    qkv_ref,
    wo_ref,
    down_ref,
    up_ref,
    readout_ref,
    bias_ref,
    block_ref,
    field_ref,
    probs_ref,
    gq_ref,
    low_ref,
    norm_ref,
    own_norm_ref,
    low_own_ref,
    w_ref,
    k_ref,
    v_ref,
    q_ref,
    att_ref,
):
    lat = lax.axis_index("lat")
    even_lon = lax.axis_index("lon") % 2 == 0
    even_lat = lat % 2 == 0
    first = (lat == 0).astype(F32)
    last = (lat == lat_count - 1).astype(F32)

    def pick(cond, a, b):
        return jnp.where(cond, a.astype(F32), b.astype(F32))

    gap = jnp.zeros((GROUP - LIVE, MODEL), F32)

    def piece(strip, group):
        rows = []
        for i in range(3):
            at = 3 * (group - 1) + i
            if group == 0:
                rows.append(pick(even_lat, far_lat_ref[strip, i], near_lat_ref[strip, i]))
            elif group == 5:
                rows.append(pick(even_lat, near_lat_ref[strip, i], far_lat_ref[strip, i]))
            elif strip == 0:
                rows.append(pick(even_lon, far_lon_ref[at], near_lon_ref[at]))
            elif strip == 3:
                rows.append(pick(even_lon, near_lon_ref[at], far_lon_ref[at]))
            else:
                rows.append(own_ref[at].astype(F32)[6 * (strip - 1) : 6 * strip])
        return jnp.concatenate(rows + [gap], axis=0)

    for strip in range(4):
        rows = []
        for pair in range(3):
            x = jnp.concatenate([piece(strip, 2 * pair + i) for i in range(2)], axis=0)
            center = x - jnp.mean(x, axis=1, keepdims=True)
            spread = jnp.mean(center * center, axis=1, keepdims=True)
            y = center * lax.rsqrt(spread + NORM_EPS)
            at = ((strip // 2) * 3 + pair) * WINDOW + (strip % 2) * 2 * GROUP
            norm_ref[at : at + 2 * GROUP, :] = y.astype(BF16)
            rows.append(y)
        if strip in (1, 2):
            mine = jnp.concatenate([rows[0][GROUP:], rows[1], rows[2][:GROUP]], axis=0)
            own_norm_ref[(strip - 1) * 4 * GROUP : strip * 4 * GROUP, :] = mine.astype(BF16)

    normed = norm_ref[...]
    rank_row = lax.broadcasted_iota(jnp.int32, (16, MODEL), 0)
    up_half = 0.5 * up_ref[...].astype(F32)
    up_query = jnp.where(rank_row < 8, up_half, 0.0).astype(BF16)
    up_value = jnp.where(rank_row >= 8, up_half, 0.0).astype(BF16)
    low = mm(normed, down_ref[...], NT).astype(BF16)
    low_ref[...] = low
    k_ref[...] = mm(normed, qkv_ref[:, MODEL : 2 * MODEL]).astype(BF16)
    v_ref[...] = (mm(normed, qkv_ref[:, 2 * MODEL :]) + mm(low, up_value)).astype(BF16)
    normed_own = own_norm_ref[...]
    low_own = mm(normed_own, down_ref[...], NT).astype(BF16)
    low_own_ref[...] = low_own.astype(F32)
    query = mm(normed_own, qkv_ref[:, :MODEL]) + mm(low_own, up_query)
    q_ref[...] = query.astype(BF16).astype(F32)

    readout = jnp.broadcast_to(readout_ref[...].astype(F32), (8, MODEL)).astype(BF16)
    w_row = mm(readout, wo_ref[...], NT)
    w_ref[...] = w_row

    scale = 1.0 / math.sqrt(HEAD_DIM)
    head_of = lax.broadcasted_iota(jnp.int32, (8, 1, 256), 2) // HEAD_DIM
    head_mask = head_of == lax.broadcasted_iota(jnp.int32, (8, 1, 256), 0)
    lane_part = (lax.broadcasted_iota(jnp.int32, (1, WINDOW), 1) // GROUP) % 2
    masked_first = jnp.where(lane_part == 0, NEG * first, 0.0)
    masked_last = jnp.where(lane_part == 1, NEG * last, 0.0)

    def fold(rows, size):
        return jnp.sum(jnp.where(head_mask, rows.reshape(8, size, 256), 0.0), axis=0)

    bias_load.wait()
    for window in range(6):
        half, window_row = window // 3, window % 3
        groups = ((0,), (1, 2), (3,))[window_row]
        size = GROUP * len(groups)
        own_rows = slice((4 * half + groups[0]) * GROUP, (4 * half + groups[0]) * GROUP + size)
        keys = slice(window * WINDOW, (window + 1) * WINDOW)
        for part in range(2):
            cols = slice(256 * part, 256 * (part + 1))
            k_win, v_win = k_ref[keys, cols], v_ref[keys, cols]
            lhs = jnp.where(head_mask, q_ref[own_rows, cols][None], 0.0)
            lhs = lhs.reshape(8 * size, 256).astype(BF16)
            bias = [bias_ref[(g % 2) * 2 + half, 8 * part : 8 * part + 8] for g in groups]
            bias = jnp.concatenate(bias, axis=1).reshape(8 * size, WINDOW)
            scores = mm(lhs, k_win, NT) * scale + bias
            if window_row == 0:
                scores = scores + masked_first
            if window_row == 2:
                scores = scores + masked_last
            raised = jnp.exp(scores - jnp.max(scores, axis=1, keepdims=True))
            probs = raised * (1.0 / jnp.sum(raised, axis=1, keepdims=True))
            probs3 = probs.reshape(8, size, WINDOW)
            for i, g in enumerate(groups):
                of_group = probs3[:, GROUP * i : GROUP * (i + 1)].reshape(8 * GROUP, WINDOW)
                rows = slice(8 * GROUP * part, 8 * GROUP * (part + 1))
                probs_ref[4 * half + g, rows, :] = of_group.astype(BF16)
            att_ref[own_rows, cols] = fold(mm(probs.astype(BF16), v_win), size)
            w_masked = jnp.where(head_mask[:, 0, :], w_row[:, cols], 0.0)
            w_high = w_masked.astype(BF16).astype(F32)
            w_pair = jnp.concatenate([w_high, w_masked - w_high], axis=0).astype(BF16)
            v_pair = mm(w_pair, v_win, NT)
            v_w = (v_pair[:8] + v_pair[8:]).reshape(8, 1, WINDOW)
            mean = jnp.sum(probs3 * v_w, axis=2, keepdims=True)
            slope = (probs3 * (v_w - mean) * scale).reshape(8 * size, WINDOW).astype(BF16)
            gq_ref[own_rows, cols] = fold(mm(slope, k_win), size)

    x_own = jnp.concatenate([piece(1 + n // 4, 1 + n % 4) for n in range(8)], axis=0)
    out = (x_own + mm(att_ref[...].astype(BF16), wo_ref[...])).astype(BF16)
    wide = out.astype(F32)
    for row in range(12):
        starts = [(half * 4 + row // 3) * GROUP + 6 * (row % 3) for half in range(2)]
        pair = jnp.concatenate([wide[start : start + 6] for start in starts], axis=0)
        block_ref[row] = pair.astype(BF16)
    field_ref[...] = jnp.zeros_like(field_ref)
    field_ref[:, :OWN] = mm(readout, out, NT)


def observe_part(
    slots_ref,
    field_ref,
    probs_ref,
    gq_ref,
    low_ref,
    norm_ref,
    own_norm_ref,
    low_own_ref,
    w_ref,
    up_ref,
    adjoint_ref,
    edge_ref,
    grads_ref,
    mine_ref,
    other_ref,
    innov_ref,
    term_ref,
    place_ref,
    loss_scale,
):
    sources = innov_ref.shape[0]
    field_low = jnp.broadcast_to(field_ref[0:1, 0:128], (sources, 128))
    field_high = jnp.broadcast_to(field_ref[0:1, 128:256], (sources, 128))
    places, weights = [], []
    for pair in range(2):
        packed = slots_ref[pl.ds(pair, sources, stride=8), :].astype(jnp.int32)
        places += [packed & 1023, packed >> 10]
    predicted = jnp.zeros((sources, 128), F32)
    for k in range(4):
        lane = places[k] & 127
        picked = jnp.where(
            places[k] < 128,
            jnp.take_along_axis(field_low, lane, axis=1),
            jnp.take_along_axis(field_high, lane, axis=1),
        )
        weights.append(slots_ref[pl.ds(2 + k, sources, stride=8), :])
        predicted = predicted + weights[k] * picked
    innov = predicted - slots_ref[pl.ds(6, sources, stride=8), :]
    innov_ref[...] = innov
    for k in range(4):
        rows = slice(k * sources, (k + 1) * sources)
        term = weights[k] * innov
        high = term.astype(BF16).astype(F32)
        term_ref[0, rows, :] = high
        term_ref[1, rows, :] = term - high
        place_ref[0, rows, :] = places[k] >> 4
        place_ref[1, rows, :] = places[k] & 15

    digit = lax.broadcasted_iota(jnp.int32, (16, 128), 0)
    per_step = 128

    def add_rows(step, total):
        left, right = [], []
        for inner in range(per_step):
            at = pl.ds(step * per_step + inner, 1)
            left.append(jnp.where(digit == place_ref[0, at, :], 1.0, 0.0).astype(BF16))
            hit = digit == place_ref[1, at, :]
            terms = [jnp.where(hit, term_ref[i, at, :], 0.0) for i in range(2)]
            right.append(jnp.concatenate(terms, axis=0).astype(BF16))
        return total + mm(jnp.concatenate(left, axis=1), jnp.concatenate(right, axis=1), NT)

    total = lax.fori_loop(0, 4 * sources // per_step, add_rows, jnp.zeros((16, 32), F32))
    total = total[:, :16] + total[:, 16:]

    def cells(shape, axis):
        cell = lax.broadcasted_iota(jnp.int32, shape, axis)
        digits = lax.broadcasted_iota(jnp.int32, shape, 1 - axis)
        return cell // 16 == digits, cell % 16 == digits

    high, low = cells((OWN, 16), 0)
    column = exact(high.astype(F32), total)
    adjoint = jnp.sum(jnp.where(low, column, 0.0), axis=1, keepdims=True)
    high, low = cells((16, OWN), 1)
    row = jnp.sum(jnp.where(high, exact(total, low.astype(F32)), 0.0), axis=0, keepdims=True)
    adjoint_ref[...] = jnp.concatenate([row, jnp.zeros((1, 256 - OWN), F32)], axis=1)
    edge_ref[...] = row[:, :128]
    low_plane = (lax.axis_index("lon") // 2) % 2 == 0
    for side in range(2):
        by_plane = [innov_ref[pl.ds(2 * h + side, sources // 4, stride=4), :] for h in range(2)]
        place = pl.ds(side, sources // 4, stride=2)
        mine_ref[place, :] = jnp.where(low_plane, by_plane[0], by_plane[1])
        other_ref[place, :] = jnp.where(low_plane, by_plane[1], by_plane[0])

    factor = 0.5 * loss_scale
    g_query = gq_ref[...].astype(BF16)
    up = up_ref[...]
    grad_low = mm(g_query, up, NT)
    up_query = mm((low_own_ref[...] * adjoint).astype(BF16), g_query, TN)
    down_query = mm((grad_low * adjoint).astype(BF16), own_norm_ref[...], TN)

    weighted = [None] * 6
    for n in range(8):
        window = (n // 4) * 3 + (n % 4 + 1) // 2
        probs = probs_ref[n].astype(F32).reshape(HEADS, GROUP, WINDOW)
        part = jnp.sum(probs * adjoint[n * GROUP : (n + 1) * GROUP].reshape(1, GROUP, 1), axis=1)
        weighted[window] = part if weighted[window] is None else weighted[window] + part
    head = lax.broadcasted_iota(jnp.int32, (HEADS, MODEL), 0)
    of_head = head == lax.broadcasted_iota(jnp.int32, (HEADS, MODEL), 1) // HEAD_DIM
    w_masked = jnp.where(of_head, jnp.broadcast_to(w_ref[0:1, :], (HEADS, MODEL)), 0.0)
    rank_head = exact(up.astype(F32), w_masked, NT)
    sums, down_value = jnp.zeros((HEADS, 16), F32), jnp.zeros((16, MODEL), F32)
    for window in range(6):
        keys = slice(window * WINDOW, (window + 1) * WINDOW)
        sums = sums + mm(weighted[window].astype(BF16), low_ref[keys, :])
        of_rank = exact(rank_head, weighted[window])
        down_value = down_value + mm(of_rank.astype(BF16), norm_ref[keys, :])
    up_value = exact(sums, w_masked, TN)

    parts = (up_query[:8], up_value[8:], down_query[:8], down_value[8:])
    for m, part in enumerate(parts):
        part = part * factor
        for q in range(4):
            grads_ref[pl.ds(q * 32 + m, 8, stride=4), :] = part[:, 128 * q : 128 * (q + 1)]


def core_kernel(
    own_ref,
    near_lon_ref,
    far_lon_ref,
    far_lat_ref,
    near_lat_ref,
    qkv_ref,
    wo_ref,
    down_ref,
    up_ref,
    readout_ref,
    bias_hbm,
    slots_ref,
    block_ref,
    adjoint_ref,
    edge_ref,
    grads_ref,
    mine_ref,
    other_ref,
    field_ref,
    probs_ref,
    gq_ref,
    low_ref,
    norm_ref,
    own_norm_ref,
    low_own_ref,
    w_ref,
    k_ref,
    v_ref,
    q_ref,
    att_ref,
    bias_ref,
    bias_sem,
    innov_ref,
    term_ref,
    place_ref,
    loss_scale,
    lat_count,
):
    bias_load = pltpu.make_async_copy(bias_hbm.at[pl.ds(0, 4)], bias_ref, bias_sem)
    bias_load.start()
    forward_part(
        bias_load,
        lat_count,
        own_ref,
        near_lon_ref,
        far_lon_ref,
        near_lat_ref,
        far_lat_ref,
        qkv_ref,
        wo_ref,
        down_ref,
        up_ref,
        readout_ref,
        bias_ref,
        block_ref,
        field_ref,
        probs_ref,
        gq_ref,
        low_ref,
        norm_ref,
        own_norm_ref,
        low_own_ref,
        w_ref,
        k_ref,
        v_ref,
        q_ref,
        att_ref,
    )
    observe_part(
        slots_ref,
        field_ref,
        probs_ref,
        gq_ref,
        low_ref,
        norm_ref,
        own_norm_ref,
        low_own_ref,
        w_ref,
        up_ref,
        adjoint_ref,
        edge_ref,
        grads_ref,
        mine_ref,
        other_ref,
        innov_ref,
        term_ref,
        place_ref,
        loss_scale,
    )


def core(own, halos, qkv, wo, down, up, readout, bias, slots, loss_scale, lat_count):
    sources = slots.shape[0] // 8
    shape = jax.ShapeDtypeStruct
    vmem = pl.BlockSpec(memory_space=pltpu.VMEM)
    return pl.pallas_call(
        functools.partial(core_kernel, loss_scale=loss_scale, lat_count=lat_count),
        in_specs=[vmem] * 10 + [pl.BlockSpec(memory_space=pl.ANY), vmem],
        out_specs=[vmem] * 6,
        out_shape=[
            shape((12, 12, MODEL), BF16),
            shape((1, 256), F32),
            shape((1, 128), F32),
            shape((128, 128), F32),
            shape((sources // 2, 128), F32),
            shape((sources // 2, 128), F32),
        ],
        scratch_shapes=[
            pltpu.VMEM((8, 256), F32),
            pltpu.VMEM((8, HEADS * GROUP, WINDOW), BF16),
            pltpu.VMEM((OWN, MODEL), F32),
            pltpu.VMEM((6 * WINDOW, 16), BF16),
            pltpu.VMEM((6 * WINDOW, MODEL), BF16),
            pltpu.VMEM((OWN, MODEL), BF16),
            pltpu.VMEM((OWN, 16), F32),
            pltpu.VMEM((8, MODEL), F32),
            pltpu.VMEM((6 * WINDOW, MODEL), BF16),
            pltpu.VMEM((6 * WINDOW, MODEL), BF16),
            pltpu.VMEM((OWN, MODEL), F32),
            pltpu.VMEM((OWN, MODEL), F32),
            pltpu.VMEM((4, HEADS, GROUP, WINDOW), F32),
            pltpu.SemaphoreType.DMA,
            pltpu.VMEM((sources, 128), F32),
            pltpu.VMEM((2, 4 * sources, 128), F32),
            pltpu.VMEM((2, 4 * sources, 128), jnp.int32),
        ],
        compiler_params=pltpu.CompilerParams(vmem_limit_bytes=49 * 1024 * 1024),
        cost_estimate=pl.CostEstimate(
            flops=3 * 10**9, bytes_accessed=8 * 10**6, transcendentals=4 * 10**5
        ),
        name="window_and_observe",
    )(own, *halos, qkv, wo, down, up, readout, bias, slots)


def finish_kernel(final_ref, moved_ref, up_ref, down_ref, innov_ref, rolled_ref):
    members = final_ref.shape[0] // 8
    for m, (ref, which) in enumerate(((up_ref, 0), (up_ref, 1), (down_ref, 0), (down_ref, 1))):
        for q in range(4):
            ref[which, :, 128 * q : 128 * (q + 1)] = final_ref[pl.ds(q * 64 + m, 8, stride=8), :]
    lon = lax.axis_index("lon")
    plane, member = (lon // 2) % 2, lon // 4 * 2 + lon % 2
    for side in range(2):
        near, far = [final_ref[pl.ds(8 * side + i, members // 2, stride=16), :] for i in (6, 7)]
        for h in range(2):
            innov_ref[pl.ds(2 * h + side, members // 2, stride=4), :] = jnp.where(plane == h, near, far)

    across = member - 1 + 2 * plane
    across = jnp.where(across >= members, 0, across)
    row = jnp.where(lon % 2 == 0, (member + 1) * 8 + 4, across * 8 + 5)
    lane = lax.broadcasted_iota(jnp.int32, (16, 128), 1)
    patch_row = lax.broadcasted_iota(jnp.int32, (16, 128), 0)
    source = (patch_row // 3 * GROUP + patch_row % 3 * 6 + lane % 6) & 127
    halves = [
        jnp.take_along_axis(jnp.broadcast_to(values, (16, 128)), source, axis=1)
        for values in (moved_ref[...], final_ref[pl.ds(row, 1), :])
    ]
    rolled_ref[...] = jnp.where(lane < 6, halves[0], halves[1])[:12, :12]


def finish(final, moved):
    members = final.shape[0] // 8
    shape = jax.ShapeDtypeStruct
    return pl.pallas_call(
        finish_kernel,
        out_shape=[
            shape((2, 8, MODEL), F32),
            shape((2, 8, MODEL), F32),
            shape((2 * members, 128), F32),
            shape((12, 12), F32),
        ],
        compiler_params=pltpu.CompilerParams(vmem_limit_bytes=4 * 1024 * 1024),
        cost_estimate=pl.CostEstimate(flops=10**4, bytes_accessed=10**5, transcendentals=0),
        name="finish",
    )(final, moved)


def paired(value, axis, odd_first):
    count = lax.axis_size(axis)
    if odd_first:
        pairs = [(i, (i + 1) % count if i % 2 else (i - 1) % count) for i in range(count)]
    else:
        pairs = [(i, i ^ 1) for i in range(count)]
    return lax.ppermute(value, axis, pairs)


def shards(
    tokens,
    query_key_value_weight,
    output_weight,
    adapter_down_map,
    adapter_up_map,
    relative_position_bias,
    readout,
    observation_index,
    observation_weight,
    observation_value,
    observation_count,
):
    lat_count, lon_count = lax.axis_size("lat"), lax.axis_size("lon")
    lat, lon = lax.axis_index("lat"), lax.axis_index("lon")
    even_lat, even_lon = lat % 2 == 0, lon % 2 == 0

    own = (tokens[:, :6], tokens[:, 6:])
    far_send, observation_index, own_later = lax.optimization_barrier(
        (jnp.where(even_lon, own[0], own[1]), observation_index, tokens)
    )
    near_send = jnp.where(even_lon, own_later[:, 6:], own_later[:, :6])
    far_lon = paired(far_send, "lon", True)

    slots = packed_slots(
        observation_index.reshape(lon_count * 4, 128),
        observation_weight.reshape(lon_count * 4, 128),
        observation_value.reshape(lon_count, 128),
        observation_count.reshape(1, lon_count),
    ).reshape(lon_count, 8, 128)
    near_send, slots = lax.optimization_barrier((near_send, slots))
    near_lon = paired(near_send, "lon", False)

    left = jnp.where(even_lon, far_lon, near_lon)
    right = jnp.where(even_lon, near_lon, far_lon)
    strips = (left, own[0], own[1], right)
    top = jnp.stack([strip[:3] for strip in strips])
    bottom = jnp.stack([strip[9:] for strip in strips])
    near_send, top, bottom, bias, readout = lax.optimization_barrier(
        (jnp.where(even_lat, bottom, top), top, bottom, relative_position_bias, readout)
    )
    readout = readout.reshape(1, MODEL)
    far_lat = paired(jnp.where(even_lat, top, bottom), "lat", True)
    near_lat = paired(near_send, "lat", False)
    slots = lax.all_to_all(slots, "lon", 0, 0, tiled=True).reshape(lon_count * 8, 128)

    down_rows = adapter_down_map.reshape(16, MODEL)
    up_rows = adapter_up_map.reshape(16, MODEL)
    loss_scale = 1.0 / math.sqrt(lat_count * lon_count)
    block_out, adjoint, edge_row, grads, mine, other = core(
        tokens,
        (near_lon, far_lon, far_lat, near_lat),
        query_key_value_weight,
        output_weight,
        down_rows,
        up_rows,
        readout,
        ordered_bias(bias),
        slots,
        loss_scale,
        lat_count,
    )
    members = lon_count // 2
    plane = (lon // 2) % 2
    planes = [[i for i in range(lon_count) if (i // 2) % 2 == h] for h in range(2)]
    columns = [
        [a * lon_count + at * 4 + h * 2 + c for h in range(2) for a in range(lat_count)]
        for at in range(members // 2)
        for c in range(2)
    ]

    chunks = lax.all_to_all(
        grads.reshape(members, 4, 128), "lon", 0, 0, axis_index_groups=planes, tiled=True
    )
    other = lax.ppermute(other, "lon", [(i, i ^ 2) for i in range(lon_count)])

    chunk = jnp.concatenate([jnp.sum(chunks, axis=0), edge_row], axis=0)
    chunk, adjoint = lax.optimization_barrier((chunk, adjoint))
    along = lax.all_to_all(
        jnp.broadcast_to(chunk[None], (2 * lat_count, 5, 128)),
        ("lat", "lon"),
        0,
        0,
        axis_index_groups=columns,
        tiled=True,
    )
    total = jnp.sum(along[:, :4], axis=0)
    edges = along[:, 4]
    below_at = (lat + 1) % lat_count

    def edge_of(h, a):
        return lax.dynamic_index_in_dim(edges, h * lat_count + a, 0, keepdims=False)

    def moved_up(here, below):
        kept = here[: 4 * GROUP].reshape(4, GROUP)[1:]
        return jnp.concatenate([kept.reshape(3 * GROUP), below[:GROUP]])

    below = edge_of(plane, below_at)
    edge = moved_up(adjoint[0], below)
    twin_edge = moved_up(edge_of(1 - plane, lat), edge_of(1 - plane, below_at))
    shared = jnp.concatenate(
        [total, jnp.pad(jnp.stack([edge, twin_edge]), ((0, 0), (0, 128 - 4 * GROUP)))], axis=0
    )
    final = jnp.concatenate(
        [jnp.broadcast_to(shared[None], (members, 6, 128)), mine[:, None], other[:, None]], axis=1
    )
    final = lax.all_to_all(final, "lon", 0, 0, axis_index_groups=planes, tiled=True)

    kept = adjoint[0, 4 * GROUP : OWN]
    moved = jnp.concatenate([kept[GROUP:], below[4 * GROUP : 5 * GROUP], jnp.zeros((GROUP + 8,), F32)])
    up_gradient, down_gradient, innovation, rolled_adjoint = finish(
        final.reshape(members * 8, 128), moved.reshape(1, 128)
    )
    return block_out, innovation[None, None], rolled_adjoint, down_gradient, up_gradient


def solution(mesh):
    return jax.shard_map(
        shards,
        mesh=mesh,
        in_specs=(
            P("lat", "lon", None),
            P(),
            P(),
            P(),
            P(),
            P(),
            P(),
            P("lat", "lon", None, None, None),
            P("lat", "lon", None, None, None),
            P("lat", "lon", None, None),
            P("lat", "lon", None),
        ),
        out_specs=(P("lat", "lon", None), P("lat", "lon", None, None), P("lat", "lon"), P(), P()),
        check_vma=False,
    )
```

```python
import functools
import math

import jax
import jax.numpy as jnp
from jax import lax
from jax.experimental import pallas as pl
from jax.experimental.pallas import tpu as pltpu
from jax.sharding import PartitionSpec as P

F32 = jnp.float32
BF16 = jnp.bfloat16
HEADS = 16
HEAD_DIM = 32
MODEL = 512
GROUP = 24
WINDOW = 4 * GROUP
LIVE = 18
OWN = 8 * GROUP
NORM_EPS = 1e-05
NEG = -1e30
NT = (((1,), (1,)), ((), ()))
TN = (((0,), (0,)), ((), ()))
NN = (((1,), (0,)), ((), ()))


def mm(a, b, dims=NN, precision=None):
    return lax.dot_general(a, b, dims, precision=precision, preferred_element_type=F32)


def parts_of(x, count):
    parts = []
    for _ in range(count):
        parts.append(x.astype(BF16))
        x = x - parts[-1].astype(F32)
    return parts


def exact(a, b, dims=NN):
    return mm(a, b, dims, precision=lax.Precision.HIGHEST)


def bias_kernel(bias_ref, out_hbm, wide_ref, out_ref, sem):
    shape = (72, WINDOW)
    lane = lax.broadcasted_iota(jnp.int32, shape, 1)
    row = lane % GROUP
    column = 12 * (3 * ((lane // GROUP) % 2) + row // 6) + 6 * (lane // (2 * GROUP)) + row % 6
    hit = (column == lax.broadcasted_iota(jnp.int32, shape, 0)) & (row < LIVE)
    wide = exact(bias_ref[...], hit.astype(F32))
    lanes = lax.broadcasted_iota(jnp.int32, (1, WINDOW), 1)
    wide = wide + jnp.where(lanes % GROUP < LIVE, 0.0, NEG)
    wide_ref[...] = wide.reshape(HEADS, 72, WINDOW)
    out_ref[...] = jnp.zeros_like(out_ref)
    for parity in range(2):
        for half in range(2):
            for m in range(3):
                start = 12 * (3 * (1 - parity) + m) + 6 * (1 - half)
                out_ref[parity * 2 + half, :, 6 * m : 6 * m + 6, :] = wide_ref[:, start : start + 6, :]
    store = pltpu.make_async_copy(out_ref, out_hbm.at[pl.ds(0, 4)], sem)
    store.start()
    store.wait()


def ordered_bias(bias):
    return pl.pallas_call(
        bias_kernel,
        out_shape=jax.ShapeDtypeStruct((64, HEADS, GROUP, WINDOW), F32),
        out_specs=pl.BlockSpec(memory_space=pl.ANY),
        scratch_shapes=[
            pltpu.VMEM((HEADS, 72, WINDOW), F32),
            pltpu.VMEM((4, HEADS, GROUP, WINDOW), F32),
            pltpu.SemaphoreType.DMA,
        ],
        compiler_params=pltpu.CompilerParams(vmem_limit_bytes=58 * 1024 * 1024),
        cost_estimate=pl.CostEstimate(flops=2 * 10**10, bytes_accessed=2 * 10**6, transcendentals=0),
        name="ordered_bias",
    )(bias.reshape(HEADS * 72, 72))


def slots_kernel(index_ref, weight_ref, value_ref, count_ref, tokens_ref, out_ref, near_ref):
    even = lax.axis_index("lon") % 2 == 0
    for row in range(tokens_ref.shape[0]):
        x = tokens_ref[row].astype(F32)
        near_ref[row] = jnp.where(even, x[6:], x[:6]).astype(BF16)
    strips = value_ref.shape[0]
    square = (strips, strips)
    own_lane = lax.broadcasted_iota(jnp.int32, square, 0) == lax.broadcasted_iota(jnp.int32, square, 1)
    counts = jnp.broadcast_to(count_ref[...].astype(F32), square)
    counts = jnp.sum(jnp.where(own_lane, counts, 0.0), axis=1, keepdims=True).astype(jnp.int32)
    live = lax.broadcasted_iota(jnp.int32, (strips, 128), 1) < counts
    places = []
    for k in range(4):
        cell = index_ref[pl.ds(k, strips, stride=4), :]
        row = (cell * 171) >> 11
        col = cell - 12 * row
        group = (row * 11) >> 5
        half = (col >= 6).astype(jnp.int32)
        places.append((half * 4 + group) * GROUP + (row - 3 * group) * 6 + col - 6 * half)
        weight = weight_ref[pl.ds(k, strips, stride=4), :]
        out_ref[pl.ds(2 + k, strips, stride=8), :] = jnp.where(live, weight, 0.0)
    for pair in range(2):
        packed = places[2 * pair] + 1024 * places[2 * pair + 1]
        out_ref[pl.ds(pair, strips, stride=8), :] = packed.astype(F32)
    out_ref[pl.ds(6, strips, stride=8), :] = jnp.where(live, value_ref[...], 0.0)
    out_ref[pl.ds(7, strips, stride=8), :] = jnp.zeros((strips, 128), F32)


def packed_slots(index, weight, value, count, tokens):
    return pl.pallas_call(
        slots_kernel,
        out_shape=[
            jax.ShapeDtypeStruct((value.shape[0] * 8, 128), F32),
            jax.ShapeDtypeStruct((12, 6, MODEL), BF16),
        ],
        cost_estimate=pl.CostEstimate(flops=10**6, bytes_accessed=5 * 10**5, transcendentals=0),
        name="packed_slots",
    )(index, weight, value, count, tokens)


def forward_part(
    bias_load,
    lat_count,
    own_ref,
    near_lon_ref,
    far_lon_ref,
    near_lat_ref,
    far_lat_ref,
    qkv_ref,
    wo_ref,
    down_ref,
    up_ref,
    readout_ref,
    bias_ref,
    block_ref,
    field_ref,
    probs_ref,
    gq_ref,
    low_ref,
    norm_ref,
    own_norm_ref,
    low_own_ref,
    w_ref,
    k_ref,
    v_ref,
    q_ref,
    att_ref,
):
    lat = lax.axis_index("lat")
    even_lon = lax.axis_index("lon") % 2 == 0
    even_lat = lat % 2 == 0
    first = (lat == 0).astype(F32)
    last = (lat == lat_count - 1).astype(F32)

    def pick(cond, a, b):
        return jnp.where(cond, a.astype(F32), b.astype(F32))

    gap = jnp.zeros((GROUP - LIVE, MODEL), F32)

    def piece(strip, group):
        rows = []
        for i in range(3):
            at = 3 * (group - 1) + i
            if group == 0:
                rows.append(pick(even_lat, far_lat_ref[strip, i], near_lat_ref[strip, i]))
            elif group == 5:
                rows.append(pick(even_lat, near_lat_ref[strip, i], far_lat_ref[strip, i]))
            elif strip == 0:
                rows.append(pick(even_lon, far_lon_ref[at], near_lon_ref[at]))
            elif strip == 3:
                rows.append(pick(even_lon, near_lon_ref[at], far_lon_ref[at]))
            else:
                rows.append(own_ref[at].astype(F32)[6 * (strip - 1) : 6 * strip])
        return jnp.concatenate(rows + [gap], axis=0)

    for strip in range(4):
        rows = []
        for pair in range(3):
            x = jnp.concatenate([piece(strip, 2 * pair + i) for i in range(2)], axis=0)
            center = x - jnp.mean(x, axis=1, keepdims=True)
            spread = jnp.mean(center * center, axis=1, keepdims=True)
            y = center * lax.rsqrt(spread + NORM_EPS)
            at = ((strip // 2) * 3 + pair) * WINDOW + (strip % 2) * 2 * GROUP
            norm_ref[at : at + 2 * GROUP, :] = y.astype(BF16)
            rows.append(y)
        if strip in (1, 2):
            mine = jnp.concatenate([rows[0][GROUP:], rows[1], rows[2][:GROUP]], axis=0)
            own_norm_ref[(strip - 1) * 4 * GROUP : strip * 4 * GROUP, :] = mine.astype(BF16)

    normed = norm_ref[...]
    rank_row = lax.broadcasted_iota(jnp.int32, (16, MODEL), 0)
    up_half = 0.5 * up_ref[...].astype(F32)
    up_query = jnp.where(rank_row < 8, up_half, 0.0).astype(BF16)
    up_value = jnp.where(rank_row >= 8, up_half, 0.0).astype(BF16)
    low = mm(normed, down_ref[...], NT).astype(BF16)
    low_ref[...] = low
    k_ref[...] = mm(normed, qkv_ref[:, MODEL : 2 * MODEL]).astype(BF16)
    v_ref[...] = (mm(normed, qkv_ref[:, 2 * MODEL :]) + mm(low, up_value)).astype(BF16)
    normed_own = own_norm_ref[...]
    low_own = mm(normed_own, down_ref[...], NT).astype(BF16)
    low_own_ref[...] = low_own.astype(F32)
    query = mm(normed_own, qkv_ref[:, :MODEL]) + mm(low_own, up_query)
    q_ref[...] = query.astype(BF16).astype(F32)

    readout = jnp.broadcast_to(readout_ref[...].astype(F32), (8, MODEL)).astype(BF16)
    w_row = mm(readout, wo_ref[...], NT)
    w_ref[...] = w_row

    scale = 1.0 / math.sqrt(HEAD_DIM)
    head_of = lax.broadcasted_iota(jnp.int32, (8, 1, 256), 2) // HEAD_DIM
    head_mask = head_of == lax.broadcasted_iota(jnp.int32, (8, 1, 256), 0)
    lane_part = (lax.broadcasted_iota(jnp.int32, (1, WINDOW), 1) // GROUP) % 2
    masked_first = jnp.where(lane_part == 0, NEG * first, 0.0)
    masked_last = jnp.where(lane_part == 1, NEG * last, 0.0)

    def fold(rows, size):
        return jnp.sum(jnp.where(head_mask, rows.reshape(8, size, 256), 0.0), axis=0)

    bias_load.wait()
    for window in range(6):
        half, window_row = window // 3, window % 3
        groups = ((0,), (1, 2), (3,))[window_row]
        size = GROUP * len(groups)
        own_rows = slice((4 * half + groups[0]) * GROUP, (4 * half + groups[0]) * GROUP + size)
        keys = slice(window * WINDOW, (window + 1) * WINDOW)
        for part in range(2):
            cols = slice(256 * part, 256 * (part + 1))
            k_win, v_win = k_ref[keys, cols], v_ref[keys, cols]
            lhs = jnp.where(head_mask, q_ref[own_rows, cols][None], 0.0)
            lhs = lhs.reshape(8 * size, 256).astype(BF16)
            bias = [bias_ref[(g % 2) * 2 + half, 8 * part : 8 * part + 8] for g in groups]
            bias = jnp.concatenate(bias, axis=1).reshape(8 * size, WINDOW)
            scores = mm(lhs, k_win, NT) * scale + bias
            if window_row == 0:
                scores = scores + masked_first
            if window_row == 2:
                scores = scores + masked_last
            raised = jnp.exp(scores - jnp.max(scores, axis=1, keepdims=True))
            probs = raised * (1.0 / jnp.sum(raised, axis=1, keepdims=True))
            probs3 = probs.reshape(8, size, WINDOW)
            for i, g in enumerate(groups):
                of_group = probs3[:, GROUP * i : GROUP * (i + 1)].reshape(8 * GROUP, WINDOW)
                rows = slice(8 * GROUP * part, 8 * GROUP * (part + 1))
                probs_ref[4 * half + g, rows, :] = of_group.astype(BF16)
            att_ref[own_rows, cols] = fold(mm(probs.astype(BF16), v_win), size)
            w_masked = jnp.where(head_mask[:, 0, :], w_row[:, cols], 0.0)
            w_high = w_masked.astype(BF16).astype(F32)
            w_pair = jnp.concatenate([w_high, w_masked - w_high], axis=0).astype(BF16)
            v_pair = mm(w_pair, v_win, NT)
            v_w = (v_pair[:8] + v_pair[8:]).reshape(8, 1, WINDOW)
            mean = jnp.sum(probs3 * v_w, axis=2, keepdims=True)
            slope = (probs3 * (v_w - mean) * scale).reshape(8 * size, WINDOW).astype(BF16)
            gq_ref[own_rows, cols] = fold(mm(slope, k_win), size)

    x_own = jnp.concatenate([piece(1 + n // 4, 1 + n % 4) for n in range(8)], axis=0)
    out = (x_own + mm(att_ref[...].astype(BF16), wo_ref[...])).astype(BF16)
    wide = out.astype(F32)
    for row in range(12):
        starts = [(half * 4 + row // 3) * GROUP + 6 * (row % 3) for half in range(2)]
        pair = jnp.concatenate([wide[start : start + 6] for start in starts], axis=0)
        block_ref[row] = pair.astype(BF16)
    field_ref[...] = jnp.zeros_like(field_ref)
    field_ref[:, :OWN] = mm(readout, out, NT)


def observe_part(
    slots_ref,
    field_ref,
    probs_ref,
    gq_ref,
    low_ref,
    norm_ref,
    own_norm_ref,
    low_own_ref,
    w_ref,
    up_ref,
    adjoint_ref,
    edge_ref,
    grads_ref,
    mine_ref,
    other_ref,
    innov_ref,
    term_ref,
    place_ref,
    loss_scale,
):
    sources = innov_ref.shape[0]
    field_low = jnp.broadcast_to(field_ref[0:1, 0:128], (sources, 128))
    field_high = jnp.broadcast_to(field_ref[0:1, 128:256], (sources, 128))
    places, weights = [], []
    for pair in range(2):
        packed = slots_ref[pl.ds(pair, sources, stride=8), :].astype(jnp.int32)
        places += [packed & 1023, packed >> 10]
    predicted = jnp.zeros((sources, 128), F32)
    for k in range(4):
        lane = places[k] & 127
        picked = jnp.where(
            places[k] < 128,
            jnp.take_along_axis(field_low, lane, axis=1),
            jnp.take_along_axis(field_high, lane, axis=1),
        )
        weights.append(slots_ref[pl.ds(2 + k, sources, stride=8), :])
        predicted = predicted + weights[k] * picked
    innov = predicted - slots_ref[pl.ds(6, sources, stride=8), :]
    innov_ref[...] = innov
    for k in range(4):
        rows = slice(k * sources, (k + 1) * sources)
        term = weights[k] * innov
        high = term.astype(BF16).astype(F32)
        term_ref[0, rows, :] = high
        term_ref[1, rows, :] = term - high
        place_ref[0, rows, :] = places[k] >> 4
        place_ref[1, rows, :] = places[k] & 15

    digit = lax.broadcasted_iota(jnp.int32, (16, 128), 0)
    per_step = 128

    def add_rows(step, total):
        left, right = [], []
        for inner in range(per_step):
            at = pl.ds(step * per_step + inner, 1)
            left.append(jnp.where(digit == place_ref[0, at, :], 1.0, 0.0).astype(BF16))
            hit = digit == place_ref[1, at, :]
            terms = [jnp.where(hit, term_ref[i, at, :], 0.0) for i in range(2)]
            right.append(jnp.concatenate(terms, axis=0).astype(BF16))
        return total + mm(jnp.concatenate(left, axis=1), jnp.concatenate(right, axis=1), NT)

    total = lax.fori_loop(0, 4 * sources // per_step, add_rows, jnp.zeros((16, 32), F32))
    total = total[:, :16] + total[:, 16:]

    def cells(shape, axis):
        cell = lax.broadcasted_iota(jnp.int32, shape, axis)
        digits = lax.broadcasted_iota(jnp.int32, shape, 1 - axis)
        return cell // 16 == digits, cell % 16 == digits

    total = jnp.concatenate([part.astype(F32) for part in parts_of(total, 3)], axis=0).astype(BF16)
    cell = lax.broadcasted_iota(jnp.int32, (OWN, 48), 0)
    high = cell // 16 == lax.broadcasted_iota(jnp.int32, (OWN, 48), 1) % 16
    column = mm(jnp.where(high, 1.0, 0.0).astype(BF16), total)
    low = cells((OWN, 16), 0)[1]
    adjoint = jnp.sum(jnp.where(low, column, 0.0), axis=1, keepdims=True)
    high, low = cells((16, OWN), 1)
    row = mm(total, jnp.where(low, 1.0, 0.0).astype(BF16))
    row = jnp.where(high, row[:16] + row[16:32] + row[32:], 0.0)
    row = jnp.sum(row, axis=0, keepdims=True)
    adjoint_ref[...] = jnp.concatenate([row, jnp.zeros((1, 256 - OWN), F32)], axis=1)
    edge_ref[...] = row[:, :128]
    low_plane = (lax.axis_index("lon") // 2) % 2 == 0
    for side in range(2):
        by_plane = [innov_ref[pl.ds(2 * h + side, sources // 4, stride=4), :] for h in range(2)]
        place = pl.ds(side, sources // 4, stride=2)
        mine_ref[place, :] = jnp.where(low_plane, by_plane[0], by_plane[1])
        other_ref[place, :] = jnp.where(low_plane, by_plane[1], by_plane[0])

    factor = 0.5 * loss_scale
    g_query = gq_ref[...].astype(BF16)
    up = up_ref[...]
    grad_low = mm(g_query, up, NT)
    up_query = mm((low_own_ref[...] * adjoint).astype(BF16), g_query, TN)
    down_query = mm((grad_low * adjoint).astype(BF16), own_norm_ref[...], TN)

    weighted = [None] * 6
    for n in range(8):
        window = (n // 4) * 3 + (n % 4 + 1) // 2
        probs = probs_ref[n].astype(F32).reshape(HEADS, GROUP, WINDOW)
        part = jnp.sum(probs * adjoint[n * GROUP : (n + 1) * GROUP].reshape(1, GROUP, 1), axis=1)
        weighted[window] = part if weighted[window] is None else weighted[window] + part
    head = lax.broadcasted_iota(jnp.int32, (HEADS, MODEL), 0)
    of_head = head == lax.broadcasted_iota(jnp.int32, (HEADS, MODEL), 1) // HEAD_DIM
    w_masked = jnp.where(of_head, jnp.broadcast_to(w_ref[0:1, :], (HEADS, MODEL)), 0.0)
    w_high, w_low = [part.astype(F32) for part in parts_of(w_masked, 2)]
    rank_head = mm(up, w_high.astype(BF16), NT) + mm(up, w_low.astype(BF16), NT)
    rank_head = [part.astype(F32) for part in parts_of(rank_head, 2)]
    rank_head = jnp.concatenate(rank_head, axis=0).astype(BF16)
    sums, down_value = jnp.zeros((HEADS, 16), F32), jnp.zeros((16, MODEL), F32)
    for window in range(6):
        keys = slice(window * WINDOW, (window + 1) * WINDOW)
        sums = sums + mm(weighted[window].astype(BF16), low_ref[keys, :])
        of_rank = sum(mm(rank_head, part) for part in parts_of(weighted[window], 2))
        of_rank = (of_rank[:HEADS] + of_rank[HEADS:]).astype(BF16)
        down_value = down_value + mm(of_rank, norm_ref[keys, :])
    high, low = [part.astype(F32) for part in parts_of(sums, 2)]
    up_value = mm(
        jnp.concatenate([high, high, low], axis=0).astype(BF16),
        jnp.concatenate([w_high, w_low, w_high], axis=0).astype(BF16),
        TN,
    )

    parts = (up_query[:8], up_value[8:], down_query[:8], down_value[8:])
    for m, part in enumerate(parts):
        part = part * factor
        for q in range(4):
            grads_ref[pl.ds(q * 32 + m, 8, stride=4), :] = part[:, 128 * q : 128 * (q + 1)]


def core_kernel(
    own_ref,
    near_lon_ref,
    far_lon_ref,
    far_lat_ref,
    near_lat_ref,
    qkv_ref,
    wo_ref,
    down_ref,
    up_ref,
    readout_ref,
    bias_hbm,
    slots_ref,
    block_ref,
    adjoint_ref,
    edge_ref,
    grads_ref,
    mine_ref,
    other_ref,
    field_ref,
    probs_ref,
    gq_ref,
    low_ref,
    norm_ref,
    own_norm_ref,
    low_own_ref,
    w_ref,
    k_ref,
    v_ref,
    q_ref,
    att_ref,
    bias_ref,
    bias_sem,
    innov_ref,
    term_ref,
    place_ref,
    loss_scale,
    lat_count,
):
    bias_load = pltpu.make_async_copy(bias_hbm.at[pl.ds(0, 4)], bias_ref, bias_sem)
    bias_load.start()
    forward_part(
        bias_load,
        lat_count,
        own_ref,
        near_lon_ref,
        far_lon_ref,
        near_lat_ref,
        far_lat_ref,
        qkv_ref,
        wo_ref,
        down_ref,
        up_ref,
        readout_ref,
        bias_ref,
        block_ref,
        field_ref,
        probs_ref,
        gq_ref,
        low_ref,
        norm_ref,
        own_norm_ref,
        low_own_ref,
        w_ref,
        k_ref,
        v_ref,
        q_ref,
        att_ref,
    )
    observe_part(
        slots_ref,
        field_ref,
        probs_ref,
        gq_ref,
        low_ref,
        norm_ref,
        own_norm_ref,
        low_own_ref,
        w_ref,
        up_ref,
        adjoint_ref,
        edge_ref,
        grads_ref,
        mine_ref,
        other_ref,
        innov_ref,
        term_ref,
        place_ref,
        loss_scale,
    )


def core(own, halos, qkv, wo, down, up, readout, bias, slots, loss_scale, lat_count):
    sources = slots.shape[0] // 8
    shape = jax.ShapeDtypeStruct
    vmem = pl.BlockSpec(memory_space=pltpu.VMEM)
    return pl.pallas_call(
        functools.partial(core_kernel, loss_scale=loss_scale, lat_count=lat_count),
        in_specs=[vmem] * 10 + [pl.BlockSpec(memory_space=pl.ANY), vmem],
        out_specs=[vmem] * 6,
        out_shape=[
            shape((12, 12, MODEL), BF16),
            shape((1, 256), F32),
            shape((1, 128), F32),
            shape((128, 128), F32),
            shape((sources // 2, 128), F32),
            shape((sources // 2, 128), F32),
        ],
        scratch_shapes=[
            pltpu.VMEM((8, 256), F32),
            pltpu.VMEM((8, HEADS * GROUP, WINDOW), BF16),
            pltpu.VMEM((OWN, MODEL), F32),
            pltpu.VMEM((6 * WINDOW, 16), BF16),
            pltpu.VMEM((6 * WINDOW, MODEL), BF16),
            pltpu.VMEM((OWN, MODEL), BF16),
            pltpu.VMEM((OWN, 16), F32),
            pltpu.VMEM((8, MODEL), F32),
            pltpu.VMEM((6 * WINDOW, MODEL), BF16),
            pltpu.VMEM((6 * WINDOW, MODEL), BF16),
            pltpu.VMEM((OWN, MODEL), F32),
            pltpu.VMEM((OWN, MODEL), F32),
            pltpu.VMEM((4, HEADS, GROUP, WINDOW), F32),
            pltpu.SemaphoreType.DMA,
            pltpu.VMEM((sources, 128), F32),
            pltpu.VMEM((2, 4 * sources, 128), F32),
            pltpu.VMEM((2, 4 * sources, 128), jnp.int32),
        ],
        compiler_params=pltpu.CompilerParams(vmem_limit_bytes=49 * 1024 * 1024),
        cost_estimate=pl.CostEstimate(
            flops=3 * 10**9, bytes_accessed=8 * 10**6, transcendentals=4 * 10**5
        ),
        name="window_and_observe",
    )(own, *halos, qkv, wo, down, up, readout, bias, slots)


def finish_kernel(final_ref, moved_ref, up_ref, down_ref, innov_ref, rolled_ref):
    members = final_ref.shape[0] // 8
    for m, (ref, which) in enumerate(((up_ref, 0), (up_ref, 1), (down_ref, 0), (down_ref, 1))):
        for q in range(4):
            ref[which, :, 128 * q : 128 * (q + 1)] = final_ref[pl.ds(q * 64 + m, 8, stride=8), :]
    lon = lax.axis_index("lon")
    plane, member = (lon // 2) % 2, lon // 4 * 2 + lon % 2
    for side in range(2):
        near, far = [final_ref[pl.ds(8 * side + i, members // 2, stride=16), :] for i in (6, 7)]
        for h in range(2):
            innov_ref[pl.ds(2 * h + side, members // 2, stride=4), :] = jnp.where(plane == h, near, far)

    across = member - 1 + 2 * plane
    across = jnp.where(across >= members, 0, across)
    row = jnp.where(lon % 2 == 0, (member + 1) * 8 + 4, across * 8 + 5)
    lane = lax.broadcasted_iota(jnp.int32, (16, 128), 1)
    patch_row = lax.broadcasted_iota(jnp.int32, (16, 128), 0)
    source = (patch_row // 3 * GROUP + patch_row % 3 * 6 + lane % 6) & 127
    halves = [
        jnp.take_along_axis(jnp.broadcast_to(values, (16, 128)), source, axis=1)
        for values in (moved_ref[...], final_ref[pl.ds(row, 1), :])
    ]
    rolled_ref[...] = jnp.where(lane < 6, halves[0], halves[1])[:12, :12]


def finish(final, moved):
    members = final.shape[0] // 8
    shape = jax.ShapeDtypeStruct
    return pl.pallas_call(
        finish_kernel,
        out_shape=[
            shape((2, 8, MODEL), F32),
            shape((2, 8, MODEL), F32),
            shape((2 * members, 128), F32),
            shape((12, 12), F32),
        ],
        compiler_params=pltpu.CompilerParams(vmem_limit_bytes=4 * 1024 * 1024),
        cost_estimate=pl.CostEstimate(flops=10**4, bytes_accessed=10**5, transcendentals=0),
        name="finish",
    )(final, moved)


def paired(value, axis, odd_first):
    count = lax.axis_size(axis)
    if odd_first:
        pairs = [(i, (i + 1) % count if i % 2 else (i - 1) % count) for i in range(count)]
    else:
        pairs = [(i, i ^ 1) for i in range(count)]
    return lax.ppermute(value, axis, pairs)


def shards(
    tokens,
    query_key_value_weight,
    output_weight,
    adapter_down_map,
    adapter_up_map,
    relative_position_bias,
    readout,
    observation_index,
    observation_weight,
    observation_value,
    observation_count,
):
    lat_count, lon_count = lax.axis_size("lat"), lax.axis_size("lon")
    lat, lon = lax.axis_index("lat"), lax.axis_index("lon")
    even_lat, even_lon = lat % 2 == 0, lon % 2 == 0

    own = (tokens[:, :6], tokens[:, 6:])
    far_send, observation_index = lax.optimization_barrier(
        (jnp.where(even_lon, own[0], own[1]), observation_index)
    )
    far_lon = paired(far_send, "lon", True)

    slots, near_send = packed_slots(
        observation_index.reshape(lon_count * 4, 128),
        observation_weight.reshape(lon_count * 4, 128),
        observation_value.reshape(lon_count, 128),
        observation_count.reshape(1, lon_count),
        tokens,
    )
    slots = slots.reshape(lon_count, 8, 128)
    near_lon = paired(near_send, "lon", False)

    left = jnp.where(even_lon, far_lon, near_lon)
    right = jnp.where(even_lon, near_lon, far_lon)
    strips = (left, own[0], own[1], right)
    top = jnp.stack([strip[:3] for strip in strips])
    bottom = jnp.stack([strip[9:] for strip in strips])
    near_send, top, bottom, bias, readout = lax.optimization_barrier(
        (jnp.where(even_lat, bottom, top), top, bottom, relative_position_bias, readout)
    )
    readout = readout.reshape(1, MODEL)
    far_lat = paired(jnp.where(even_lat, top, bottom), "lat", True)
    near_lat = paired(near_send, "lat", False)
    slots = lax.all_to_all(slots, "lon", 0, 0, tiled=True).reshape(lon_count * 8, 128)

    down_rows = adapter_down_map.reshape(16, MODEL)
    up_rows = adapter_up_map.reshape(16, MODEL)
    loss_scale = 1.0 / math.sqrt(lat_count * lon_count)
    block_out, adjoint, edge_row, grads, mine, other = core(
        tokens,
        (near_lon, far_lon, far_lat, near_lat),
        query_key_value_weight,
        output_weight,
        down_rows,
        up_rows,
        readout,
        ordered_bias(bias),
        slots,
        loss_scale,
        lat_count,
    )
    members = lon_count // 2
    plane = (lon // 2) % 2
    planes = [[i for i in range(lon_count) if (i // 2) % 2 == h] for h in range(2)]
    columns = [
        [a * lon_count + at * 4 + h * 2 + c for h in range(2) for a in range(lat_count)]
        for at in range(members // 2)
        for c in range(2)
    ]

    chunks = lax.all_to_all(
        grads.reshape(members, 4, 128), "lon", 0, 0, axis_index_groups=planes, tiled=True
    )
    other = lax.ppermute(other, "lon", [(i, i ^ 2) for i in range(lon_count)])

    chunk = jnp.concatenate([jnp.sum(chunks, axis=0), edge_row], axis=0)
    chunk, adjoint = lax.optimization_barrier((chunk, adjoint))
    along = lax.all_to_all(
        jnp.broadcast_to(chunk[None], (2 * lat_count, 5, 128)),
        ("lat", "lon"),
        0,
        0,
        axis_index_groups=columns,
        tiled=True,
    )
    total = jnp.sum(along[:, :4], axis=0)
    edges = along[:, 4]
    below_at = (lat + 1) % lat_count

    def edge_of(h, a):
        return lax.dynamic_index_in_dim(edges, h * lat_count + a, 0, keepdims=False)

    def moved_up(here, below):
        kept = here[: 4 * GROUP].reshape(4, GROUP)[1:]
        return jnp.concatenate([kept.reshape(3 * GROUP), below[:GROUP]])

    below = edge_of(plane, below_at)
    edge = moved_up(adjoint[0], below)
    twin_edge = moved_up(edge_of(1 - plane, lat), edge_of(1 - plane, below_at))
    shared = jnp.concatenate(
        [total, jnp.pad(jnp.stack([edge, twin_edge]), ((0, 0), (0, 128 - 4 * GROUP)))], axis=0
    )
    final = jnp.concatenate(
        [jnp.broadcast_to(shared[None], (members, 6, 128)), mine[:, None], other[:, None]], axis=1
    )
    final = lax.all_to_all(final, "lon", 0, 0, axis_index_groups=planes, tiled=True)

    kept = adjoint[0, 4 * GROUP : OWN]
    moved = jnp.concatenate([kept[GROUP:], below[4 * GROUP : 5 * GROUP], jnp.zeros((GROUP + 8,), F32)])
    up_gradient, down_gradient, innovation, rolled_adjoint = finish(
        final.reshape(members * 8, 128), moved.reshape(1, 128)
    )
    return block_out, innovation[None, None], rolled_adjoint, down_gradient, up_gradient


def solution(mesh):
    return jax.shard_map(
        shards,
        mesh=mesh,
        in_specs=(
            P("lat", "lon", None),
            P(),
            P(),
            P(),
            P(),
            P(),
            P(),
            P("lat", "lon", None, None, None),
            P("lat", "lon", None, None, None),
            P("lat", "lon", None, None),
            P("lat", "lon", None),
        ),
        out_specs=(P("lat", "lon", None), P("lat", "lon", None, None), P("lat", "lon"), P(), P()),
        check_vma=False,
    )
```

```python
import functools
import math

import jax
import jax.numpy as jnp
from jax import lax
from jax.experimental import pallas as pl
from jax.experimental.pallas import tpu as pltpu
from jax.sharding import PartitionSpec as P

F32 = jnp.float32
BF16 = jnp.bfloat16
HEADS = 16
HEAD_DIM = 32
MODEL = 512
GROUP = 24
WINDOW = 4 * GROUP
LIVE = 18
OWN = 8 * GROUP
NORM_EPS = 1e-05
NEG = -1e30
NT = (((1,), (1,)), ((), ()))
TN = (((0,), (0,)), ((), ()))
NN = (((1,), (0,)), ((), ()))


def mm(a, b, dims=NN, precision=None):
    return lax.dot_general(a, b, dims, precision=precision, preferred_element_type=F32)


def parts_of(x, count):
    parts = []
    for _ in range(count):
        parts.append(x.astype(BF16))
        x = x - parts[-1].astype(F32)
    return parts


def exact(a, b, dims=NN):
    return mm(a, b, dims, precision=lax.Precision.HIGHEST)


def bias_kernel(bias_ref, out_hbm, wide_ref, out_ref, sem):
    shape = (72, WINDOW)
    lane = lax.broadcasted_iota(jnp.int32, shape, 1)
    row = lane % GROUP
    column = 12 * (3 * ((lane // GROUP) % 2) + row // 6) + 6 * (lane // (2 * GROUP)) + row % 6
    hit = (column == lax.broadcasted_iota(jnp.int32, shape, 0)) & (row < LIVE)
    wide = exact(bias_ref[...], hit.astype(F32))
    lanes = lax.broadcasted_iota(jnp.int32, (1, WINDOW), 1)
    wide = wide + jnp.where(lanes % GROUP < LIVE, 0.0, NEG)
    wide_ref[...] = wide.reshape(HEADS, 72, WINDOW)
    out_ref[...] = jnp.zeros_like(out_ref)
    for parity in range(2):
        for half in range(2):
            for m in range(3):
                start = 12 * (3 * (1 - parity) + m) + 6 * (1 - half)
                out_ref[parity * 2 + half, :, 6 * m : 6 * m + 6, :] = wide_ref[:, start : start + 6, :]
    store = pltpu.make_async_copy(out_ref, out_hbm.at[pl.ds(0, 4)], sem)
    store.start()
    store.wait()


def ordered_bias(bias):
    return pl.pallas_call(
        bias_kernel,
        out_shape=jax.ShapeDtypeStruct((64, HEADS, GROUP, WINDOW), F32),
        out_specs=pl.BlockSpec(memory_space=pl.ANY),
        scratch_shapes=[
            pltpu.VMEM((HEADS, 72, WINDOW), F32),
            pltpu.VMEM((4, HEADS, GROUP, WINDOW), F32),
            pltpu.SemaphoreType.DMA,
        ],
        compiler_params=pltpu.CompilerParams(vmem_limit_bytes=58 * 1024 * 1024),
        cost_estimate=pl.CostEstimate(flops=2 * 10**10, bytes_accessed=2 * 10**6, transcendentals=0),
        name="ordered_bias",
    )(bias.reshape(HEADS * 72, 72))


def slots_kernel(index_ref, weight_ref, value_ref, count_ref, tokens_ref, out_ref, near_ref, edge_ref):
    even = lax.axis_index("lon") % 2 == 0
    for row in range(tokens_ref.shape[0]):
        x = tokens_ref[row].astype(F32)
        near_ref[row] = jnp.where(even, x[6:], x[:6]).astype(BF16)
        if row < 3 or row >= 9:
            for half in range(2):
                edge_ref[row // 9, half, row % 3] = x[6 * half : 6 * half + 6].astype(BF16)
    strips = value_ref.shape[0]
    square = (strips, strips)
    own_lane = lax.broadcasted_iota(jnp.int32, square, 0) == lax.broadcasted_iota(jnp.int32, square, 1)
    counts = jnp.broadcast_to(count_ref[...].astype(F32), square)
    counts = jnp.sum(jnp.where(own_lane, counts, 0.0), axis=1, keepdims=True).astype(jnp.int32)
    live = lax.broadcasted_iota(jnp.int32, (strips, 128), 1) < counts
    places = []
    for k in range(4):
        cell = index_ref[pl.ds(k, strips, stride=4), :]
        row = (cell * 171) >> 11
        col = cell - 12 * row
        group = (row * 11) >> 5
        half = (col >= 6).astype(jnp.int32)
        places.append((half * 4 + group) * GROUP + (row - 3 * group) * 6 + col - 6 * half)
        weight = weight_ref[pl.ds(k, strips, stride=4), :]
        out_ref[pl.ds(2 + k, strips, stride=8), :] = jnp.where(live, weight, 0.0)
    for pair in range(2):
        packed = places[2 * pair] + 1024 * places[2 * pair + 1]
        out_ref[pl.ds(pair, strips, stride=8), :] = packed.astype(F32)
    out_ref[pl.ds(6, strips, stride=8), :] = jnp.where(live, value_ref[...], 0.0)
    out_ref[pl.ds(7, strips, stride=8), :] = jnp.zeros((strips, 128), F32)


def packed_slots(index, weight, value, count, tokens):
    return pl.pallas_call(
        slots_kernel,
        out_shape=[
            jax.ShapeDtypeStruct((value.shape[0] * 8, 128), F32),
            jax.ShapeDtypeStruct((12, 6, MODEL), BF16),
            jax.ShapeDtypeStruct((2, 2, 3, 6, MODEL), BF16),
        ],
        cost_estimate=pl.CostEstimate(flops=10**6, bytes_accessed=5 * 10**5, transcendentals=0),
        name="packed_slots",
    )(index, weight, value, count, tokens)


def forward_part(
    bias_load,
    lat_count,
    own_ref,
    near_lon_ref,
    far_lon_ref,
    near_lat_ref,
    far_lat_ref,
    qkv_ref,
    wo_ref,
    down_ref,
    up_ref,
    readout_ref,
    bias_ref,
    block_ref,
    field_ref,
    probs_ref,
    gq_ref,
    low_ref,
    norm_ref,
    own_norm_ref,
    low_own_ref,
    w_ref,
    k_ref,
    v_ref,
    q_ref,
    att_ref,
):
    lat = lax.axis_index("lat")
    even_lon = lax.axis_index("lon") % 2 == 0
    even_lat = lat % 2 == 0
    first = (lat == 0).astype(F32)
    last = (lat == lat_count - 1).astype(F32)

    def pick(cond, a, b):
        return jnp.where(cond, a.astype(F32), b.astype(F32))

    gap = jnp.zeros((GROUP - LIVE, MODEL), F32)

    def piece(strip, group):
        rows = []
        for i in range(3):
            at = 3 * (group - 1) + i
            if group == 0:
                rows.append(pick(even_lat, far_lat_ref[strip, i], near_lat_ref[strip, i]))
            elif group == 5:
                rows.append(pick(even_lat, near_lat_ref[strip, i], far_lat_ref[strip, i]))
            elif strip == 0:
                rows.append(pick(even_lon, far_lon_ref[at], near_lon_ref[at]))
            elif strip == 3:
                rows.append(pick(even_lon, near_lon_ref[at], far_lon_ref[at]))
            else:
                rows.append(own_ref[at].astype(F32)[6 * (strip - 1) : 6 * strip])
        return jnp.concatenate(rows + [gap], axis=0)

    for strip in range(4):
        rows = []
        for pair in range(3):
            x = jnp.concatenate([piece(strip, 2 * pair + i) for i in range(2)], axis=0)
            center = x - jnp.mean(x, axis=1, keepdims=True)
            spread = jnp.mean(center * center, axis=1, keepdims=True)
            y = center * lax.rsqrt(spread + NORM_EPS)
            at = ((strip // 2) * 3 + pair) * WINDOW + (strip % 2) * 2 * GROUP
            norm_ref[at : at + 2 * GROUP, :] = y.astype(BF16)
            rows.append(y)
        if strip in (1, 2):
            mine = jnp.concatenate([rows[0][GROUP:], rows[1], rows[2][:GROUP]], axis=0)
            own_norm_ref[(strip - 1) * 4 * GROUP : strip * 4 * GROUP, :] = mine.astype(BF16)

    normed = norm_ref[...]
    rank_row = lax.broadcasted_iota(jnp.int32, (16, MODEL), 0)
    up_half = 0.5 * up_ref[...].astype(F32)
    up_query = jnp.where(rank_row < 8, up_half, 0.0).astype(BF16)
    up_value = jnp.where(rank_row >= 8, up_half, 0.0).astype(BF16)
    low = mm(normed, down_ref[...], NT).astype(BF16)
    low_ref[...] = low
    k_ref[...] = mm(normed, qkv_ref[:, MODEL : 2 * MODEL]).astype(BF16)
    v_ref[...] = (mm(normed, qkv_ref[:, 2 * MODEL :]) + mm(low, up_value)).astype(BF16)
    normed_own = own_norm_ref[...]
    low_own = mm(normed_own, down_ref[...], NT).astype(BF16)
    low_own_ref[...] = low_own.astype(F32)
    query = mm(normed_own, qkv_ref[:, :MODEL]) + mm(low_own, up_query)
    q_ref[...] = query.astype(BF16).astype(F32)

    readout = jnp.broadcast_to(readout_ref[...].astype(F32), (8, MODEL)).astype(BF16)
    w_row = mm(readout, wo_ref[...], NT)
    w_ref[...] = w_row

    scale = 1.0 / math.sqrt(HEAD_DIM)
    head_of = lax.broadcasted_iota(jnp.int32, (8, 1, 256), 2) // HEAD_DIM
    head_mask = head_of == lax.broadcasted_iota(jnp.int32, (8, 1, 256), 0)
    lane_part = (lax.broadcasted_iota(jnp.int32, (1, WINDOW), 1) // GROUP) % 2
    masked_first = jnp.where(lane_part == 0, NEG * first, 0.0)
    masked_last = jnp.where(lane_part == 1, NEG * last, 0.0)

    def fold(rows, size):
        return jnp.sum(jnp.where(head_mask, rows.reshape(8, size, 256), 0.0), axis=0)

    bias_load.wait()
    for window in range(6):
        half, window_row = window // 3, window % 3
        groups = ((0,), (1, 2), (3,))[window_row]
        size = GROUP * len(groups)
        own_rows = slice((4 * half + groups[0]) * GROUP, (4 * half + groups[0]) * GROUP + size)
        keys = slice(window * WINDOW, (window + 1) * WINDOW)
        for part in range(2):
            cols = slice(256 * part, 256 * (part + 1))
            k_win, v_win = k_ref[keys, cols], v_ref[keys, cols]
            lhs = jnp.where(head_mask, q_ref[own_rows, cols][None], 0.0)
            lhs = lhs.reshape(8 * size, 256).astype(BF16)
            bias = [bias_ref[(g % 2) * 2 + half, 8 * part : 8 * part + 8] for g in groups]
            bias = jnp.concatenate(bias, axis=1).reshape(8 * size, WINDOW)
            scores = mm(lhs, k_win, NT) * scale + bias
            if window_row == 0:
                scores = scores + masked_first
            if window_row == 2:
                scores = scores + masked_last
            raised = jnp.exp(scores - jnp.max(scores, axis=1, keepdims=True))
            probs = raised * (1.0 / jnp.sum(raised, axis=1, keepdims=True))
            probs3 = probs.reshape(8, size, WINDOW)
            for i, g in enumerate(groups):
                of_group = probs3[:, GROUP * i : GROUP * (i + 1)].reshape(8 * GROUP, WINDOW)
                rows = slice(8 * GROUP * part, 8 * GROUP * (part + 1))
                probs_ref[4 * half + g, rows, :] = of_group.astype(BF16)
            att_ref[own_rows, cols] = fold(mm(probs.astype(BF16), v_win), size)
            w_masked = jnp.where(head_mask[:, 0, :], w_row[:, cols], 0.0)
            w_high = w_masked.astype(BF16).astype(F32)
            w_pair = jnp.concatenate([w_high, w_masked - w_high], axis=0).astype(BF16)
            v_pair = mm(w_pair, v_win, NT)
            v_w = (v_pair[:8] + v_pair[8:]).reshape(8, 1, WINDOW)
            mean = jnp.sum(probs3 * v_w, axis=2, keepdims=True)
            slope = (probs3 * (v_w - mean) * scale).reshape(8 * size, WINDOW).astype(BF16)
            gq_ref[own_rows, cols] = fold(mm(slope, k_win), size)

    x_own = jnp.concatenate([piece(1 + n // 4, 1 + n % 4) for n in range(8)], axis=0)
    out = (x_own + mm(att_ref[...].astype(BF16), wo_ref[...])).astype(BF16)
    wide = out.astype(F32)
    for row in range(12):
        starts = [(half * 4 + row // 3) * GROUP + 6 * (row % 3) for half in range(2)]
        pair = jnp.concatenate([wide[start : start + 6] for start in starts], axis=0)
        block_ref[row] = pair.astype(BF16)
    field_ref[...] = jnp.zeros_like(field_ref)
    field_ref[:, :OWN] = mm(readout, out, NT)


def observe_part(
    slots_ref,
    field_ref,
    probs_ref,
    gq_ref,
    low_ref,
    norm_ref,
    own_norm_ref,
    low_own_ref,
    w_ref,
    up_ref,
    adjoint_ref,
    edge_ref,
    grads_ref,
    mine_ref,
    other_ref,
    innov_ref,
    term_ref,
    place_ref,
    loss_scale,
):
    sources = innov_ref.shape[0]
    field_low = jnp.broadcast_to(field_ref[0:1, 0:128], (sources, 128))
    field_high = jnp.broadcast_to(field_ref[0:1, 128:256], (sources, 128))
    places, weights = [], []
    for pair in range(2):
        packed = slots_ref[pl.ds(pair, sources, stride=8), :].astype(jnp.int32)
        places += [packed & 1023, packed >> 10]
    predicted = jnp.zeros((sources, 128), F32)
    for k in range(4):
        lane = places[k] & 127
        picked = jnp.where(
            places[k] < 128,
            jnp.take_along_axis(field_low, lane, axis=1),
            jnp.take_along_axis(field_high, lane, axis=1),
        )
        weights.append(slots_ref[pl.ds(2 + k, sources, stride=8), :])
        predicted = predicted + weights[k] * picked
    innov = predicted - slots_ref[pl.ds(6, sources, stride=8), :]
    innov_ref[...] = innov
    for k in range(4):
        rows = slice(k * sources, (k + 1) * sources)
        term = weights[k] * innov
        high = term.astype(BF16).astype(F32)
        term_ref[0, rows, :] = high
        term_ref[1, rows, :] = term - high
        place_ref[0, rows, :] = places[k] >> 4
        place_ref[1, rows, :] = places[k] & 15

    digit = lax.broadcasted_iota(jnp.int32, (16, 128), 0)
    per_step = 128

    def add_rows(step, total):
        left, right = [], []
        for inner in range(per_step):
            at = pl.ds(step * per_step + inner, 1)
            left.append(jnp.where(digit == place_ref[0, at, :], 1.0, 0.0).astype(BF16))
            hit = digit == place_ref[1, at, :]
            terms = [jnp.where(hit, term_ref[i, at, :], 0.0) for i in range(2)]
            right.append(jnp.concatenate(terms, axis=0).astype(BF16))
        return total + mm(jnp.concatenate(left, axis=1), jnp.concatenate(right, axis=1), NT)

    total = lax.fori_loop(0, 4 * sources // per_step, add_rows, jnp.zeros((16, 32), F32))
    total = total[:, :16] + total[:, 16:]

    def cells(shape, axis):
        cell = lax.broadcasted_iota(jnp.int32, shape, axis)
        digits = lax.broadcasted_iota(jnp.int32, shape, 1 - axis)
        return cell // 16 == digits, cell % 16 == digits

    total = jnp.concatenate([part.astype(F32) for part in parts_of(total, 3)], axis=0).astype(BF16)
    cell = lax.broadcasted_iota(jnp.int32, (OWN, 48), 0)
    high = cell // 16 == lax.broadcasted_iota(jnp.int32, (OWN, 48), 1) % 16
    column = mm(jnp.where(high, 1.0, 0.0).astype(BF16), total)
    low = cells((OWN, 16), 0)[1]
    adjoint = jnp.sum(jnp.where(low, column, 0.0), axis=1, keepdims=True)
    high, low = cells((16, OWN), 1)
    row = mm(total, jnp.where(low, 1.0, 0.0).astype(BF16))
    row = jnp.where(high, row[:16] + row[16:32] + row[32:], 0.0)
    row = jnp.sum(row, axis=0, keepdims=True)
    adjoint_ref[...] = jnp.concatenate([row, jnp.zeros((1, 256 - OWN), F32)], axis=1)
    edge_ref[...] = row[:, :128]
    low_plane = (lax.axis_index("lon") // 2) % 2 == 0
    for side in range(2):
        by_plane = [innov_ref[pl.ds(2 * h + side, sources // 4, stride=4), :] for h in range(2)]
        place = pl.ds(side, sources // 4, stride=2)
        mine_ref[place, :] = jnp.where(low_plane, by_plane[0], by_plane[1])
        other_ref[place, :] = jnp.where(low_plane, by_plane[1], by_plane[0])

    factor = 0.5 * loss_scale
    g_query = gq_ref[...].astype(BF16)
    up = up_ref[...]
    grad_low = mm(g_query, up, NT)
    up_query = mm((low_own_ref[...] * adjoint).astype(BF16), g_query, TN)
    down_query = mm((grad_low * adjoint).astype(BF16), own_norm_ref[...], TN)

    weighted = [None] * 6
    for n in range(8):
        window = (n // 4) * 3 + (n % 4 + 1) // 2
        probs = probs_ref[n].astype(F32).reshape(HEADS, GROUP, WINDOW)
        part = jnp.sum(probs * adjoint[n * GROUP : (n + 1) * GROUP].reshape(1, GROUP, 1), axis=1)
        weighted[window] = part if weighted[window] is None else weighted[window] + part
    head = lax.broadcasted_iota(jnp.int32, (HEADS, MODEL), 0)
    of_head = head == lax.broadcasted_iota(jnp.int32, (HEADS, MODEL), 1) // HEAD_DIM
    w_masked = jnp.where(of_head, jnp.broadcast_to(w_ref[0:1, :], (HEADS, MODEL)), 0.0)
    w_high, w_low = [part.astype(F32) for part in parts_of(w_masked, 2)]
    rank_head = mm(up, w_high.astype(BF16), NT) + mm(up, w_low.astype(BF16), NT)
    rank_head = [part.astype(F32) for part in parts_of(rank_head, 2)]
    rank_head = jnp.concatenate(rank_head, axis=0).astype(BF16)
    sums, down_value = jnp.zeros((HEADS, 16), F32), jnp.zeros((16, MODEL), F32)
    for window in range(6):
        keys = slice(window * WINDOW, (window + 1) * WINDOW)
        sums = sums + mm(weighted[window].astype(BF16), low_ref[keys, :])
        of_rank = sum(mm(rank_head, part) for part in parts_of(weighted[window], 2))
        of_rank = (of_rank[:HEADS] + of_rank[HEADS:]).astype(BF16)
        down_value = down_value + mm(of_rank, norm_ref[keys, :])
    high, low = [part.astype(F32) for part in parts_of(sums, 2)]
    up_value = mm(
        jnp.concatenate([high, high, low], axis=0).astype(BF16),
        jnp.concatenate([w_high, w_low, w_high], axis=0).astype(BF16),
        TN,
    )

    parts = (up_query[:8], up_value[8:], down_query[:8], down_value[8:])
    for m, part in enumerate(parts):
        part = part * factor
        for q in range(4):
            grads_ref[pl.ds(q * 32 + m, 8, stride=4), :] = part[:, 128 * q : 128 * (q + 1)]


def core_kernel(
    own_ref,
    near_lon_ref,
    far_lon_ref,
    far_lat_ref,
    near_lat_ref,
    qkv_ref,
    wo_ref,
    down_ref,
    up_ref,
    readout_ref,
    bias_hbm,
    slots_ref,
    block_ref,
    adjoint_ref,
    edge_ref,
    grads_ref,
    mine_ref,
    other_ref,
    field_ref,
    probs_ref,
    gq_ref,
    low_ref,
    norm_ref,
    own_norm_ref,
    low_own_ref,
    w_ref,
    k_ref,
    v_ref,
    q_ref,
    att_ref,
    bias_ref,
    bias_sem,
    innov_ref,
    term_ref,
    place_ref,
    loss_scale,
    lat_count,
):
    bias_load = pltpu.make_async_copy(bias_hbm.at[pl.ds(0, 4)], bias_ref, bias_sem)
    bias_load.start()
    forward_part(
        bias_load,
        lat_count,
        own_ref,
        near_lon_ref,
        far_lon_ref,
        near_lat_ref,
        far_lat_ref,
        qkv_ref,
        wo_ref,
        down_ref,
        up_ref,
        readout_ref,
        bias_ref,
        block_ref,
        field_ref,
        probs_ref,
        gq_ref,
        low_ref,
        norm_ref,
        own_norm_ref,
        low_own_ref,
        w_ref,
        k_ref,
        v_ref,
        q_ref,
        att_ref,
    )
    observe_part(
        slots_ref,
        field_ref,
        probs_ref,
        gq_ref,
        low_ref,
        norm_ref,
        own_norm_ref,
        low_own_ref,
        w_ref,
        up_ref,
        adjoint_ref,
        edge_ref,
        grads_ref,
        mine_ref,
        other_ref,
        innov_ref,
        term_ref,
        place_ref,
        loss_scale,
    )


def core(own, halos, qkv, wo, down, up, readout, bias, slots, loss_scale, lat_count):
    sources = slots.shape[0] // 8
    shape = jax.ShapeDtypeStruct
    vmem = pl.BlockSpec(memory_space=pltpu.VMEM)
    return pl.pallas_call(
        functools.partial(core_kernel, loss_scale=loss_scale, lat_count=lat_count),
        in_specs=[vmem] * 10 + [pl.BlockSpec(memory_space=pl.ANY), vmem],
        out_specs=[vmem] * 6,
        out_shape=[
            shape((12, 12, MODEL), BF16),
            shape((1, 256), F32),
            shape((1, 128), F32),
            shape((128, 128), F32),
            shape((sources // 2, 128), F32),
            shape((sources // 2, 128), F32),
        ],
        scratch_shapes=[
            pltpu.VMEM((8, 256), F32),
            pltpu.VMEM((8, HEADS * GROUP, WINDOW), BF16),
            pltpu.VMEM((OWN, MODEL), F32),
            pltpu.VMEM((6 * WINDOW, 16), BF16),
            pltpu.VMEM((6 * WINDOW, MODEL), BF16),
            pltpu.VMEM((OWN, MODEL), BF16),
            pltpu.VMEM((OWN, 16), F32),
            pltpu.VMEM((8, MODEL), F32),
            pltpu.VMEM((6 * WINDOW, MODEL), BF16),
            pltpu.VMEM((6 * WINDOW, MODEL), BF16),
            pltpu.VMEM((OWN, MODEL), F32),
            pltpu.VMEM((OWN, MODEL), F32),
            pltpu.VMEM((4, HEADS, GROUP, WINDOW), F32),
            pltpu.SemaphoreType.DMA,
            pltpu.VMEM((sources, 128), F32),
            pltpu.VMEM((2, 4 * sources, 128), F32),
            pltpu.VMEM((2, 4 * sources, 128), jnp.int32),
        ],
        compiler_params=pltpu.CompilerParams(vmem_limit_bytes=49 * 1024 * 1024),
        cost_estimate=pl.CostEstimate(
            flops=3 * 10**9, bytes_accessed=8 * 10**6, transcendentals=4 * 10**5
        ),
        name="window_and_observe",
    )(own, *halos, qkv, wo, down, up, readout, bias, slots)


def finish_kernel(final_ref, moved_ref, up_ref, down_ref, innov_ref, rolled_ref):
    members = final_ref.shape[0] // 8
    for m, (ref, which) in enumerate(((up_ref, 0), (up_ref, 1), (down_ref, 0), (down_ref, 1))):
        for q in range(4):
            ref[which, :, 128 * q : 128 * (q + 1)] = final_ref[pl.ds(q * 64 + m, 8, stride=8), :]
    lon = lax.axis_index("lon")
    plane, member = (lon // 2) % 2, lon // 4 * 2 + lon % 2
    for side in range(2):
        near, far = [final_ref[pl.ds(8 * side + i, members // 2, stride=16), :] for i in (6, 7)]
        for h in range(2):
            innov_ref[pl.ds(2 * h + side, members // 2, stride=4), :] = jnp.where(plane == h, near, far)

    across = member - 1 + 2 * plane
    across = jnp.where(across >= members, 0, across)
    row = jnp.where(lon % 2 == 0, (member + 1) * 8 + 4, across * 8 + 5)
    lane = lax.broadcasted_iota(jnp.int32, (16, 128), 1)
    patch_row = lax.broadcasted_iota(jnp.int32, (16, 128), 0)
    source = (patch_row // 3 * GROUP + patch_row % 3 * 6 + lane % 6) & 127
    halves = [
        jnp.take_along_axis(jnp.broadcast_to(values, (16, 128)), source, axis=1)
        for values in (moved_ref[...], final_ref[pl.ds(row, 1), :])
    ]
    rolled_ref[...] = jnp.where(lane < 6, halves[0], halves[1])[:12, :12]


def finish(final, moved):
    members = final.shape[0] // 8
    shape = jax.ShapeDtypeStruct
    return pl.pallas_call(
        finish_kernel,
        out_shape=[
            shape((2, 8, MODEL), F32),
            shape((2, 8, MODEL), F32),
            shape((2 * members, 128), F32),
            shape((12, 12), F32),
        ],
        compiler_params=pltpu.CompilerParams(vmem_limit_bytes=4 * 1024 * 1024),
        cost_estimate=pl.CostEstimate(flops=10**4, bytes_accessed=10**5, transcendentals=0),
        name="finish",
    )(final, moved)


def paired(value, axis, odd_first):
    count = lax.axis_size(axis)
    if odd_first:
        pairs = [(i, (i + 1) % count if i % 2 else (i - 1) % count) for i in range(count)]
    else:
        pairs = [(i, i ^ 1) for i in range(count)]
    return lax.ppermute(value, axis, pairs)


def shards(
    tokens,
    query_key_value_weight,
    output_weight,
    adapter_down_map,
    adapter_up_map,
    relative_position_bias,
    readout,
    observation_index,
    observation_weight,
    observation_value,
    observation_count,
):
    lat_count, lon_count = lax.axis_size("lat"), lax.axis_size("lon")
    lat, lon = lax.axis_index("lat"), lax.axis_index("lon")
    even_lat, even_lon = lat % 2 == 0, lon % 2 == 0

    own = (tokens[:, :6], tokens[:, 6:])
    far_send, observation_index = lax.optimization_barrier(
        (jnp.where(even_lon, own[0], own[1]), observation_index)
    )
    far_lon = paired(far_send, "lon", True)

    slots, near_send, edges = packed_slots(
        observation_index.reshape(lon_count * 4, 128),
        observation_weight.reshape(lon_count * 4, 128),
        observation_value.reshape(lon_count, 128),
        observation_count.reshape(1, lon_count),
        tokens,
    )
    slots = slots.reshape(lon_count, 8, 128)
    near_lon = paired(near_send, "lon", False)

    left = jnp.where(even_lon, far_lon, near_lon)
    right = jnp.where(even_lon, near_lon, far_lon)
    top = jnp.concatenate([left[None, :3], edges[0], right[None, :3]])
    bottom = jnp.concatenate([left[None, 9:], edges[1], right[None, 9:]])
    near_send, top, bottom, bias, readout = lax.optimization_barrier(
        (jnp.where(even_lat, bottom, top), top, bottom, relative_position_bias, readout)
    )
    readout = readout.reshape(1, MODEL)
    far_lat = paired(jnp.where(even_lat, top, bottom), "lat", True)
    near_lat = paired(near_send, "lat", False)
    slots = lax.all_to_all(slots, "lon", 0, 0, tiled=True).reshape(lon_count * 8, 128)

    down_rows = adapter_down_map.reshape(16, MODEL)
    up_rows = adapter_up_map.reshape(16, MODEL)
    loss_scale = 1.0 / math.sqrt(lat_count * lon_count)
    block_out, adjoint, edge_row, grads, mine, other = core(
        tokens,
        (near_lon, far_lon, far_lat, near_lat),
        query_key_value_weight,
        output_weight,
        down_rows,
        up_rows,
        readout,
        ordered_bias(bias),
        slots,
        loss_scale,
        lat_count,
    )
    members = lon_count // 2
    plane = (lon // 2) % 2
    planes = [[i for i in range(lon_count) if (i // 2) % 2 == h] for h in range(2)]
    columns = [
        [a * lon_count + at * 4 + h * 2 + c for h in range(2) for a in range(lat_count)]
        for at in range(members // 2)
        for c in range(2)
    ]

    chunks = lax.all_to_all(
        grads.reshape(members, 4, 128), "lon", 0, 0, axis_index_groups=planes, tiled=True
    )
    other = lax.ppermute(other, "lon", [(i, i ^ 2) for i in range(lon_count)])

    chunk = jnp.concatenate([jnp.sum(chunks, axis=0), edge_row], axis=0)
    chunk, adjoint = lax.optimization_barrier((chunk, adjoint))
    along = lax.all_to_all(
        jnp.broadcast_to(chunk[None], (2 * lat_count, 5, 128)),
        ("lat", "lon"),
        0,
        0,
        axis_index_groups=columns,
        tiled=True,
    )
    total = jnp.sum(along[:, :4], axis=0)
    edges = along[:, 4]
    below_at = (lat + 1) % lat_count

    def edge_of(h, a):
        return lax.dynamic_index_in_dim(edges, h * lat_count + a, 0, keepdims=False)

    def moved_up(here, below):
        kept = here[: 4 * GROUP].reshape(4, GROUP)[1:]
        return jnp.concatenate([kept.reshape(3 * GROUP), below[:GROUP]])

    below = edge_of(plane, below_at)
    edge = moved_up(adjoint[0], below)
    twin_edge = moved_up(edge_of(1 - plane, lat), edge_of(1 - plane, below_at))
    shared = jnp.concatenate(
        [total, jnp.pad(jnp.stack([edge, twin_edge]), ((0, 0), (0, 128 - 4 * GROUP)))], axis=0
    )
    final = jnp.concatenate(
        [jnp.broadcast_to(shared[None], (members, 6, 128)), mine[:, None], other[:, None]], axis=1
    )
    final = lax.all_to_all(final, "lon", 0, 0, axis_index_groups=planes, tiled=True)

    kept = adjoint[0, 4 * GROUP : OWN]
    moved = jnp.concatenate([kept[GROUP:], below[4 * GROUP : 5 * GROUP], jnp.zeros((GROUP + 8,), F32)])
    up_gradient, down_gradient, innovation, rolled_adjoint = finish(
        final.reshape(members * 8, 128), moved.reshape(1, 128)
    )
    return block_out, innovation[None, None], rolled_adjoint, down_gradient, up_gradient


def solution(mesh):
    return jax.shard_map(
        shards,
        mesh=mesh,
        in_specs=(
            P("lat", "lon", None),
            P(),
            P(),
            P(),
            P(),
            P(),
            P(),
            P("lat", "lon", None, None, None),
            P("lat", "lon", None, None, None),
            P("lat", "lon", None, None),
            P("lat", "lon", None),
        ),
        out_specs=(P("lat", "lon", None), P("lat", "lon", None, None), P("lat", "lon"), P(), P()),
        check_vma=False,
    )
```
